128 devices in a mesh: rep: 16 (over z, x), shard: 8 (over y, core).
Axes of the slice: x: 4, y: 4, z: 4, core: 2. Of those that a mesh axis runs over, the one named last changes fastest.
Arguments:
- tokens: bfloat16 [32768, 1024], P(('rep', 'shard')), may hold values from -6 to 6
- segment_ids: int32 [32768], P(('rep', 'shard')), may hold values from 0 to 4, as said below
- pad_mask: int32 [32768], P(('rep', 'shard')), may hold values from 0 to 1, as said below
- adapter_id: int32 [16], P('rep'), may hold values from 0 to 7
- out_grad: bfloat16 [32768, 1024], P(('rep', 'shard')), may hold values from -6 to 6
- gain_first: float32 [1024], replicated, may hold values from 0.5 to 1.5
- proj_in: bfloat16 [1024, 4096], P('shard'), may hold values from -0.1875 to 0.1875
- proj_rates: bfloat16 [1024, 16], replicated, may hold values from -0.1875 to 0.1875
- conv_taps: float32 [4, 3072], replicated, may hold values from -3 to 3
- decay_rate: float32 [8], replicated, may hold values from 0.0005 to 0.1
- ridge: float32 [8], replicated, may hold values from 0.5 to 2
- gain_heads: float32 [1024], replicated, may hold values from 0.5 to 1.5
- proj_out: bfloat16 [1024, 1024], P('shard'), may hold values from -0.1875 to 0.1875
- gain_second: float32 [1024], replicated, may hold values from 0.5 to 1.5
- proj_gu: bfloat16 [1024, 5632], P('shard'), may hold values from -0.1875 to 0.1875
- proj_down: bfloat16 [2816, 1024], P('shard'), may hold values from -0.109375 to 0.109375
- in_lower: bfloat16 [1024, 512], replicated, may hold values from -0.1875 to 0.1875
- in_upper: bfloat16 [4096, 128], replicated, may hold values from -0.75 to 0.75
- out_lower: bfloat16 [1024, 128], replicated, may hold values from -0.1875 to 0.1875
- out_upper: bfloat16 [1024, 128], replicated, may hold values from -0.75 to 0.75
- ffn_lower: bfloat16 [1024, 256], replicated, may hold values from -0.1875 to 0.1875
- ffn_upper: bfloat16 [5632, 128], replicated, may hold values from -0.75 to 0.75
- proj_lower: bfloat16 [2816, 128], replicated, may hold values from -0.109375 to 0.109375
- proj_upper: bfloat16 [1024, 128], replicated, may hold values from -0.75 to 0.75
Outputs:
- mixed: bfloat16 [32768, 1024], P(('rep', 'shard'))
- token_grad: float32 [32768, 1024], P(('rep', 'shard'))
- grad_in_lower: float32 [1024, 512], P('shard')
- grad_in_upper: float32 [4096, 128], P('shard')
- grad_out_lower: float32 [1024, 128], P('shard')
- grad_out_upper: float32 [1024, 128], P('shard')
- grad_ffn_lower: float32 [1024, 256], P('shard')
- grad_ffn_upper: float32 [5632, 128], P('shard')
- grad_proj_lower: float32 [2816, 128], P('shard')
- grad_proj_upper: float32 [1024, 128], P('shard')
The draws below stay inside these ranges and needn't reach their ends.
Inputs may be any that keep to these rules, and one draw needn't show every extreme that they name: `segment_ids`: within each sequence (rows 2048 apart) the numbers start at 0, never fall, and end at 4: five documents; the middle one starts at a position from 2 to 128 and ends 2 to 128 tokens before the sequence's end. `pad_mask`: each sequence's padding is at its end, at most 64 tokens.
All inputs are finite; a program needn't handle non-finite values.
Results may differ from the reference program's by a relative error of at most 0.018.
The reference program's roundings to bfloat16 on the way count: a program that leaves them out, or rounds other values in their place, can miss the bound.
Values may be sent and summed in bfloat16 or wider, within the bound.
No kernel may reach another device: no remote copies, remote signals or barrier semaphores. Data moves between devices by JAX's collectives and lax.ppermute only.
A program may use at most 384 MiB of HBM per device.

```python
import math
import jax
import jax.numpy as jnp
from jax import lax

D = 1024
HEADS = 8
HEAD = 128
FF = 2816
RANK = 16
ADAPTERS = 8
CONV = 4
ITERS = 8
TOK_DEV = 256
SEQ_LEN = 2048
SEQS = 16
TOKENS = 32768


def draw_segment_ids(key, part):
    key = jax.random.fold_in(key, 11)
    first_key, last_key = jax.random.split(key, 2)
    first = jax.random.randint(first_key, (SEQS, 1), 2, TOK_DEV // 2 + 1)
    last = SEQ_LEN - jax.random.randint(last_key, (SEQS, 1), 2, TOK_DEV // 2 + 1)
    early = first // 2
    late = last + (SEQ_LEN - last) // 2
    places = jnp.arange(SEQ_LEN)[None, :]
    flags = (places == early) | (places == first) | (places == last) | (places == late)
    return jnp.cumsum(flags.astype(jnp.int32), axis=1).reshape(SEQS * SEQ_LEN).astype(jnp.int32)


def draw_pad_mask(key, part):
    key = jax.random.fold_in(key, 23)
    padding = jax.random.randint(key, (SEQS, 1), 0, TOK_DEV // 4 + 1)
    places = jnp.arange(SEQ_LEN)[None, :]
    return (places < SEQ_LEN - padding).astype(jnp.int32).reshape(SEQS * SEQ_LEN)


def touch_ends(values, stream_key, smallest, largest):
    longest = values.shape.index(max(values.shape))
    spots = []
    for shift in (0, 1):
        where = [jax.random.randint(jax.random.fold_in(stream_key, axis), (), 0, length) for axis, length in enumerate(values.shape)]
        where[longest] = (where[longest] + shift) % values.shape[longest]
        spots.append(tuple(where))
    return values.at[spots[0]].set(smallest).at[spots[1]].set(largest)


def level_of(rng, extent, pieces, least, high):
    factor_of, own = 1.0, jax.random.fold_in(rng, 6)
    for position, blocks in pieces:
        draws = jnp.exp(jax.random.uniform(jax.random.fold_in(own, position), (blocks,), jnp.float32, least / len(pieces), high / len(pieces)))
        factor_of = factor_of * jnp.repeat(draws, extent[position] // blocks).reshape([-1 if axis == position else 1 for axis in range(len(extent))])
    return factor_of


def gaussian(rng, shape, deviation, reach, shards=(), kind=jnp.bfloat16):
    values = deviation * jax.random.normal(rng, shape, jnp.float32)
    if shards:
        values = values * level_of(rng, shape, shards, -0.22, 0.18)
    return jnp.clip(values, -reach, reach).astype(kind)


def setup_inputs(seed: int = 0) -> dict:
    streams_of = jax.random.split(jax.random.key(seed), 25)
    return {
        "tokens": gaussian(streams_of[0], (TOKENS, D), 1.0, 6.0, ((0, 128),)),
        "segment_ids": draw_segment_ids(jax.random.fold_in(streams_of[24], 71), 0),
        "pad_mask": draw_pad_mask(jax.random.fold_in(streams_of[24], 71), 0),
        "adapter_id": touch_ends(jax.random.randint(streams_of[3], (SEQS,), 0, ADAPTERS), jax.random.fold_in(streams_of[3], 1), 0, ADAPTERS - 1).astype(jnp.int32),
        "out_grad": gaussian(streams_of[4], (TOKENS, D), 1.0, 6.0, ((0, 128),)),
        "gain_first": jnp.clip(1.0 + 0.1 * jax.random.normal(streams_of[5], (D,), jnp.float32), 0.5, 1.5),
        "proj_in": gaussian(streams_of[6], (D, 4 * D), D ** -0.5, 0.1875, ((0, 8),)),
        "proj_rates": gaussian(streams_of[7], (D, 2 * HEADS), D ** -0.5, 0.1875),
        "conv_taps": gaussian(streams_of[8], (CONV, 3 * D), 0.5, 3.0, (), jnp.float32),
        "decay_rate": jnp.clip(jnp.exp(jax.random.uniform(streams_of[9], (HEADS,), jnp.float32, math.log(0.0005), math.log(0.1))), 0.0005, 0.1),
        "ridge": jnp.clip(jnp.exp(jax.random.uniform(streams_of[10], (HEADS,), jnp.float32, math.log(0.5), math.log(2.0))), 0.5, 2.0),
        "gain_heads": jnp.clip(1.0 + 0.1 * jax.random.normal(streams_of[11], (D,), jnp.float32), 0.5, 1.5),
        "proj_out": gaussian(streams_of[12], (D, D), D ** -0.5, 0.1875, ((0, 8),)),
        "gain_second": jnp.clip(1.0 + 0.1 * jax.random.normal(streams_of[13], (D,), jnp.float32), 0.5, 1.5),
        "proj_gu": gaussian(streams_of[14], (D, 2 * FF), D ** -0.5, 0.1875, ((0, 8),)),
        "proj_down": gaussian(streams_of[15], (FF, D), FF ** -0.5, 0.109375, ((0, 8),)),
        "in_lower": gaussian(streams_of[16], (D, 4 * ADAPTERS * RANK), D ** -0.5, 0.1875),
        "in_upper": gaussian(streams_of[17], (4 * D, ADAPTERS * RANK), (4 * RANK) ** -0.5, 0.75),
        "out_lower": gaussian(streams_of[18], (D, ADAPTERS * RANK), D ** -0.5, 0.1875),
        "out_upper": gaussian(streams_of[19], (D, ADAPTERS * RANK), (4 * RANK) ** -0.5, 0.75),
        "ffn_lower": gaussian(streams_of[20], (D, 2 * ADAPTERS * RANK), D ** -0.5, 0.1875),
        "ffn_upper": gaussian(streams_of[21], (2 * FF, ADAPTERS * RANK), (4 * RANK) ** -0.5, 0.75),
        "proj_lower": gaussian(streams_of[22], (FF, ADAPTERS * RANK), FF ** -0.5, 0.109375),
        "proj_upper": gaussian(streams_of[23], (D, ADAPTERS * RANK), (4 * RANK) ** -0.5, 0.75),
    }


@jax.custom_vjp
def low(v):
    return lax.optimization_barrier(v.astype(jnp.bfloat16)).astype(jnp.float32)

@jax.custom_vjp
def low_back(v):
    return v

def low_keep(v):
    return (low(v), None)

def low_pass(kept, grad):
    return (grad,)

def back_keep(v):
    return (v, None)

def back_low(kept, grad):
    return (low(grad),)
low.defvjp(low_keep, low_pass)
low_back.defvjp(back_keep, back_low)

def mult(left, right):
    return jnp.dot(left, right, precision=lax.Precision.HIGHEST, preferred_element_type=jnp.float32)

def contract(form, *operands):
    return jnp.einsum(form, *operands, precision=lax.Precision.HIGHEST, preferred_element_type=jnp.float32)

def rms_norm(value, gain):
    return value * lax.rsqrt(lax.optimization_barrier(jnp.mean(value * value, axis=-1, keepdims=True)) + 1e-06) * gain

def unit_rows(block, heads):
    shaped = block.reshape(block.shape[0], heads, -1)
    return shaped * lax.rsqrt(lax.optimization_barrier(jnp.sum(shaped * shaped, axis=-1, keepdims=True)) + 1e-06)

def front(extended, rate_logits, ext_ids, live, conv_taps, decay_rate):
    taps = conv_taps.shape[0]
    length = extended.shape[0] - taps + 1
    current = ext_ids[taps - 1:]
    summed = jnp.zeros((length, extended.shape[1]), jnp.float32)
    for offset in range(taps):
        begin = taps - 1 - offset
        same = (ext_ids[begin:begin + length] == current).astype(jnp.float32)
        summed = summed + conv_taps[offset] * extended[begin:begin + length] * same[:, None]
    active = jax.nn.silu(summed)
    width = active.shape[1] // 3
    heads = decay_rate.shape[0]
    query = unit_rows(active[:, :width], heads)
    keys = unit_rows(active[:, width:2 * width], heads)
    values = active[:, 2 * width:].reshape(length, heads, -1)
    beta = jax.nn.sigmoid(rate_logits[:, :heads]) * live[:, None]
    log_decay = -decay_rate[None, :] * jax.nn.softplus(rate_logits[:, heads:] + 1.0)
    return (query, keys, values, beta, log_decay)

def decay_table(log_decay, block_ids, previous):
    total = jnp.cumsum(log_decay, axis=0)
    places = jnp.arange(block_ids.shape[0])
    allowed = ((places[:, None] >= places[None, :]) & (block_ids[:, None] == block_ids[None, :])).astype(jnp.float32)
    spread = (total[:, None, :] - total[None, :, :]) * allowed[:, :, None]
    weights = jnp.exp(spread) * allowed[:, :, None]
    kept = (block_ids == previous).astype(jnp.float32)
    opening = jnp.exp(total) * kept[:, None]
    return (weights, opening)

def recent(vectors, keys, weights, beta):
    scores = contract('thd,shd->tsh', vectors, keys)
    return weights * beta[None, :, :] * scores

def operator(vectors, keys, weights, beta, opening, memory, ridge):
    mixing = recent(vectors, keys, weights, beta)
    result = contract('tsh,shd->thd', mixing, keys)
    result = result + opening[:, :, None] * contract('hde,the->thd', memory, vectors)
    return result + ridge[None, :, None] * vectors

def readout(query, keys, values, beta, log_decay, memory, lookup, block_ids, previous, ridge):
    weights, opening = decay_table(log_decay, block_ids, previous)
    solution = jnp.zeros_like(query)
    residual = query
    direction = query
    norm_now = lax.optimization_barrier(jnp.sum(residual * residual, axis=-1))
    for step in range(ITERS):
        image = operator(direction, keys, weights, beta, opening, memory, ridge)
        alpha = norm_now / (lax.optimization_barrier(jnp.sum(direction * image, axis=-1)) + 0.01)
        solution = solution + alpha[:, :, None] * direction
        residual = residual - alpha[:, :, None] * image
        norm_next = lax.optimization_barrier(jnp.sum(residual * residual, axis=-1))
        direction = residual + (norm_next / (norm_now + 0.01))[:, :, None] * direction
        norm_now = norm_next
    mixing = recent(solution, keys, weights, beta)
    return contract('tsh,shd->thd', mixing, values) + opening[:, :, None] * contract('hde,the->thd', lookup, solution)

def block_state(keys, values, beta, log_decay, block_ids, previous):
    weights, opening = decay_table(log_decay, block_ids, previous)
    last = weights[-1] * beta
    return (opening[-1], contract('sh,shd,she->hde', last, keys, keys), contract('sh,shd,she->hde', last, values, keys))

def gate_rows(mixed_heads, gate_in, gain_heads):
    length, heads, size = mixed_heads.shape
    normed = mixed_heads * lax.rsqrt(lax.optimization_barrier(jnp.mean(mixed_heads * mixed_heads, axis=-1, keepdims=True)) + 1e-06)
    normed = normed * gain_heads.reshape(heads, size)
    return normed.reshape(length, heads * size) * jax.nn.silu(gate_in)

def swiglu(joined):
    half = joined.shape[1] // 2
    return jax.nn.silu(joined[:, :half]) * joined[:, half:]

def mixer(query, keys, values, beta, log_decay, ids, ridge):
    blocks = SEQ_LEN // TOK_DEV

    def split(array):
        return array.reshape((blocks, TOK_DEV) + array.shape[1:])
    before = jnp.concatenate([jnp.full((1,), -1, jnp.int32), ids[TOK_DEV - 1:-1:TOK_DEV].astype(jnp.int32)])

    def advance(carry, item):
        memory, lookup = carry
        part_q, part_k, part_v, part_b, part_l, part_ids, previous = item
        out = readout(part_q, part_k, part_v, part_b, part_l, memory, lookup, part_ids, previous, ridge)
        opening, memory_part, lookup_part = block_state(part_k, part_v, part_b, part_l, part_ids, previous)
        return ((opening[:, None, None] * memory + memory_part, opening[:, None, None] * lookup + lookup_part), out)
    zero = jnp.zeros((HEADS, HEAD, HEAD), jnp.float32)
    items = (split(query), split(keys), split(values), split(beta), split(log_decay), split(ids), before)
    _, outs = lax.scan(jax.checkpoint(advance), (zero, zero), items)
    return outs.reshape(SEQ_LEN, HEADS, HEAD)

def layer(inputs, trained, frozen, ids, live, picked, gain_first, conv_taps, decay_rate, ridge, gain_heads, gain_second):
    in_lower, in_upper, out_lower, out_upper, ffn_lower, ffn_upper, proj_lower, proj_upper = trained
    proj_in, proj_rates, proj_out, proj_gu, proj_down = frozen
    length = inputs.shape[0]
    span = picked.shape[0]
    first = low(rms_norm(inputs, gain_first))
    inner_in = low_back(low(mult(first, in_lower) * jnp.tile(picked, 4)))
    extra = contract('tjr,jdr->tjd', inner_in.reshape(length, 4, span), in_upper.reshape(4, D, span)).reshape(length, 4 * D)
    projected = low_back(mult(first, proj_in) + extra)
    rate_logits = low_back(mult(first, proj_rates))
    conv_in = low(projected[:, :3 * D])
    gate_in = projected[:, 3 * D:]
    extended = jnp.concatenate([jnp.zeros((CONV - 1, 3 * D), jnp.float32), conv_in], axis=0)
    ext_ids = jnp.concatenate([jnp.full((CONV - 1,), -1, jnp.int32), ids.astype(jnp.int32)])
    query, keys, values, beta, log_decay = front(extended, rate_logits, ext_ids, live, conv_taps, decay_rate)
    mixed_heads = mixer(query, keys, values, beta, log_decay, ids, ridge)
    merged = low(gate_rows(mixed_heads, gate_in, gain_heads))
    inner_out = low_back(low(mult(merged, out_lower) * picked))
    branch = low_back(mult(merged, proj_out) + mult(inner_out, out_upper.T))
    middle = inputs + branch
    second = low(rms_norm(middle, gain_second))
    inner_ffn = low_back(low(mult(second, ffn_lower) * jnp.tile(picked, 2)))
    extra_ffn = contract('tjr,jfr->tjf', inner_ffn.reshape(length, 2, span), ffn_upper.reshape(2, FF, span)).reshape(length, 2 * FF)
    joined = low_back(mult(second, proj_gu) + extra_ffn)
    hidden = low(swiglu(joined))
    inner_proj = low_back(low(mult(hidden, proj_lower) * picked))
    return middle + low_back(mult(hidden, proj_down) + mult(inner_proj, proj_upper.T))

def reference(tokens, segment_ids, pad_mask, adapter_id, out_grad, gain_first, proj_in, proj_rates, conv_taps, decay_rate, ridge, gain_heads, proj_out, gain_second, proj_gu, proj_down, in_lower, in_upper, out_lower, out_upper, ffn_lower, ffn_upper, proj_lower, proj_upper):
    frozen = tuple((item.astype(jnp.float32) for item in (proj_in, proj_rates, proj_out, proj_gu, proj_down)))
    adapters = tuple((item.astype(jnp.float32) for item in (in_lower, in_upper, out_lower, out_upper, ffn_lower, ffn_upper, proj_lower, proj_upper)))
    inputs = tokens.astype(jnp.float32).reshape(SEQS, SEQ_LEN, D)
    ids = segment_ids.astype(jnp.int32).reshape(SEQS, SEQ_LEN)
    live = pad_mask.astype(jnp.float32).reshape(SEQS, SEQ_LEN)
    cotangent = out_grad.astype(jnp.float32).reshape(SEQS, SEQ_LEN, D)

    def one_sequence(totals, item):
        seq_in, seq_ids, seq_live, adapter_number, seq_cot = item
        picked = (jnp.arange(ADAPTERS * RANK) // RANK == adapter_number).astype(jnp.float32)

        def forward(values, trained):
            return layer(values, trained, frozen, seq_ids, seq_live, picked, gain_first, conv_taps, decay_rate, ridge, gain_heads, gain_second)
        result, pull = jax.vjp(forward, seq_in, adapters)
        grad_in, grad_adapt = pull(seq_cot)
        totals = tuple((left + right for left, right in zip(totals, grad_adapt)))
        return (totals, (result.astype(jnp.bfloat16), grad_in))
    start = tuple((jnp.zeros_like(item) for item in adapters))
    totals, (results, grads) = lax.scan(one_sequence, start, (inputs, ids, live, adapter_id.astype(jnp.int32), cotangent))
    return (results.reshape(SEQS * SEQ_LEN, D), grads.reshape(SEQS * SEQ_LEN, D), totals[0], totals[1], totals[2], totals[3], totals[4], totals[5], totals[6], totals[7])
```

```python
import jax
import jax.numpy as jnp
from jax import lax
from jax.experimental import pallas as pl
from jax.experimental.pallas import tpu as pltpu
from jax.sharding import PartitionSpec as P

F32 = jnp.float32
BF16 = jnp.bfloat16
ROWS = 256
CHUNK = 128
HEADS = 8
HEAD = 128
D = 1024
FF = 2816
RANK = 16
CONV = 4
ITERS = 8
VMEM = 60 * 1024 * 1024
TOT, KEPT, SAME, IDS = 8, 16, 17, 20


def nt(a, b):
    return lax.dot_general(a, b, (((1,), (1,)), ((), ())), preferred_element_type=F32)


def nn(a, b):
    return lax.dot_general(a, b, (((1,), (0,)), ((), ())), preferred_element_type=F32)


def tn(a, b):
    return lax.dot_general(a, b, (((0,), (0,)), ((), ())), preferred_element_type=F32)


def halves(x):
    high = x.astype(BF16)
    return high, (x - high.astype(F32)).astype(BF16)


def left3(x):
    high, rest = halves(x)
    return jnp.concatenate([high, rest, high], axis=1)


def right3(x, axis):
    high, rest = halves(x)
    return jnp.concatenate([high, high, rest], axis=axis)


def row_dot(a, b):
    return jnp.sum(a * b, axis=1, keepdims=True)


def column(packed, index):
    lane = lax.broadcasted_iota(jnp.int32, packed.shape, 1)
    return jnp.sum(jnp.where(lane == index, packed, 0.0), axis=1, keepdims=True)


def sigmoid(x):
    return 1.0 / (1.0 + jnp.exp(-x))


def chunk_scalars(cols, row_ref, head, chunk):
    begin = chunk * CHUNK
    part = cols[begin : begin + CHUNK]
    total = column(part, TOT + head)
    kept = column(part, KEPT)
    ids = column(part, IDS)
    span = slice(begin, begin + CHUNK)
    return {
        "beta": column(part, head),
        "total": total,
        "kept": kept,
        "ids": ids,
        "opening": jnp.exp(total) * kept,
        "beta_row": row_ref[0, 0:1, span],
        "total_row": row_ref[0, 1:2, span],
        "ids_row": row_ref[0, 2:3, span],
    }


def weights_of(s):
    t = lax.broadcasted_iota(jnp.int32, (CHUNK, CHUNK), 0)
    u = lax.broadcasted_iota(jnp.int32, (CHUNK, CHUNK), 1)
    allowed = (t >= u) & (s["ids"] == s["ids_row"])
    return jnp.where(allowed, jnp.exp(jnp.where(allowed, s["total"] - s["total_row"], 0.0)), 0.0)


def weights_t_of(s):
    u = lax.broadcasted_iota(jnp.int32, (CHUNK, CHUNK), 0)
    t = lax.broadcasted_iota(jnp.int32, (CHUNK, CHUNK), 1)
    allowed = (t >= u) & (s["ids"] == s["ids_row"])
    return jnp.where(allowed, jnp.exp(jnp.where(allowed, s["total_row"] - s["total"], 0.0)), 0.0)


def last_weight(s):
    end = CHUNK - 1
    same = s["ids"] == s["ids"][end:]
    return jnp.where(same, jnp.exp(jnp.where(same, s["total"][end:] - s["total"], 0.0)), 0.0)


def conv_rows(x_ref, tail_ref, taps_ref, ext, cols):
    ext[0:8, :] = tail_ref[8:16, :].astype(F32)
    ext[8 : 8 + ROWS, :] = x_ref[...].astype(F32)
    total = taps_ref[0:1, :] * ext[8 : 8 + ROWS, :]
    for j in range(1, CONV):
        same = cols[:, SAME + j - 1 : SAME + j]
        total = total + (taps_ref[j : j + 1, :] * ext[8 - j : 8 - j + ROWS, :]) * same
    return total


def front_kernel(
    q_in, k_in, v_in, q_tail, k_tail, v_tail, q_taps, k_taps, v_taps, cols_ref, row_ref,
    q_out, k_out, v_out, m_first, w_first, m_all, w_all, ext,
):
    head = pl.program_id(0)
    cols = cols_ref[...]
    acts = []
    for x_ref, tail_ref, taps_ref in (
        (q_in, q_tail, q_taps), (k_in, k_tail, k_taps), (v_in, v_tail, v_taps),
    ):
        c = conv_rows(x_ref, tail_ref, taps_ref, ext, cols)
        acts.append(c * sigmoid(c))
    q, k, v = acts
    q = q * lax.rsqrt(row_dot(q, q) + 1e-06)
    k = k * lax.rsqrt(row_dot(k, k) + 1e-06)
    q_out[...] = q
    k_out[...] = k
    v_out[...] = v
    parts = []
    for chunk in range(2):
        begin = chunk * CHUNK
        s = chunk_scalars(cols, row_ref, head, chunk)
        kc, vc = k[begin : begin + CHUNK], v[begin : begin + CHUNK]
        last = last_weight(s) * s["beta"]
        right = right3(kc, 0)
        parts.append((
            tn(jnp.concatenate(halves(kc * last) + (halves(kc * last)[0],), axis=0), right),
            tn(jnp.concatenate(halves(vc * last) + (halves(vc * last)[0],), axis=0), right),
            s["opening"][CHUNK - 1 :],
        ))
    m_first[0] = parts[0][0]
    w_first[0] = parts[0][1]
    m_all[0] = parts[1][2] * parts[0][0] + parts[1][0]
    w_all[0] = parts[1][2] * parts[0][1] + parts[1][1]


def head_block(rows, offset=0):
    return pl.BlockSpec((rows, HEAD), lambda h: (0, h + offset))


def whole(shape):
    return pl.BlockSpec(shape, lambda h: (0,) * len(shape))


def head_rows(count):
    return pl.BlockSpec((1, count, ROWS), lambda h: (h, 0, 0))


def square():
    return pl.BlockSpec((1, HEAD, HEAD), lambda h: (h, 0, 0))


def params():
    return pltpu.CompilerParams(vmem_limit_bytes=VMEM)


def front(conv_in, tail16, taps, cols, rows):
    shape = jax.ShapeDtypeStruct((ROWS, D), F32)
    states = jax.ShapeDtypeStruct((HEADS, HEAD, HEAD), F32)
    return pl.pallas_call(
        front_kernel,
        grid=(HEADS,),
        in_specs=[head_block(ROWS, o) for o in (0, 8, 16)]
        + [head_block(16, o) for o in (0, 8, 16)]
        + [head_block(CONV, o) for o in (0, 8, 16)]
        + [whole((ROWS, 128)), head_rows(8)],
        out_specs=[head_block(ROWS)] * 3 + [square()] * 4,
        out_shape=[shape] * 3 + [states] * 4,
        scratch_shapes=[pltpu.VMEM((ROWS + 8, HEAD), F32)],
        compiler_params=params(),
        name="front",
    )(conv_in, conv_in, conv_in, tail16, tail16, tail16, taps, taps, taps, cols, rows)


def read_kernel(
    ridge_ref, q_ref, k_ref, v_ref, gate_ref, gain_ref, cols_ref, row_ref,
    m0_ref, w0_ref, m_first, w_first, merged_ref, r_ref, y_ref, p_ref, i_ref,
):
    head = pl.program_id(0)
    cols = cols_ref[...]
    ridge = ridge_ref[head]
    chains = []
    memory, lookup = m0_ref[0], w0_ref[0]
    for chunk in range(2):
        begin = chunk * CHUNK
        at = slice(begin, begin + CHUNK)
        s = chunk_scalars(cols, row_ref, head, chunk)
        if chunk == 1:
            o1 = chains[0]["o"][CHUNK - 1 :]
            memory = o1 * memory + m_first[0]
            lookup = o1 * lookup + w_first[0]
        kc = k_ref[at, :]
        q = q_ref[at, :]
        chains.append({
            "at": at,
            "g": weights_of(s) * s["beta_row"],
            "o": s["opening"],
            "score": jnp.concatenate([right3(kc, 1), right3(memory, 1)], axis=0),
            "score_w": jnp.concatenate([right3(kc, 1), right3(lookup, 1)], axis=0),
            "keys": right3(kc, 0),
            "y": jnp.zeros_like(q),
            "r": q,
            "p": q,
            "rr": row_dot(q, q),
        })
    for j in range(ITERS):
        for c in chains:
            p = c["p"]
            both = nt(left3(p), c["score"])
            mixing = c["g"] * both[:, :CHUNK]
            image = nn(left3(mixing), c["keys"]) + c["o"] * both[:, CHUNK:] + ridge * p
            p_ref[j, c["at"], :] = p
            i_ref[j, c["at"], :] = image
            alpha = c["rr"] / (row_dot(p, image) + 0.01)
            c["y"] = c["y"] + alpha * p
            if j < ITERS - 1:
                c["r"] = c["r"] - alpha * image
                following = row_dot(c["r"], c["r"])
                c["p"] = c["r"] + (following / (c["rr"] + 0.01)) * p
                c["rr"] = following
    for c in chains:
        both = nt(left3(c["y"]), c["score_w"])
        mixing = c["g"] * both[:, :CHUNK]
        out = nn(left3(mixing), right3(v_ref[c["at"], :], 0)) + c["o"] * both[:, CHUNK:]
        y_ref[c["at"], :] = c["y"]
        r_ref[c["at"], :] = out
        normed = out * lax.rsqrt(row_dot(out, out) * (1.0 / HEAD) + 1e-06) * gain_ref[...]
        gate = gate_ref[c["at"], :]
        merged_ref[c["at"], :] = (normed * (gate * sigmoid(gate))).astype(BF16)


def read(ridge, q, k, v, gate, gain, cols, rows, m0, w0, m_first, w_first):
    flat = jax.ShapeDtypeStruct((ROWS, D), F32)
    steps = jax.ShapeDtypeStruct((ITERS, ROWS, D), F32)
    step_block = pl.BlockSpec((ITERS, ROWS, HEAD), lambda h: (0, 0, h))
    return pl.pallas_call(
        read_kernel,
        grid=(HEADS,),
        in_specs=[pl.BlockSpec(memory_space=pltpu.SMEM)]
        + [head_block(ROWS)] * 4
        + [head_block(1), whole((ROWS, 128)), head_rows(8)]
        + [square()] * 4,
        out_specs=[head_block(ROWS)] * 3 + [step_block] * 2,
        out_shape=[jax.ShapeDtypeStruct((ROWS, D), BF16), flat, flat, steps, steps],
        compiler_params=params(),
        name="readout",
    )(ridge, q, k, v, gate, gain, cols, rows, m0, w0, m_first, w_first)


def read_back_kernel(
    ridge_ref, q_ref, k_ref, v_ref, gate_ref, gain_ref, cols_ref, row_ref,
    m0_ref, w0_ref, m_first, w_first, r_ref, y_ref, p_ref, i_ref, dm_ref,
    dgate_ref, dq_ref, dk_ref, dv_ref, dcol_ref, drow_ref, dm0_ref, dw0_ref, dm1_ref, dw1_ref,
    stack_a, stack_b,
):
    head = pl.program_id(0)
    cols = cols_ref[...]
    ridge = ridge_ref[head]
    chains = []
    memory, lookup = m0_ref[0], w0_ref[0]
    for chunk in range(2):
        begin = chunk * CHUNK
        at = slice(begin, begin + CHUNK)
        s = chunk_scalars(cols, row_ref, head, chunk)
        if chunk == 1:
            o1 = chains[0]["o"][CHUNK - 1 :]
            memory = o1 * memory + m_first[0]
            lookup = o1 * lookup + w_first[0]
        kc, vc, q, y = k_ref[at, :], v_ref[at, :], q_ref[at, :], y_ref[at, :]
        o = s["opening"]
        weights_t = weights_t_of(s)
        g = weights_of(s) * s["beta_row"]
        g_t = weights_t * s["beta"]
        out, gate, dm, gain = r_ref[at, :], gate_ref[at, :], dm_ref[at, :], gain_ref[...]
        scale = lax.rsqrt(row_dot(out, out) * (1.0 / HEAD) + 1e-06)
        sig = sigmoid(gate)
        dgate_ref[at, :] = (dm * (out * scale * gain) * (sig * (1.0 + gate * (1.0 - sig)))).astype(BF16)
        dn = dm * (gate * sig) * gain
        dout = scale * dn - out * ((scale * scale * scale) * (row_dot(out, dn) * (1.0 / HEAD)))
        k_high, y_high, d_high, v_high = (a.astype(BF16) for a in (kc, y, dout, vc))
        dmix_dy = nn(left3(dout), right3(lookup, 0))
        dmix = nt(left3(dout), right3(vc, 1))
        keys = right3(kc, 0)
        score = jnp.concatenate([right3(kc, 1), right3(memory, 1)], axis=0)
        dy = nn(left3(g * dmix), keys) + o * dmix_dy
        s_t = nt(k_high, y_high)
        dmix_t = nt(v_high, d_high)
        dv_ref[at, :] = nn((g_t * s_t).astype(BF16), d_high)
        dk = nn((g_t * dmix_t).astype(BF16), y_high)
        dg_t = dmix_t * s_t
        do = row_dot(y, dmix_dy)
        dlookup = tn((o * dout).astype(BF16), y_high)
        r, rr = q, row_dot(q, q)
        rs, rrs, alphas, dens = [r], [rr], [], []
        for j in range(ITERS):
            image = i_ref[j, at, :]
            den = row_dot(p_ref[j, at, :], image) + 0.01
            alpha = rr / den
            alphas.append(alpha)
            dens.append(den)
            if j < ITERS - 1:
                r = r - alpha * image
                rr = row_dot(r, r)
                rs.append(r)
                rrs.append(rr)
        chains.append({
            "at": at, "g": g, "g_t": g_t, "w_t": weights_t, "o": o, "score": score, "keys": keys,
            "k_high": k_high, "dy": dy, "dk": dk, "dg_t": dg_t, "do": do, "dlookup": dlookup,
            "rs": rs, "rrs": rrs, "alphas": alphas, "dens": dens, "q": q, "chunk": chunk,
            "r_bar": None, "p_bar": None, "rr_bar": None,
        })
    for j in range(ITERS - 1, -1, -1):
        for c in chains:
            at = c["at"]
            p, image = p_ref[j, at, :], i_ref[j, at, :]
            alpha, den, rr = c["alphas"][j], c["dens"][j], c["rrs"][j]
            dy = c["dy"]
            if j == ITERS - 1:
                alpha_bar = row_dot(dy, p)
                p_bar = alpha * dy
                rr_bar = alpha_bar / den
                den_bar = -alpha_bar * alpha / den
                i_bar = den_bar * p
                r_bar = None
            else:
                below = 1.0 / (rr + 0.01)
                b = c["rrs"][j + 1] * below
                b_bar = row_dot(c["p_bar"], p)
                r_bar = c["p_bar"] if c["r_bar"] is None else c["r_bar"] + c["p_bar"]
                rr_next = c["rr_bar"] + b_bar * below
                r_bar = r_bar + (2.0 * rr_next) * c["rs"][j + 1]
                alpha_bar = jnp.sum(dy * p - r_bar * image, axis=1, keepdims=True)
                p_bar = b * c["p_bar"] + alpha * dy
                rr_bar = alpha_bar / den - b_bar * b * below
                den_bar = -alpha_bar * alpha / den
                i_bar = den_bar * p - alpha * r_bar
            p_bar = p_bar + den_bar * image
            left = left3(i_bar)
            both = nt(left, c["score"])
            im = both[:, CHUNK:]
            mixed = nn(left3(c["g"] * both[:, :CHUNK]), c["keys"])
            p_bar = p_bar + mixed + c["o"] * im + ridge * i_bar
            c["do"] = c["do"] + row_dot(p, im)
            i_high, p_high = left[:, :CHUNK], p.astype(BF16)
            turned = nt(c["k_high"], jnp.concatenate([p_high, i_high], axis=0))
            s_t, d_t = turned[:, :CHUNK], turned[:, CHUNK:]
            c["dg_t"] = c["dg_t"] + s_t * d_t
            c["dk"] = c["dk"] + nn(
                jnp.concatenate([c["g_t"] * s_t, c["g_t"] * d_t], axis=1).astype(BF16),
                jnp.concatenate([i_high, p_high], axis=0),
            )
            stack_a[c["chunk"], j * CHUNK : (j + 1) * CHUNK, :] = (c["o"] * i_bar).astype(BF16)
            stack_b[c["chunk"], j * CHUNK : (j + 1) * CHUNK, :] = p_high
            c["r_bar"], c["p_bar"], c["rr_bar"] = r_bar, p_bar, rr_bar
    dmem = []
    lane = lax.broadcasted_iota(jnp.int32, (CHUNK, 128), 1)
    for c in chains:
        at, chunk = c["at"], c["chunk"]
        dq_ref[at, :] = c["r_bar"] + c["p_bar"] + (2.0 * c["rr_bar"]) * c["q"]
        dk_ref[at, :] = c["dk"]
        dmem.append(tn(stack_a[chunk], stack_b[chunk]))
        scaled = c["dg_t"] * c["w_t"]
        z_t = c["dg_t"] * c["g_t"]
        dbeta = jnp.sum(scaled, axis=1, keepdims=True)
        dtotal = c["do"] * c["o"] - jnp.sum(z_t, axis=1, keepdims=True)
        before = dcol_ref[at, :]
        dcol_ref[at, :] = jnp.where(lane == head, dbeta, jnp.where(lane == TOT + head, dtotal, before))
        drow_ref[0, :, at] = jnp.sum(z_t, axis=0, keepdims=True)
    o1 = chains[0]["o"][CHUNK - 1 :]
    dm0_ref[0] = dmem[0] + o1 * dmem[1]
    dw0_ref[0] = chains[0]["dlookup"] + o1 * chains[1]["dlookup"]
    dm1_ref[0] = dmem[1]
    dw1_ref[0] = chains[1]["dlookup"]


def read_back(ridge, q, k, v, gate, gain, cols, rows, m0, w0, m_first, w_first, r, y, p, i, dm):
    flat = jax.ShapeDtypeStruct((ROWS, D), F32)
    states = jax.ShapeDtypeStruct((HEADS, HEAD, HEAD), F32)
    step_block = pl.BlockSpec((ITERS, ROWS, HEAD), lambda h: (0, 0, h))
    return pl.pallas_call(
        read_back_kernel,
        grid=(HEADS,),
        in_specs=[pl.BlockSpec(memory_space=pltpu.SMEM)]
        + [head_block(ROWS)] * 4
        + [head_block(1), whole((ROWS, 128)), head_rows(8)]
        + [square()] * 4
        + [head_block(ROWS)] * 2
        + [step_block] * 2
        + [head_block(ROWS)],
        out_specs=[head_block(ROWS)] * 4
        + [whole((ROWS, 128)), head_rows(1)]
        + [square()] * 4,
        out_shape=[jax.ShapeDtypeStruct((ROWS, D), BF16)]
        + [flat] * 3
        + [jax.ShapeDtypeStruct((ROWS, 128), F32), jax.ShapeDtypeStruct((HEADS, 1, ROWS), F32)]
        + [states] * 4,
        scratch_shapes=[
            pltpu.VMEM((2, ITERS * CHUNK, HEAD), BF16),
            pltpu.VMEM((2, ITERS * CHUNK, HEAD), BF16),
        ],
        compiler_params=params(),
        name="readout_back",
    )(ridge, q, k, v, gate, gain, cols, rows, m0, w0, m_first, w_first, r, y, p, i, dm)


def front_back_kernel(
    q_in, k_in, v_in, q_tail, k_tail, v_tail, q_taps, k_taps, v_taps, cols_ref, row_ref, shift_ref,
    k_ref, v_ref, dq_ref, dk_ref, dv_ref, dcol_ref,
    m0_ref, w0_ref, m_first, w_first, dm1_ref, dw1_ref, dm2_ref, dw2_ref,
    q_out, k_out, v_out, q_edge, k_edge, v_edge, q_head, k_head, v_head, dcol_out, ext, grown,
):
    head = pl.program_id(0)
    cols = cols_ref[...]
    s1 = chunk_scalars(cols, row_ref, head, 0)
    s2 = chunk_scalars(cols, row_ref, head, 1)
    o1, o2 = s1["opening"][CHUNK - 1 :], s2["opening"][CHUNK - 1 :]
    dm2, dw2 = dm2_ref[0], dw2_ref[0]
    m0, w0 = m0_ref[0], w0_ref[0]
    m1, w1 = o1 * m0 + m_first[0], o1 * w0 + w_first[0]
    dm1, dw1 = dm1_ref[0] + o2 * dm2, dw1_ref[0] + o2 * dw2
    lane = lax.broadcasted_iota(jnp.int32, (CHUNK, 128), 1)
    row = lax.broadcasted_iota(jnp.int32, (CHUNK, 1), 0)
    dks, dvs = [], []
    for chunk, s, dm, dw, m, w in ((0, s1, dm1, dw1, m0, w0), (1, s2, dm2, dw2, m1, w1)):
        at = slice(chunk * CHUNK, (chunk + 1) * CHUNK)
        kc, vc = k_ref[at, :], v_ref[at, :]
        weight = last_weight(s)
        last = weight * s["beta"]
        kb, vb, dmb, dwb = (a.astype(BF16) for a in (kc, vc, dm, dw))
        mk = nt(kb, dmb)
        wk = nt(kb, dwb)
        dks.append(dk_ref[at, :] + last * (mk + nn(kb, dmb) + nn(vb, dwb)))
        dvs.append(dv_ref[at, :] + last * wk)
        dlast = jnp.sum(kc * mk + vc * wk, axis=1, keepdims=True)
        part = dlast * last
        do = jnp.sum(jnp.sum(dm * m + dw * w, axis=1, keepdims=True), axis=0, keepdims=True)
        at_end = do * s["opening"][CHUNK - 1 :] + jnp.sum(part, axis=0, keepdims=True)
        dtotal = jnp.where(row == CHUNK - 1, at_end - part, -part)
        before = jnp.where(head == 0, dcol_ref[at, :], dcol_out[at, :])
        dcol_out[at, :] = before + jnp.where(
            lane == head, dlast * weight, jnp.where(lane == TOT + head, dtotal, 0.0)
        )
    dk = jnp.concatenate(dks, axis=0)
    dv = jnp.concatenate(dvs, axis=0)
    for x_ref, tail_ref, taps_ref, grad, unit, out, edge, top in (
        (q_in, q_tail, q_taps, dq_ref[...], True, q_out, q_edge, q_head),
        (k_in, k_tail, k_taps, dk, True, k_out, k_edge, k_head),
        (v_in, v_tail, v_taps, dv, False, v_out, v_edge, v_head),
    ):
        c = conv_rows(x_ref, tail_ref, taps_ref, ext, cols)
        sig = sigmoid(c)
        if unit:
            act = c * sig
            scale = lax.rsqrt(row_dot(act, act) + 1e-06)
            grad = scale * grad - act * ((scale * scale * scale) * row_dot(act, grad))
        dc = grad * (sig * (1.0 + c * (1.0 - sig)))
        grown[0:8, :] = jnp.zeros((8, HEAD), F32)
        grown[8 : 8 + ROWS, :] = dc
        grown[8 + ROWS :, :] = jnp.zeros((8, HEAD), F32)
        total = taps_ref[0:1, :] * grown[0 : ROWS + 8, :]
        for j in range(1, CONV):
            mask = shift_ref[:, j : j + 1]
            total = total + (taps_ref[j : j + 1, :] * grown[j : j + ROWS + 8, :]) * mask
        out[...] = total[8:, :].astype(BF16)
        edge[...] = total[ROWS:, :]
        top[...] = total[:8, :]


def front_back(conv_in, tail16, taps, cols, rows, shift, k, v, dq, dk, dv, dcol,
               m0, w0, m_first, w_first, dm1, dw1, dm2, dw2):
    small = jax.ShapeDtypeStruct((8, D), F32)
    return pl.pallas_call(
        front_back_kernel,
        grid=(HEADS,),
        in_specs=[head_block(ROWS, o) for o in (0, 8, 16)]
        + [head_block(16, o) for o in (0, 8, 16)]
        + [head_block(CONV, o) for o in (0, 8, 16)]
        + [whole((ROWS, 128)), head_rows(8), whole((ROWS + 8, 8))]
        + [head_block(ROWS)] * 5
        + [whole((ROWS, 128))]
        + [square()] * 8,
        out_specs=[head_block(ROWS)] * 3 + [head_block(8)] * 6 + [whole((ROWS, 128))],
        out_shape=[jax.ShapeDtypeStruct((ROWS, D), BF16)] * 3
        + [small] * 6
        + [jax.ShapeDtypeStruct((ROWS, 128), F32)],
        scratch_shapes=[pltpu.VMEM((ROWS + 8, HEAD), F32), pltpu.VMEM((ROWS + 16, HEAD), F32)],
        compiler_params=params(),
        name="front_back",
    )(conv_in, conv_in, conv_in, tail16, tail16, tail16, taps, taps, taps, cols, rows, shift,
      k, v, dq, dk, dv, dcol, m0, w0, m_first, w_first, dm1, dw1, dm2, dw2)


def token_scalars(logits, live, ids, tail_ids, decay_rate):
    beta = jax.nn.sigmoid(logits[:, :HEADS]) * live[:, None]
    log_decay = -decay_rate[None, :] * jax.nn.softplus(logits[:, HEADS:] + 1.0)
    total = jnp.dot(running_sums(), log_decay, precision=lax.Precision.HIGHEST)
    ext_ids = jnp.concatenate([tail_ids, ids])
    before = jnp.where(jnp.arange(ROWS) < CHUNK, tail_ids[CONV - 2], ids[CHUNK - 1])
    kept = (ids == before).astype(F32)
    same = [(ext_ids[CONV - 1 - j : CONV - 1 - j + ROWS] == ids).astype(F32) for j in range(1, CONV)]
    packed = jnp.concatenate(
        [beta, total, jnp.stack([kept] + same + [ids.astype(F32)] + [jnp.zeros_like(kept)] * 3, axis=1)],
        axis=1,
    )
    cols = jnp.pad(packed, ((0, 0), (0, 128 - packed.shape[1])))
    moved = [jnp.ones((ROWS + 8,), F32)] + [
        jnp.concatenate([jnp.zeros((8 - j,), F32), same[j - 1], jnp.zeros((j,), F32)])
        for j in range(1, CONV)
    ]
    shift = jnp.stack(moved + [jnp.zeros((ROWS + 8,), F32)] * 4, axis=1)
    id_row = jnp.broadcast_to(ids.astype(F32), (HEADS, ROWS))
    rows = jnp.pad(jnp.stack([beta.T, total.T, id_row], axis=1), ((0, 0), (0, 5), (0, 0)))
    return beta, log_decay, cols, rows, shift


def running_sums():
    t = lax.broadcasted_iota(jnp.int32, (ROWS, ROWS), 0)
    u = lax.broadcasted_iota(jnp.int32, (ROWS, ROWS), 1)
    return ((t >= u) & (t // CHUNK == u // CHUNK)).astype(F32)


def scalar_back(logits, live, decay_rate, dcol, drow):
    dtotal = dcol[:, TOT : TOT + HEADS] + drow[:, 0].T
    dbeta = dcol[:, :HEADS]
    ddecay = lax.dot_general(
        running_sums(), dtotal, (((0,), (0,)), ((), ())), precision=lax.Precision.HIGHEST
    )
    sig = jax.nn.sigmoid(logits[:, :HEADS])
    slope = jax.nn.sigmoid(logits[:, HEADS:] + 1.0)
    return jnp.concatenate(
        [dbeta * live[:, None] * sig * (1.0 - sig), -decay_rate[None, :] * slope * ddecay], axis=1
    )


def place():
    index = lax.axis_index("shard")
    return index // 2, lax.rem(index, 2)


def swap(value):
    count = lax.axis_size("shard")
    return lax.ppermute(value, "shard", [(i, i ^ 1) for i in range(count)])


def over_chips(value, steps):
    count = lax.axis_size("shard")
    pairs = [(i, i + 2 * steps) for i in range(count) if 0 <= i + 2 * steps < count]
    return lax.ppermute(value, "shard", pairs)


def packed_states(opening, parts):
    o = jnp.broadcast_to(opening[:, None, None], (opening.shape[0], 8, HEAD))
    return jnp.concatenate(parts + list(halves(o)), axis=1)


def opening_of(payload):
    rows = payload[:, -16:].astype(F32)
    return (rows[:, 0:1] + rows[:, 8:9])[:, :, :1]


def half_of(array, core):
    return lax.dynamic_slice_in_dim(array, core * (HEADS // 2), HEADS // 2, 0)


def joined_halves(own, other, core):
    low = jnp.where(core == 0, own, other)
    high = jnp.where(core == 0, other, own)
    return jnp.concatenate([low, high], axis=0)


def unpack_forward(payload):
    x = payload.astype(F32)
    return opening_of(payload), x[:, :HEAD] + x[:, HEAD : 2 * HEAD], x[:, 2 * HEAD : 3 * HEAD]


def pack_forward(opening, memory, lookup):
    high, rest = halves(memory)
    return packed_states(opening, [high, rest, lookup.astype(BF16)])


def states_before(opening, memory, lookup):
    _, core = place()
    everything = pack_forward(opening, memory, lookup)
    mine = unpack_forward(half_of(everything, core))
    other = unpack_forward(swap(half_of(everything, 1 - core)))
    first = tuple(jnp.where(core == 0, a, b) for a, b in zip(mine, other))
    second = tuple(jnp.where(core == 0, b, a) for a, b in zip(mine, other))
    chip_o = first[0] * second[0]
    chip = pack_forward(
        chip_o[:, 0, 0], second[0] * first[1] + second[1], second[0] * first[2] + second[2]
    )
    near, middle, far = (unpack_forward(over_chips(chip, n)) for n in (1, 2, 3))
    before = tuple(near[0] * (middle[0] * far[i] + middle[i]) + near[i] for i in (1, 2))
    after_first = tuple(first[0] * before[i] + first[i + 1] for i in (0, 1))
    own = tuple(jnp.where(core == 0, a, b) for a, b in zip(before, after_first))
    theirs = tuple(jnp.where(core == 0, b, a) for a, b in zip(before, after_first))
    high, rest = halves(theirs[0])
    came = swap(jnp.concatenate([high, rest, theirs[1].astype(BF16)], axis=1)).astype(F32)
    came = (came[:, :HEAD] + came[:, HEAD : 2 * HEAD], came[:, 2 * HEAD :])
    return tuple(joined_halves(a, b, core) for a, b in zip(own, came))


def unpack_backward(payload):
    x = payload.astype(F32)
    return opening_of(payload), x[:, :HEAD], x[:, HEAD : 2 * HEAD]


def pack_backward(opening, memory, lookup):
    return packed_states(opening, [memory.astype(BF16), lookup.astype(BF16)])


def states_after(opening, memory, lookup):
    _, core = place()
    everything = pack_backward(opening, memory, lookup)
    mine = unpack_backward(half_of(everything, core))
    other = unpack_backward(swap(half_of(everything, 1 - core)))
    first = tuple(jnp.where(core == 0, a, b) for a, b in zip(mine, other))
    second = tuple(jnp.where(core == 0, b, a) for a, b in zip(mine, other))
    chip_o = first[0] * second[0]
    chip = pack_backward(
        chip_o[:, 0, 0], first[1] + first[0] * second[1], first[2] + first[0] * second[2]
    )
    near, middle, far = (unpack_backward(over_chips(chip, -n)) for n in (1, 2, 3))
    later = tuple(near[i] + near[0] * (middle[i] + middle[0] * far[i]) for i in (1, 2))
    before_second = tuple(second[i + 1] + second[0] * later[i] for i in (0, 1))
    own = tuple(jnp.where(core == 0, b, a) for a, b in zip(later, before_second))
    theirs = tuple(jnp.where(core == 0, a, b) for a, b in zip(later, before_second))
    came = swap(jnp.concatenate([a.astype(BF16) for a in theirs], axis=1)).astype(F32)
    came = (came[:, :HEAD], came[:, HEAD:])
    return tuple(joined_halves(a, b, core) for a, b in zip(own, came))


def passed_along(value, steps):
    count = lax.axis_size("shard")
    pairs = [(i, i + steps) for i in range(count) if 0 <= i + steps < count]
    return lax.ppermute(value, "shard", pairs)


def rms_norm(value, gain):
    return value * lax.rsqrt(jnp.mean(value * value, axis=-1, keepdims=True) + 1e-06) * gain


def swiglu(joined):
    half = joined.shape[1] // 2
    return jax.nn.silu(joined[:, :half]) * joined[:, half:]


def chosen(array, adapter, blocks):
    rows = array.shape[0]
    span = array.shape[1] // blocks
    return jnp.concatenate(
        [
            lax.dynamic_slice(array, (0, b * span + adapter * RANK), (rows, RANK))
            for b in range(blocks)
        ],
        axis=1,
    )


def spread(upper, blocks):
    turned = jnp.tile(upper.T, (blocks, 1))
    n = upper.shape[0] // blocks
    r = lax.broadcasted_iota(jnp.int32, turned.shape, 0) // RANK
    c = lax.broadcasted_iota(jnp.int32, turned.shape, 1) // n
    return jnp.where(r == c, turned, jnp.zeros_like(turned))


def upper_grads(inner, grads, blocks):
    n = grads.shape[1] // blocks
    return [
        tn(inner[:, b * RANK : (b + 1) * RANK], grads[:, b * n : (b + 1) * n]) for b in range(blocks)
    ]


def reduced(parts, adapters):
    groups = lax.axis_size("shard")
    sizes = [p.shape[1] // groups for p in parts]
    stacked = jnp.concatenate([p.reshape(RANK, groups, -1) for p in parts], axis=2)
    stacked = stacked.transpose(1, 0, 2)
    mine = lax.psum_scatter(stacked, "shard", scatter_dimension=0, tiled=False)
    everyone = lax.all_gather(mine.astype(BF16), "rep")
    hot = (adapters[:, None] == jnp.arange(8)[None, :]).astype(BF16)
    summed = jnp.einsum("sa,srn->arn", hot, everyone, preferred_element_type=F32)
    summed = summed.reshape(8 * RANK, -1)
    outs, begin = [], 0
    for size in sizes:
        outs.append(summed[:, begin : begin + size].T)
        begin += size
    return outs


def per_device(
    tokens, segment_ids, pad_mask, adapter_id, out_grad, gain_first, proj_in, proj_rates,
    conv_taps, decay_rate, ridge, gain_heads, proj_out, gain_second, proj_gu, proj_down,
    in_lower, in_upper, out_lower, out_upper, ffn_lower, ffn_upper, proj_lower, proj_upper,
):
    tail = CONV - 1
    adapter = adapter_id[0]
    full_in, full_out, full_gu, full_down = (
        lax.all_gather(w, "shard", axis=0, tiled=True) for w in (proj_in, proj_out, proj_gu, proj_down)
    )
    adapters = lax.all_gather(adapter_id, "rep", axis=0, tiled=True)
    in_low, in_up = chosen(in_lower, adapter, 4), spread(chosen(in_upper, adapter, 1), 4)
    out_low, out_up = chosen(out_lower, adapter, 1), chosen(out_upper, adapter, 1)
    ffn_low, ffn_up = chosen(ffn_lower, adapter, 2), spread(chosen(ffn_upper, adapter, 1), 2)
    proj_low, proj_up = chosen(proj_lower, adapter, 1), chosen(proj_upper, adapter, 1)
    tail_ids = passed_along(segment_ids[ROWS - tail :], 1)

    inputs = tokens.astype(F32)
    normed_first, first_back = jax.vjp(lambda value: rms_norm(value, gain_first), inputs)
    first = normed_first.astype(BF16)
    inner_in = nn(first, in_low).astype(BF16)
    projected = nn(first, full_in) + nn(inner_in, in_up)
    logits = nn(first, proj_rates)
    conv_in = projected[:, : 3 * D].astype(BF16)
    gate_in = projected[:, 3 * D :]
    tail16 = jnp.pad(passed_along(conv_in[ROWS - tail :], 1), ((16 - tail, 0), (0, 0)))
    live = pad_mask.astype(F32)
    _, _, cols, rows, shift = token_scalars(logits, live, segment_ids, tail_ids, decay_rate)
    q, k, v, m_first, w_first, m_all, w_all = front(conv_in, tail16, conv_taps, cols, rows)
    ends = [jnp.exp(cols[t, TOT : TOT + HEADS]) * cols[t, KEPT] for t in (CHUNK - 1, ROWS - 1)]
    opening = ends[0] * ends[1]
    m0, w0 = states_before(opening, m_all, w_all)
    gain = gain_heads[None]
    merged, r, y, p, i = read(ridge, q, k, v, gate_in, gain, cols, rows, m0, w0, m_first, w_first)

    inner_out = nn(merged, out_low).astype(BF16)
    middle = inputs + (nn(merged, full_out) + nt(inner_out, out_up))
    normed_second, second_back = jax.vjp(lambda value: rms_norm(value, gain_second), middle)
    second = normed_second.astype(BF16)
    inner_ffn = nn(second, ffn_low).astype(BF16)
    joined = nn(second, full_gu) + nn(inner_ffn, ffn_up)
    activated, swiglu_back = jax.vjp(swiglu, joined)
    hidden = activated.astype(BF16)
    inner_proj = nn(hidden, proj_low).astype(BF16)
    mixed = (middle + nn(hidden, full_down) + nt(inner_proj, proj_up)).astype(BF16)

    d_inner_proj = nn(out_grad, proj_up).astype(BF16)
    d_hidden = nt(out_grad, full_down) + nt(d_inner_proj, proj_low)
    g_proj_upper = tn(inner_proj, out_grad)
    g_proj_lower = tn(d_inner_proj, hidden)
    (d_joined,) = swiglu_back(d_hidden)
    d_joined = d_joined.astype(BF16)
    d_inner_ffn = nt(d_joined, ffn_up).astype(BF16)
    d_second = nt(d_joined, full_gu) + nt(d_inner_ffn, ffn_low)
    g_ffn_upper = jnp.concatenate(upper_grads(inner_ffn, d_joined, 2), axis=1)
    g_ffn_lower = tn(d_inner_ffn, second)
    (d_normed,) = second_back(d_second)
    d_middle = out_grad.astype(F32) + d_normed
    d_branch = d_middle.astype(BF16)
    d_inner_out = nn(d_branch, out_up).astype(BF16)
    d_merged = nt(d_branch, full_out) + nt(d_inner_out, out_low)
    g_out_upper = tn(inner_out, d_branch)
    g_out_lower = tn(d_inner_out, merged)
    early = reduced(
        [g_out_lower, g_out_upper, g_ffn_lower[:RANK], g_ffn_lower[RANK:], g_ffn_upper, g_proj_lower, g_proj_upper],
        adapters,
    )

    d_gate, dq, dk, dv, dcol, drow, dm0, dw0, dm1, dw1 = read_back(
        ridge, q, k, v, gate_in, gain, cols, rows, m0, w0, m_first, w_first, r, y, p, i, d_merged
    )
    dm2, dw2 = states_after(opening, dm0, dw0)
    out = front_back(
        conv_in, tail16, conv_taps, cols, rows, shift, k, v, dq, dk, dv, dcol,
        m0, w0, m_first, w_first, dm1, dw1, dm2, dw2,
    )
    heads = jnp.concatenate([h[8 - tail :] for h in out[6:9]], axis=1)
    edge = jnp.concatenate(out[3:6], axis=1)
    returned = passed_along(heads.astype(BF16), -1).astype(F32)
    edge = (edge + jnp.pad(returned, ((8 - tail, 0), (0, 0)))).astype(BF16)
    d_conv = jnp.concatenate([jnp.concatenate(out[:3], axis=1)[: ROWS - 8], edge], axis=0)
    d_projected = jnp.concatenate([d_conv, d_gate], axis=1)
    d_logits = scalar_back(logits, live, decay_rate, out[9], drow).astype(BF16)
    d_inner_in = nt(d_projected, in_up).astype(BF16)
    d_first = nt(d_projected, full_in) + nt(d_inner_in, in_low) + nt(d_logits, proj_rates)
    g_in_upper = jnp.concatenate(upper_grads(inner_in, d_projected, 4), axis=1)
    g_in_lower = tn(d_inner_in, first)
    (d_normed,) = first_back(d_first)
    token_grad = d_middle + d_normed
    late = reduced([g_in_lower[j * RANK : (j + 1) * RANK] for j in range(4)] + [g_in_upper], adapters)
    return (
        mixed, token_grad,
        jnp.concatenate(late[:4], axis=1), late[4],
        early[0], early[1], jnp.concatenate(early[2:4], axis=1), early[4], early[5], early[6],
    )


def solution(mesh):
    whole_spec, by_shard, by_token = P(), P("shard", None), P(("rep", "shard"), None)
    by_row = P(("rep", "shard"))
    return jax.shard_map(
        per_device,
        mesh=mesh,
        in_specs=(
            by_token, by_row, by_row, P("rep"), by_token, whole_spec, by_shard, whole_spec,
            whole_spec, whole_spec, whole_spec, whole_spec, by_shard, whole_spec, by_shard, by_shard,
        )
        + (whole_spec,) * 8,
        out_specs=(by_token, by_token) + (by_shard,) * 8,
        check_vma=False,
    )
```

```python
import functools

import jax
import jax.numpy as jnp
from jax import lax
from jax.experimental import pallas as pl
from jax.experimental.pallas import tpu as pltpu
from jax.sharding import PartitionSpec as P

F32 = jnp.float32
BF16 = jnp.bfloat16
ROWS = 256
CHUNK = 128
HEADS = 8
HEAD = 128
D = 1024
FF = 2816
RANK = 16
CONV = 4
ITERS = 8
VMEM = 60 * 1024 * 1024
TOGETHER = 2
TOT, KEPT, SAME, IDS = 8, 16, 17, 20


def nt(a, b):
    return lax.dot_general(a, b, (((1,), (1,)), ((), ())), preferred_element_type=F32)


def nn(a, b):
    return lax.dot_general(a, b, (((1,), (0,)), ((), ())), preferred_element_type=F32)


def tn(a, b):
    return lax.dot_general(a, b, (((0,), (0,)), ((), ())), preferred_element_type=F32)


def halves(x):
    high = x.astype(BF16)
    return high, (x - high.astype(F32)).astype(BF16)


def left3(x, axis=1):
    high, rest = halves(x)
    return jnp.concatenate([high, rest, high], axis=axis)


def right3(x, axis):
    high, rest = halves(x)
    return jnp.concatenate([high, high, rest], axis=axis)


def row_dot(a, b):
    return jnp.sum(a * b, axis=1, keepdims=True)


def column(packed, index):
    lane = lax.broadcasted_iota(jnp.int32, packed.shape, 1)
    return jnp.sum(jnp.where(lane == index, packed, 0.0), axis=1, keepdims=True)


def sigmoid(x):
    return 1.0 / (1.0 + jnp.exp(-x))


def chunk_scalars(cols, row_ref, head, chunk, slot=0):
    begin = chunk * CHUNK
    part = cols[begin : begin + CHUNK]
    total = column(part, TOT + head)
    kept = column(part, KEPT)
    ids = column(part, IDS)
    span = slice(begin, begin + CHUNK)
    return {
        "beta": column(part, head),
        "total": total,
        "kept": kept,
        "ids": ids,
        "opening": jnp.exp(total) * kept,
        "beta_row": row_ref[slot, 0:1, span],
        "total_row": row_ref[slot, 1:2, span],
        "ids_row": row_ref[slot, 2:3, span],
    }


def weights_of(s):
    t = lax.broadcasted_iota(jnp.int32, (CHUNK, CHUNK), 0)
    u = lax.broadcasted_iota(jnp.int32, (CHUNK, CHUNK), 1)
    allowed = (t >= u) & (s["ids"] == s["ids_row"])
    return jnp.where(allowed, jnp.exp(jnp.where(allowed, s["total"] - s["total_row"], 0.0)), 0.0)


def weights_t_of(s):
    u = lax.broadcasted_iota(jnp.int32, (CHUNK, CHUNK), 0)
    t = lax.broadcasted_iota(jnp.int32, (CHUNK, CHUNK), 1)
    allowed = (t >= u) & (s["ids"] == s["ids_row"])
    return jnp.where(allowed, jnp.exp(jnp.where(allowed, s["total_row"] - s["total"], 0.0)), 0.0)


def last_weight(s):
    end = CHUNK - 1
    same = s["ids"] == s["ids"][end:]
    return jnp.where(same, jnp.exp(jnp.where(same, s["total"][end:] - s["total"], 0.0)), 0.0)


LOAD = 272


def places():
    return (
        lax.broadcasted_iota(jnp.int32, (HEAD, HEAD), 0),
        lax.broadcasted_iota(jnp.int32, (HEAD, HEAD), 1),
    )


def extra_rows(opening, diagonal):
    row = lax.broadcasted_iota(jnp.int32, (16, HEAD), 0)
    high, rest = halves(opening)
    out = jnp.where(row == 1, high.astype(F32), jnp.where(row == 2, rest.astype(F32), 0.0))
    return jnp.where(row == 0, diagonal, out).astype(BF16)


def pack_state(opening, memory, lookup):
    r, c = places()
    high, rest = halves(memory)
    high, rest = high.astype(F32), rest.astype(F32)
    diagonal = jnp.sum(jnp.where(r == c, rest, 0.0), axis=0, keepdims=True)
    mixed = jnp.where(r >= c, high, rest).astype(BF16)
    return jnp.concatenate([mixed, lookup.astype(BF16), extra_rows(opening, diagonal)], axis=0)


def unpack_state(load):
    r, c = places()
    x = load.astype(F32)
    mixed, extra = x[:HEAD], x[2 * HEAD :]
    turned = mixed.T
    high = jnp.where(r >= c, mixed, turned)
    rest = jnp.where(r < c, mixed, jnp.where(r > c, turned, extra[0:1]))
    return extra[1:2, 0:1] + extra[2:3, 0:1], high + rest, x[HEAD : 2 * HEAD]


def pack_plain(opening, memory, lookup):
    zero = jnp.zeros((1, HEAD), F32)
    return jnp.concatenate(
        [memory.astype(BF16), lookup.astype(BF16), extra_rows(opening, zero)], axis=0
    )


def unpack_plain(load):
    x = load.astype(F32)
    extra = x[2 * HEAD :]
    return extra[1:2, 0:1] + extra[2:3, 0:1], x[:HEAD], x[HEAD : 2 * HEAD]


def then(earlier, later):
    return tuple([earlier[0] * later[0]] + [later[0] * a + b for a, b in zip(earlier[1:], later[1:])])


def back_then(earlier, later):
    return tuple([earlier[0] * later[0]] + [a + earlier[0] * b for a, b in zip(earlier[1:], later[1:])])


def pair_kernel(forward, core_ref, mine_ref, came_ref, out_ref):
    pack, unpack = (pack_state, unpack_state) if forward else (pack_plain, unpack_plain)
    core = core_ref[0]
    for n in range(HEADS // 2):
        mine = jnp.where(core == 0, mine_ref[n], mine_ref[n + HEADS // 2])
        came = came_ref[n]
        first = unpack(jnp.where(core == 0, mine, came))
        second = unpack(jnp.where(core == 0, came, mine))
        out_ref[n] = pack(*(then if forward else back_then)(first, second))


def entry_kernel(forward, core_ref, mine_ref, came_ref, near_ref, middle_ref, far_ref, m_ref, w_ref, out_ref):
    pack, unpack = (pack_state, unpack_state) if forward else (pack_plain, unpack_plain)
    core = core_ref[0]
    for n in range(HEADS // 2):
        mine = jnp.where(core == 0, mine_ref[n], mine_ref[n + HEADS // 2])
        near, middle, far = unpack(near_ref[n]), unpack(middle_ref[n]), unpack(far_ref[n])
        own_first = core == 0
        if forward:
            outer = then(then(far, middle), near)
            inner = then(outer, unpack(jnp.where(own_first, mine, came_ref[n])))
            own = [jnp.where(own_first, a, b) for a, b in zip(outer, inner)]
            other = [jnp.where(own_first, b, a) for a, b in zip(outer, inner)]
        else:
            outer = back_then(near, back_then(middle, far))
            inner = back_then(unpack(jnp.where(own_first, came_ref[n], mine)), outer)
            own = [jnp.where(own_first, b, a) for a, b in zip(outer, inner)]
            other = [jnp.where(own_first, a, b) for a, b in zip(outer, inner)]
        m_ref[n] = own[1]
        w_ref[n] = own[2]
        out_ref[n] = pack(*other)


def join_kernel(forward, core_ref, own_m, own_w, came_ref, m_ref, w_ref):
    unpack = unpack_state if forward else unpack_plain
    core = core_ref[0]
    for n in range(HEADS // 2):
        _, memory, lookup = unpack(came_ref[n])
        for out, own, came in ((m_ref, own_m[n], memory), (w_ref, own_w[n], lookup)):
            out[n] = jnp.where(core == 0, own, came)
            out[n + HEADS // 2] = jnp.where(core == 0, came, own)


def small_call(kernel, forward, outs, *operands):
    return pl.pallas_call(
        functools.partial(kernel, forward),
        in_specs=[pl.BlockSpec(memory_space=pltpu.SMEM)]
        + [pl.BlockSpec(memory_space=pltpu.VMEM)] * (len(operands) - 1),
        out_specs=[pl.BlockSpec(memory_space=pltpu.VMEM)] * len(outs),
        out_shape=outs,
        compiler_params=params(),
        cost_estimate=cost(2),
    )(*operands)


def swap(value):
    count = lax.axis_size("shard")
    return lax.ppermute(value, "shard", [(i, i ^ 1) for i in range(count)])


def over_chips(value, steps):
    count = lax.axis_size("shard")
    pairs = [(i, i + 2 * steps) for i in range(count) if 0 <= i + 2 * steps < count]
    return lax.ppermute(value, "shard", pairs)


def exchanged(load, forward):
    half = HEADS // 2
    core = lax.rem(lax.axis_index("shard"), 2)
    scalar = core.reshape(1)
    packed = jax.ShapeDtypeStruct((half, LOAD, HEAD), BF16)
    states = jax.ShapeDtypeStruct((half, HEAD, HEAD), F32)
    full = jax.ShapeDtypeStruct((HEADS, HEAD, HEAD), F32)
    came = swap(lax.dynamic_slice_in_dim(load, (1 - core) * half, half, 0))
    (chip,) = small_call(pair_kernel, forward, [packed], scalar, load, came)
    others = [over_chips(chip, n if forward else -n) for n in (1, 2, 3)]
    own_m, own_w, out = small_call(
        entry_kernel, forward, [states, states, packed], scalar, load, came, *others
    )
    return small_call(join_kernel, forward, [full, full], scalar, own_m, own_w, swap(out))


def conv_rows(x_ref, tail_ref, taps_ref, ext_ref, spot, cols, lanes):
    ext = ext_ref.at[spot]
    ext[0:8, :] = tail_ref[8:16, lanes].astype(F32)
    ext[8 : 8 + ROWS, :] = x_ref[:, lanes].astype(F32)
    total = taps_ref[0:1, lanes] * ext[8 : 8 + ROWS, :]
    for j in range(1, CONV):
        same = cols[:, SAME + j - 1 : SAME + j]
        total = total + (taps_ref[j : j + 1, lanes] * ext[8 - j : 8 - j + ROWS, :]) * same
    return total


def front_kernel(
    k_in, v_in, k_tail, v_tail, k_taps, v_taps, cols_ref, row_ref,
    k_out, v_out, m_first, w_first, load_ref, ext,
):
    cols = cols_ref[...]
    for slot in range(TOGETHER):
        head = pl.program_id(0) * TOGETHER + slot
        lanes = slice(slot * HEAD, (slot + 1) * HEAD)
        acts = []
        for n, (x_ref, tail_ref, taps_ref) in enumerate(((k_in, k_tail, k_taps), (v_in, v_tail, v_taps))):
            c = conv_rows(x_ref, tail_ref, taps_ref, ext, 2 * slot + n, cols, lanes)
            acts.append(c * sigmoid(c))
        k, v = acts
        k = k * lax.rsqrt(row_dot(k, k) + 1e-06)
        k_out[:, lanes] = k
        v_out[:, lanes] = v
        parts = []
        for chunk in range(2):
            begin = chunk * CHUNK
            s = chunk_scalars(cols, row_ref, head, chunk, slot)
            kc, vc = k[begin : begin + CHUNK], v[begin : begin + CHUNK]
            last = last_weight(s) * s["beta"]
            right = right3(kc, 0)
            parts.append((
                tn(left3(kc * last, 0), right), tn(left3(vc * last, 0), right), s["opening"][CHUNK - 1 :]
            ))
        m_first[slot] = parts[0][0]
        w_first[slot] = parts[0][1]
        o2 = parts[1][2]
        load_ref[slot] = pack_state(
            parts[0][2] * o2, o2 * parts[0][0] + parts[1][0], o2 * parts[0][1] + parts[1][1]
        )


def query_kernel(q_in, q_tail, q_taps, cols_ref, q_out, ext):
    for slot in range(TOGETHER):
        lanes = slice(slot * HEAD, (slot + 1) * HEAD)
        c = conv_rows(q_in, q_tail, q_taps, ext, slot, cols_ref[...], lanes)
        q = c * sigmoid(c)
        q_out[:, lanes] = q * lax.rsqrt(row_dot(q, q) + 1e-06)


def head_block(rows, offset=0, heads=1):
    return pl.BlockSpec((rows, heads * HEAD), lambda h: (0, h + offset))


def whole(shape):
    return pl.BlockSpec(shape, lambda h: (0,) * len(shape))


def head_rows(count, heads=1):
    return pl.BlockSpec((heads, count, ROWS), lambda h: (h, 0, 0))


def square(heads=1):
    return pl.BlockSpec((heads, HEAD, HEAD), lambda h: (h, 0, 0))


def loads(heads=1):
    return pl.BlockSpec((heads, LOAD, HEAD), lambda h: (h, 0, 0))


def params():
    return pltpu.CompilerParams(vmem_limit_bytes=VMEM)


def cost(micros):
    return pl.CostEstimate(
        flops=int(micros * 1.15e9), bytes_accessed=int(micros * 3.0e6), transcendentals=0
    )


def front(conv_kv, tail_kv, taps, cols, rows):
    flat = jax.ShapeDtypeStruct((ROWS, D), F32)
    states = jax.ShapeDtypeStruct((HEADS, HEAD, HEAD), F32)
    per = HEADS // TOGETHER
    return pl.pallas_call(
        front_kernel,
        grid=(per,),
        in_specs=[head_block(ROWS, o, TOGETHER) for o in (0, per)]
        + [head_block(16, o, TOGETHER) for o in (0, per)]
        + [head_block(CONV, o, TOGETHER) for o in (per, 2 * per)]
        + [whole((ROWS, 128)), head_rows(8, TOGETHER)],
        out_specs=[head_block(ROWS, 0, TOGETHER)] * 2 + [square(TOGETHER)] * 2 + [loads(TOGETHER)],
        out_shape=[flat] * 2 + [states] * 2 + [jax.ShapeDtypeStruct((HEADS, LOAD, HEAD), BF16)],
        scratch_shapes=[pltpu.VMEM((2 * TOGETHER, ROWS + 8, HEAD), F32)],
        compiler_params=params(),
        name="front",
        cost_estimate=cost(6.4),
    )(conv_kv, conv_kv, tail_kv, tail_kv, taps, taps, cols, rows)


def front_query(conv_q, tail_q, taps, cols):
    return pl.pallas_call(
        query_kernel,
        grid=(HEADS // TOGETHER,),
        in_specs=[head_block(n, 0, TOGETHER) for n in (ROWS, 16, CONV)] + [whole((ROWS, 128))],
        out_specs=head_block(ROWS, 0, TOGETHER),
        out_shape=jax.ShapeDtypeStruct((ROWS, D), F32),
        scratch_shapes=[pltpu.VMEM((TOGETHER, ROWS + 8, HEAD), F32)],
        compiler_params=params(),
        name="front_query",
        cost_estimate=cost(4.5),
    )(conv_q, tail_q, taps, cols)


def read_kernel(
    ridge_ref, q_ref, k_ref, v_ref, gate_ref, gain_ref, cols_ref, row_ref,
    m0_ref, w0_ref, m_first, w_first, merged_ref, r_ref, y_ref, p_ref, i_ref,
):
    cols = cols_ref[...]
    chains = []
    for slot in range(TOGETHER):
        head = pl.program_id(0) * TOGETHER + slot
        lanes = slice(slot * HEAD, (slot + 1) * HEAD)
        memory, lookup = m0_ref[slot], w0_ref[slot]
        for chunk in range(2):
            begin = chunk * CHUNK
            at = slice(begin, begin + CHUNK)
            s = chunk_scalars(cols, row_ref, head, chunk, slot)
            if chunk == 1:
                o1 = chains[-1]["o"][CHUNK - 1 :]
                memory = o1 * memory + m_first[slot]
                lookup = o1 * lookup + w_first[slot]
            kc = k_ref[at, lanes]
            q = q_ref[at, lanes]
            chains.append({
                "at": (at, lanes),
                "lanes": lanes,
                "ridge": ridge_ref[head],
                "g": weights_of(s) * s["beta_row"],
                "o": s["opening"],
                "score": jnp.concatenate([right3(kc, 1), right3(memory, 1)], axis=0),
                "score_w": jnp.concatenate([right3(kc, 1), right3(lookup, 1)], axis=0),
                "keys": right3(kc, 0),
                "y": jnp.zeros_like(q),
                "r": q,
                "p": q,
                "rr": row_dot(q, q),
            })
    for j in range(ITERS):
        boths = [nt(left3(c["p"]), c["score"]) for c in chains]
        mixings = [left3(c["g"] * both[:, :CHUNK]) for c, both in zip(chains, boths)]
        recents = [nn(mixing, c["keys"]) for c, mixing in zip(chains, mixings)]
        for c, both, recent in zip(chains, boths, recents):
            p = c["p"]
            image = recent + c["o"] * both[:, CHUNK:] + c["ridge"] * p
            p_ref[(j,) + c["at"]] = p
            i_ref[(j,) + c["at"]] = image
            alpha = c["rr"] / (row_dot(p, image) + 0.01)
            c["y"] = c["y"] + alpha * p
            if j < ITERS - 1:
                c["r"] = c["r"] - alpha * image
                following = row_dot(c["r"], c["r"])
                c["p"] = c["r"] + (following / (c["rr"] + 0.01)) * p
                c["rr"] = following
    for c in chains:
        both = nt(left3(c["y"]), c["score_w"])
        mixing = c["g"] * both[:, :CHUNK]
        out = nn(left3(mixing), right3(v_ref[c["at"]], 0)) + c["o"] * both[:, CHUNK:]
        y_ref[c["at"]] = c["y"]
        r_ref[c["at"]] = out
        gain = gain_ref[:, c["lanes"]]
        normed = out * lax.rsqrt(row_dot(out, out) * (1.0 / HEAD) + 1e-06) * gain
        gate = gate_ref[c["at"]]
        merged_ref[c["at"]] = (normed * (gate * sigmoid(gate))).astype(BF16)


def read(ridge, q, k, v, gate, gain, cols, rows, m0, w0, m_first, w_first):
    flat = jax.ShapeDtypeStruct((ROWS, D), F32)
    steps = jax.ShapeDtypeStruct((ITERS, ROWS, D), F32)
    step_block = pl.BlockSpec((ITERS, ROWS, TOGETHER * HEAD), lambda h: (0, 0, h))
    return pl.pallas_call(
        read_kernel,
        grid=(HEADS // TOGETHER,),
        in_specs=[pl.BlockSpec(memory_space=pltpu.SMEM)]
        + [head_block(ROWS, 0, TOGETHER)] * 4
        + [head_block(1, 0, TOGETHER), whole((ROWS, 128)), head_rows(8, TOGETHER)]
        + [square(TOGETHER)] * 4,
        out_specs=[head_block(ROWS, 0, TOGETHER)] * 3 + [step_block] * 2,
        out_shape=[jax.ShapeDtypeStruct((ROWS, D), BF16), flat, flat, steps, steps],
        compiler_params=params(),
        name="readout",
        cost_estimate=cost(26),
    )(ridge, q, k, v, gate, gain, cols, rows, m0, w0, m_first, w_first)


def read_back_kernel(
    ridge_ref, q_ref, k_ref, v_ref, gate_ref, gain_ref, cols_ref, row_ref,
    m0_ref, w0_ref, m_first, w_first, r_ref, y_ref, p_ref, i_ref, dm_ref,
    dgate_ref, dq_ref, dk_ref, dv_ref, dcol_ref, drow_ref, load_ref, dm1_ref, dw1_ref,
    stack_a, stack_b,
):
    cols = cols_ref[...]
    chains = []
    for slot in range(TOGETHER):
        head = pl.program_id(0) * TOGETHER + slot
        lanes = slice(slot * HEAD, (slot + 1) * HEAD)
        memory, lookup = m0_ref[slot], w0_ref[slot]
        for chunk in range(2):
            begin = chunk * CHUNK
            at = (slice(begin, begin + CHUNK), lanes)
            s = chunk_scalars(cols, row_ref, head, chunk, slot)
            if chunk == 1:
                o1 = chains[-1]["o"][CHUNK - 1 :]
                memory = o1 * memory + m_first[slot]
                lookup = o1 * lookup + w_first[slot]
            kc, vc, q, y = k_ref[at], v_ref[at], q_ref[at], y_ref[at]
            o = s["opening"]
            weights_t = weights_t_of(s)
            g = weights_of(s) * s["beta_row"]
            g_t = weights_t * s["beta"]
            out, gate, dm, gain = r_ref[at], gate_ref[at], dm_ref[at], gain_ref[:, lanes]
            scale = lax.rsqrt(row_dot(out, out) * (1.0 / HEAD) + 1e-06)
            sig = sigmoid(gate)
            dgate_ref[at] = (
                dm * (out * scale * gain) * (sig * (1.0 + gate * (1.0 - sig)))
            ).astype(BF16)
            dn = dm * (gate * sig) * gain
            dout = scale * dn - out * ((scale * scale * scale) * (row_dot(out, dn) * (1.0 / HEAD)))
            k_high, y_high, d_high, v_high = (a.astype(BF16) for a in (kc, y, dout, vc))
            dmix_dy = nn(left3(dout), right3(lookup, 0))
            dmix = nt(left3(dout), right3(vc, 1))
            keys = right3(kc, 0)
            score = jnp.concatenate([right3(kc, 1), right3(memory, 1)], axis=0)
            dy = nn(left3(g * dmix), keys) + o * dmix_dy
            s_t = nt(k_high, y_high)
            dmix_t = nt(v_high, d_high)
            dv_ref[at] = nn((g_t * s_t).astype(BF16), d_high)
            chains.append({
                "at": at, "g": g, "g_t": g_t, "w_t": weights_t, "o": o, "score": score, "keys": keys,
                "k_high": k_high, "dy": dy, "dk": nn((g_t * dmix_t).astype(BF16), y_high),
                "dg_t": dmix_t * s_t, "do": row_dot(y, dmix_dy),
                "dlookup": tn((o * dout).astype(BF16), y_high),
                "rs": [q], "rrs": [row_dot(q, q)], "alphas": [], "dens": [], "q": q,
                "number": slot * 2 + chunk, "head": head, "slot": slot, "ridge": ridge_ref[head],
                "r_bar": None, "p_bar": None, "rr_bar": None,
            })
    for j in range(ITERS):
        for c in chains:
            image = i_ref[(j,) + c["at"]]
            den = row_dot(p_ref[(j,) + c["at"]], image) + 0.01
            alpha = c["rrs"][j] / den
            c["alphas"].append(alpha)
            c["dens"].append(den)
            if j < ITERS - 1:
                r = c["rs"][j] - alpha * image
                c["rs"].append(r)
                c["rrs"].append(row_dot(r, r))
    for j in range(ITERS - 1, -1, -1):
        for c in chains:
            p, image = p_ref[(j,) + c["at"]], i_ref[(j,) + c["at"]]
            alpha, den, rr = c["alphas"][j], c["dens"][j], c["rrs"][j]
            dy = c["dy"]
            if j == ITERS - 1:
                alpha_bar = row_dot(dy, p)
                p_bar = alpha * dy
                rr_bar = alpha_bar / den
                den_bar = -alpha_bar * alpha / den
                i_bar = den_bar * p
                r_bar = None
            else:
                below = 1.0 / (rr + 0.01)
                b = c["rrs"][j + 1] * below
                b_bar = row_dot(c["p_bar"], p)
                r_bar = c["p_bar"] if c["r_bar"] is None else c["r_bar"] + c["p_bar"]
                rr_next = c["rr_bar"] + b_bar * below
                r_bar = r_bar + (2.0 * rr_next) * c["rs"][j + 1]
                alpha_bar = row_dot(dy, p) - row_dot(r_bar, image)
                p_bar = b * c["p_bar"] + alpha * dy
                rr_bar = alpha_bar / den - b_bar * b * below
                den_bar = -alpha_bar * alpha / den
                i_bar = den_bar * p - alpha * r_bar
            c["r_bar"], c["p_bar"], c["rr_bar"] = r_bar, p_bar + den_bar * image, rr_bar
            c["i_bar"], c["left"] = i_bar, left3(i_bar)
        boths = [nt(c["left"], c["score"]) for c in chains]
        mixes = [left3(c["g"] * both[:, :CHUNK]) for c, both in zip(chains, boths)]
        moves = [nn(mix, c["keys"]) for c, mix in zip(chains, mixes)]
        for c, both, moved in zip(chains, boths, moves):
            im = both[:, CHUNK:]
            p = p_ref[(j,) + c["at"]]
            c["p_bar"] = c["p_bar"] + moved + c["o"] * im + c["ridge"] * c["i_bar"]
            c["do"] = c["do"] + row_dot(p, im)
            i_high, p_high = c["left"][:, :CHUNK], p.astype(BF16)
            turned = nt(c["k_high"], jnp.concatenate([p_high, i_high], axis=0))
            s_t, d_t = turned[:, :CHUNK], turned[:, CHUNK:]
            c["dg_t"] = c["dg_t"] + s_t * d_t
            c["dk"] = c["dk"] + nn(
                jnp.concatenate([c["g_t"] * s_t, c["g_t"] * d_t], axis=1).astype(BF16),
                jnp.concatenate([i_high, p_high], axis=0),
            )
            rows = slice(j * CHUNK, (j + 1) * CHUNK)
            stack_a[c["number"], rows, :] = (c["o"] * c["i_bar"]).astype(BF16)
            stack_b[c["number"], rows, :] = p_high
    lane = lax.broadcasted_iota(jnp.int32, (CHUNK, 128), 1)
    for c in chains:
        at = c["at"]
        dq_ref[at] = c["r_bar"] + c["p_bar"] + (2.0 * c["rr_bar"]) * c["q"]
        dk_ref[at] = c["dk"]
        c["dmem"] = tn(stack_a[c["number"]], stack_b[c["number"]])
        scaled = c["dg_t"] * c["w_t"]
        z_t = c["dg_t"] * c["g_t"]
        dbeta = jnp.sum(scaled, axis=1, keepdims=True)
        dtotal = c["do"] * c["o"] - jnp.sum(z_t, axis=1, keepdims=True)
        span, head = at[0], c["head"]
        dcol_ref[span, :] = jnp.where(
            lane == head, dbeta, jnp.where(lane == TOT + head, dtotal, dcol_ref[span, :])
        )
        drow_ref[c["slot"], :, span] = jnp.sum(z_t, axis=0, keepdims=True)
    for slot in range(TOGETHER):
        one, two = chains[2 * slot], chains[2 * slot + 1]
        o1 = one["o"][CHUNK - 1 :]
        load_ref[slot] = pack_plain(
            o1 * two["o"][CHUNK - 1 :],
            one["dmem"] + o1 * two["dmem"],
            one["dlookup"] + o1 * two["dlookup"],
        )
        dm1_ref[slot] = two["dmem"]
        dw1_ref[slot] = two["dlookup"]


def read_back(ridge, q, k, v, gate, gain, cols, rows, m0, w0, m_first, w_first, r, y, p, i, dm):
    flat = jax.ShapeDtypeStruct((ROWS, D), F32)
    states = jax.ShapeDtypeStruct((HEADS, HEAD, HEAD), F32)
    step_block = pl.BlockSpec((ITERS, ROWS, TOGETHER * HEAD), lambda h: (0, 0, h))
    return pl.pallas_call(
        read_back_kernel,
        grid=(HEADS // TOGETHER,),
        in_specs=[pl.BlockSpec(memory_space=pltpu.SMEM)]
        + [head_block(ROWS, 0, TOGETHER)] * 4
        + [head_block(1, 0, TOGETHER), whole((ROWS, 128)), head_rows(8, TOGETHER)]
        + [square(TOGETHER)] * 4
        + [head_block(ROWS, 0, TOGETHER)] * 2
        + [step_block] * 2
        + [head_block(ROWS, 0, TOGETHER)],
        out_specs=[head_block(ROWS, 0, TOGETHER)] * 4
        + [whole((ROWS, 128)), head_rows(1, TOGETHER)]
        + [loads(TOGETHER)]
        + [square(TOGETHER)] * 2,
        out_shape=[jax.ShapeDtypeStruct((ROWS, D), BF16)]
        + [flat] * 3
        + [jax.ShapeDtypeStruct((ROWS, 128), F32), jax.ShapeDtypeStruct((HEADS, 1, ROWS), F32)]
        + [jax.ShapeDtypeStruct((HEADS, LOAD, HEAD), BF16)]
        + [states] * 2,
        scratch_shapes=[
            pltpu.VMEM((2 * TOGETHER, ITERS * CHUNK, HEAD), BF16),
            pltpu.VMEM((2 * TOGETHER, ITERS * CHUNK, HEAD), BF16),
        ],
        compiler_params=params(),
        name="readout_back",
        cost_estimate=cost(39),
    )(ridge, q, k, v, gate, gain, cols, rows, m0, w0, m_first, w_first, r, y, p, i, dm)


def front_back_kernel(
    q_in, k_in, v_in, q_tail, k_tail, v_tail, q_taps, k_taps, v_taps, cols_ref, row_ref, shift_ref,
    k_ref, v_ref, dq_ref, dk_ref, dv_ref, dcol_ref,
    m0_ref, w0_ref, m_first, w_first, dm1_ref, dw1_ref, dm2_ref, dw2_ref,
    out_ref, edge_ref, top_ref, dcol_out, ext, grown_ref,
):
    cols = cols_ref[...]
    lane = lax.broadcasted_iota(jnp.int32, (CHUNK, 128), 1)
    row = lax.broadcasted_iota(jnp.int32, (CHUNK, 1), 0)
    added = [dcol_ref[:CHUNK, :], dcol_ref[CHUNK:, :]]
    fresh = pl.program_id(0) == 0
    added = [jnp.where(fresh, a, dcol_out[c * CHUNK : (c + 1) * CHUNK, :]) for c, a in enumerate(added)]
    for slot in range(TOGETHER):
        head = pl.program_id(0) * TOGETHER + slot
        lanes = slice(slot * HEAD, (slot + 1) * HEAD)
        s1 = chunk_scalars(cols, row_ref, head, 0, slot)
        s2 = chunk_scalars(cols, row_ref, head, 1, slot)
        o1, o2 = s1["opening"][CHUNK - 1 :], s2["opening"][CHUNK - 1 :]
        dm2, dw2 = dm2_ref[slot], dw2_ref[slot]
        m0, w0 = m0_ref[slot], w0_ref[slot]
        m1, w1 = o1 * m0 + m_first[slot], o1 * w0 + w_first[slot]
        dm1, dw1 = dm1_ref[slot] + o2 * dm2, dw1_ref[slot] + o2 * dw2
        dks, dvs = [], []
        for chunk, s, dm, dw, m, w in ((0, s1, dm1, dw1, m0, w0), (1, s2, dm2, dw2, m1, w1)):
            at = (slice(chunk * CHUNK, (chunk + 1) * CHUNK), lanes)
            kc, vc = k_ref[at], v_ref[at]
            weight = last_weight(s)
            last = weight * s["beta"]
            kb, vb, dmb, dwb = (a.astype(BF16) for a in (kc, vc, dm, dw))
            mk = nt(kb, dmb)
            wk = nt(kb, dwb)
            dks.append(dk_ref[at] + last * (mk + nn(kb, dmb) + nn(vb, dwb)))
            dvs.append(dv_ref[at] + last * wk)
            dlast = jnp.sum(kc * mk + vc * wk, axis=1, keepdims=True)
            part = dlast * last
            do = jnp.sum(jnp.sum(dm * m + dw * w, axis=0, keepdims=True), axis=1, keepdims=True)
            at_end = do * s["opening"][CHUNK - 1 :] + jnp.sum(part, axis=0, keepdims=True)
            dtotal = jnp.where(row == CHUNK - 1, at_end - part, -part)
            added[chunk] = added[chunk] + jnp.where(
                lane == head, dlast * weight, jnp.where(lane == TOT + head, dtotal, 0.0)
            )
        dk = jnp.concatenate(dks, axis=0)
        dv = jnp.concatenate(dvs, axis=0)
        for n, (x_ref, tail_ref, taps_ref, grad, unit) in enumerate((
            (q_in, q_tail, q_taps, dq_ref[:, lanes], True),
            (k_in, k_tail, k_taps, dk, True),
            (v_in, v_tail, v_taps, dv, False),
        )):
            c = conv_rows(x_ref, tail_ref, taps_ref, ext, 3 * slot + n, cols, lanes)
            sig = sigmoid(c)
            if unit:
                act = c * sig
                scale = lax.rsqrt(row_dot(act, act) + 1e-06)
                grad = scale * grad - act * ((scale * scale * scale) * row_dot(act, grad))
            dc = grad * (sig * (1.0 + c * (1.0 - sig)))
            grown = grown_ref.at[3 * slot + n]
            grown[0:8, :] = jnp.zeros((8, HEAD), F32)
            grown[8 : 8 + ROWS, :] = dc
            grown[8 + ROWS :, :] = jnp.zeros((8, HEAD), F32)
            total = taps_ref[0:1, lanes] * grown[0 : ROWS + 8, :]
            for j in range(1, CONV):
                mask = shift_ref[:, j : j + 1]
                total = total + (taps_ref[j : j + 1, lanes] * grown[j : j + ROWS + 8, :]) * mask
            out_ref[n, :, lanes] = total[8:, :].astype(BF16)
            edge_ref[n, :, lanes] = total[ROWS:, :]
            top_ref[n, :, lanes] = total[:8, :].astype(BF16)
    for chunk in range(2):
        dcol_out[chunk * CHUNK : (chunk + 1) * CHUNK, :] = added[chunk]


def front_back(conv_q, conv_kv, tail_q, tail_kv, taps, cols, rows, shift, k, v, dq, dk, dv, dcol,
               m0, w0, m_first, w_first, dm1, dw1, dm2, dw2):
    per = HEADS // TOGETHER

    def stacked(count):
        return pl.BlockSpec((3, count, TOGETHER * HEAD), lambda h: (0, 0, h))

    return pl.pallas_call(
        front_back_kernel,
        grid=(per,),
        in_specs=[head_block(ROWS, o, TOGETHER) for o in (0, 0, per)]
        + [head_block(16, o, TOGETHER) for o in (0, 0, per)]
        + [head_block(CONV, o, TOGETHER) for o in (0, per, 2 * per)]
        + [whole((ROWS, 128)), head_rows(8, TOGETHER), whole((ROWS + 8, 8))]
        + [head_block(ROWS, 0, TOGETHER)] * 5
        + [whole((ROWS, 128))]
        + [square(TOGETHER)] * 8,
        out_specs=[stacked(ROWS), stacked(8), stacked(8), whole((ROWS, 128))],
        out_shape=[
            jax.ShapeDtypeStruct((3, ROWS, D), BF16),
            jax.ShapeDtypeStruct((3, 8, D), F32),
            jax.ShapeDtypeStruct((3, 8, D), BF16),
            jax.ShapeDtypeStruct((ROWS, 128), F32),
        ],
        scratch_shapes=[
            pltpu.VMEM((3 * TOGETHER, ROWS + 8, HEAD), F32),
            pltpu.VMEM((3 * TOGETHER, ROWS + 16, HEAD), F32),
        ],
        compiler_params=params(),
        name="front_back",
        cost_estimate=cost(10),
    )(conv_q, conv_kv, conv_kv, tail_q, tail_kv, tail_kv, taps, taps, taps, cols, rows, shift,
      k, v, dq, dk, dv, dcol, m0, w0, m_first, w_first, dm1, dw1, dm2, dw2)


def token_scalars(logits, live, ids, tail_ids, decay_rate):
    beta = jax.nn.sigmoid(logits[:, :HEADS]) * live[:, None]
    log_decay = -decay_rate[None, :] * jax.nn.softplus(logits[:, HEADS:] + 1.0)
    total = jnp.dot(running_sums(), log_decay, precision=lax.Precision.HIGHEST)
    ext_ids = jnp.concatenate([tail_ids, ids])
    before = jnp.where(jnp.arange(ROWS) < CHUNK, tail_ids[CONV - 2], ids[CHUNK - 1])
    kept = (ids == before).astype(F32)
    same = [(ext_ids[CONV - 1 - j : CONV - 1 - j + ROWS] == ids).astype(F32) for j in range(1, CONV)]
    packed = jnp.concatenate(
        [beta, total, jnp.stack([kept] + same + [ids.astype(F32)] + [jnp.zeros_like(kept)] * 3, axis=1)],
        axis=1,
    )
    cols = jnp.pad(packed, ((0, 0), (0, 128 - packed.shape[1])))
    moved = [jnp.ones((ROWS + 8,), F32)] + [
        jnp.concatenate([jnp.zeros((8 - j,), F32), same[j - 1], jnp.zeros((j,), F32)])
        for j in range(1, CONV)
    ]
    shift = jnp.stack(moved + [jnp.zeros((ROWS + 8,), F32)] * 4, axis=1)
    id_row = jnp.broadcast_to(ids.astype(F32), (HEADS, ROWS))
    rows = jnp.pad(jnp.stack([beta.T, total.T, id_row], axis=1), ((0, 0), (0, 5), (0, 0)))
    return beta, log_decay, cols, rows, shift


def running_sums():
    t = lax.broadcasted_iota(jnp.int32, (ROWS, ROWS), 0)
    u = lax.broadcasted_iota(jnp.int32, (ROWS, ROWS), 1)
    return ((t >= u) & (t // CHUNK == u // CHUNK)).astype(F32)


def scalar_back(logits, live, decay_rate, dcol, drow):
    dtotal = dcol[:, TOT : TOT + HEADS] + drow[:, 0].T
    dbeta = dcol[:, :HEADS]
    ddecay = lax.dot_general(
        running_sums(), dtotal, (((0,), (0,)), ((), ())), precision=lax.Precision.HIGHEST
    )
    sig = jax.nn.sigmoid(logits[:, :HEADS])
    slope = jax.nn.sigmoid(logits[:, HEADS:] + 1.0)
    return jnp.concatenate(
        [dbeta * live[:, None] * sig * (1.0 - sig), -decay_rate[None, :] * slope * ddecay], axis=1
    )


TILE = 1024
FF_TILE = 1408


def rms_back(value, gain, grad):
    scale = lax.rsqrt(row_dot(value, value) * (1.0 / D) + 1e-06)
    dn = grad * gain
    return scale * dn - value * ((scale * scale * scale) * (row_dot(value, dn) * (1.0 / D)))


def project_kernel(first_ref, w_ref, inner_ref, up_ref, out_ref):
    out = nn(first_ref[...], w_ref[...]) + nn(inner_ref[0], up_ref[...])
    out_ref[...] = out.astype(out_ref.dtype)


def project(first, weights, inner, up, begin, width, dtype):
    tiles, per_block = width // PROJ, D // PROJ
    return pl.pallas_call(
        project_kernel,
        grid=(tiles,),
        in_specs=[
            pl.BlockSpec((ROWS, D), lambda t: (0, 0)),
            pl.BlockSpec((D, PROJ), lambda t: (0, t + begin // PROJ)),
            pl.BlockSpec((1, ROWS, RANK), lambda t: ((t + begin // PROJ) // per_block, 0, 0)),
            pl.BlockSpec((RANK, PROJ), lambda t: (0, t + begin // PROJ)),
        ],
        out_specs=pl.BlockSpec((ROWS, PROJ), lambda t: (0, t)),
        out_shape=jax.ShapeDtypeStruct((ROWS, width), dtype),
        compiler_params=params(),
        name="project",
        cost_estimate=cost(2 * width / D),
    )(first, weights, inner, up)


PROJ = 1024


def half_kernel(
    merged_ref, tokens_ref, grad_ref, gain_ref, wout_a, wout_b, out_low, out_up, ffn_low, proj_up,
    gate_w, up_w, down_w, up_a, up_b, proj_low,
    mixed_ref, dmid_ref, dmerged_ref, g_out_low, g_out_up, g_ffn_low, g_up_a, g_up_b, g_proj_low, g_proj_up,
    middle_s, second_s, ffn_s, dproj_s, acc_out, acc_ds, acc_ip, acc_df,
):
    step = pl.program_id(0)
    g = grad_ref[...]

    @pl.when(step == 0)
    def _():
        merged = merged_ref[...]
        inner_out = nt(merged, out_low[...]).astype(BF16)
        branch = jnp.concatenate([nn(merged, wout_a[...]), nn(merged, wout_b[...])], axis=1)
        middle = tokens_ref[...].astype(F32) + (branch + nn(inner_out, out_up[...]))
        scale = lax.rsqrt(row_dot(middle, middle) * (1.0 / D) + 1e-06)
        second = (middle * scale * gain_ref[...]).astype(BF16)
        inner_ffn = nt(second, ffn_low[...]).astype(BF16)
        middle_s[...] = middle
        acc_out[...] = middle
        second_s[...] = second
        ffn_s[0] = inner_ffn[:, :RANK]
        ffn_s[1] = inner_ffn[:, RANK:]
        dproj_s[...] = nt(g, proj_up[...]).astype(BF16)
        acc_ds[...] = jnp.zeros_like(acc_ds)
        acc_ip[...] = jnp.zeros_like(acc_ip)
        acc_df[...] = jnp.zeros_like(acc_df)

    second = second_s[...]
    a = nn(second, gate_w[...]) + nn(ffn_s[0], up_a[...])
    b = nn(second, up_w[...]) + nn(ffn_s[1], up_b[...])
    down = down_w[...]
    d_hidden = nt(g, down) + nn(dproj_s[...], proj_low[...])
    sig = sigmoid(a)
    act = a * sig
    hidden = (act * b).astype(BF16)
    da = (d_hidden * b * (sig * (1.0 + a * (1.0 - sig)))).astype(BF16)
    db = (d_hidden * act).astype(BF16)
    acc_out[...] += nn(hidden, down)
    acc_ds[...] += nt(da, gate_w[...]) + nt(db, up_w[...])
    acc_ip[...] += nt(hidden, proj_low[...])
    acc_df[0] += nt(da, up_a[...])
    acc_df[1] += nt(db, up_b[...])
    g_proj_low[...] = tn(dproj_s[...], hidden)
    g_up_a[...] = tn(ffn_s[0], da)
    g_up_b[...] = tn(ffn_s[1], db)

    @pl.when(step == pl.num_programs(0) - 1)
    def _():
        merged, second, middle = merged_ref[...], second_s[...], middle_s[...]
        inner_proj = acc_ip[...].astype(BF16)
        mixed_ref[...] = (acc_out[...] + nn(inner_proj, proj_up[...])).astype(BF16)
        g_proj_up[...] = tn(inner_proj, g)
        da, db = acc_df[0].astype(BF16), acc_df[1].astype(BF16)
        d_second = acc_ds[...] + (nn(da, ffn_low[:RANK, :]) + nn(db, ffn_low[RANK:, :]))
        g_ffn_low[:RANK, :] = tn(da, second)
        g_ffn_low[RANK:, :] = tn(db, second)
        d_middle = g.astype(F32) + rms_back(middle, gain_ref[...], d_second)
        dmid_ref[...] = d_middle
        d_branch = d_middle.astype(BF16)
        d_inner = nt(d_branch, out_up[...]).astype(BF16)
        half = D // 2
        d_branch_out = nt(d_branch[:, :half], wout_a[...]) + nt(d_branch[:, half:], wout_b[...])
        dmerged_ref[...] = d_branch_out + nn(d_inner, out_low[...])
        inner_out = nt(merged, out_low[...]).astype(BF16)
        g_out_up[...] = tn(inner_out, d_branch)
        g_out_low[...] = tn(d_inner, merged)


def second_half(merged, tokens, grad, gain, w_og, w_down, out_low, out_up, ffn_low, ffn_up, proj_low, proj_up):
    steps = FF // FF_TILE
    wide = jax.ShapeDtypeStruct((ROWS, D), F32)
    thin = jax.ShapeDtypeStruct((RANK, D), F32)
    thin_ff = jax.ShapeDtypeStruct((RANK, FF), F32)
    tile = pl.BlockSpec((RANK, FF_TILE), lambda f: (0, f))
    row = whole((RANK, D))

    def out_half(n):
        return pl.BlockSpec((D, D // 2), lambda f: (0, 4 * FF // D + n))

    return pl.pallas_call(
        half_kernel,
        grid=(steps,),
        in_specs=[whole((ROWS, D))] * 3
        + [whole((1, D)), out_half(0), out_half(1), row, row, whole((2 * RANK, D)), row]
        + [
            pl.BlockSpec((D, FF_TILE), lambda f: (0, f)),
            pl.BlockSpec((D, FF_TILE), lambda f: (0, f + steps)),
            pl.BlockSpec((FF_TILE, D), lambda f: (f, 0)),
            tile,
            pl.BlockSpec((RANK, FF_TILE), lambda f: (0, f + steps)),
            tile,
        ],
        out_specs=[whole((ROWS, D))] * 3 + [row, row, whole((2 * RANK, D)), tile, tile, tile, row],
        out_shape=[
            jax.ShapeDtypeStruct((ROWS, D), BF16), wide, wide,
            thin, thin, jax.ShapeDtypeStruct((2 * RANK, D), F32), thin_ff, thin_ff, thin_ff, thin,
        ],
        scratch_shapes=[
            pltpu.VMEM((ROWS, D), F32), pltpu.VMEM((ROWS, D), BF16),
            pltpu.VMEM((2, ROWS, RANK), BF16), pltpu.VMEM((ROWS, RANK), BF16),
            pltpu.VMEM((ROWS, D), F32), pltpu.VMEM((ROWS, D), F32),
            pltpu.VMEM((ROWS, RANK), F32), pltpu.VMEM((2, ROWS, RANK), F32),
        ],
        compiler_params=params(),
        name="second_half",
        cost_estimate=cost(23),
    )(merged, tokens, grad, gain, w_og, w_og, out_low, out_up, ffn_low, proj_up,
      w_og, w_og, w_down, ffn_up, ffn_up, proj_low)


def repaired(grown_ref, edge_ref, back_ref):
    end = edge_ref[0] + back_ref[0].astype(F32)
    return jnp.concatenate([grown_ref[0, : ROWS - 8, :].astype(F32), end], axis=0).astype(BF16)


def inner_kernel(
    grown_ref, edge_ref, back_ref, inner_ref, up_ref, gate_inner, first_ref,
    inner_out, g_up, g_low,
):
    block = pl.program_id(0)
    grown = repaired(grown_ref, edge_ref, back_ref)
    inner_out[block] = nt(grown, up_ref[...]).astype(BF16)
    up = tn(inner_ref[0], grown)
    g_up[0] = up[:, : D // 2]
    g_up[1] = up[:, D // 2 :]

    @pl.when(block == pl.num_programs(0) - 1)
    def _():
        inner_out[3] = gate_inner[...].astype(BF16)
        for j in range(4):
            low = tn(inner_out[j], first_ref[...])
            for owner in range(8):
                g_low[owner, :, j * 128 : (j + 1) * 128] = low[:, owner * 128 : (owner + 1) * 128]


def block_piece(rows):
    return pl.BlockSpec((1, rows, D), lambda t: (t, 0, 0))


def inner_part(grown, edge, back, inner, up, gate_inner, first):
    return pl.pallas_call(
        inner_kernel,
        grid=(3,),
        in_specs=[
            block_piece(ROWS), block_piece(8), block_piece(8),
            pl.BlockSpec((1, ROWS, RANK), lambda t: (t, 0, 0)),
            pl.BlockSpec((RANK, D), lambda t: (0, t)),
            whole((ROWS, RANK)), whole((ROWS, D)),
        ],
        out_specs=[
            whole((4, ROWS, RANK)),
            pl.BlockSpec((2, RANK, D // 2), lambda t: (t, 0, 0)),
            whole((8, RANK, D // 2)),
        ],
        out_shape=[
            jax.ShapeDtypeStruct((4, ROWS, RANK), BF16),
            jax.ShapeDtypeStruct((6, RANK, D // 2), F32),
            jax.ShapeDtypeStruct((8, RANK, D // 2), F32),
        ],
        compiler_params=params(),
        name="inner_part",
        cost_estimate=cost(4),
    )(grown, edge, back, inner, up, gate_inner, first)


def last_kernel(
    grown_ref, edge_ref, back_ref, w_ref, inner_ref, gate_ref, tokens_ref, gain_ref,
    low_ref, logits_ref, rates_ref, dmid_ref, out_ref, acc,
):
    step = pl.program_id(0)

    @pl.when(step == 0)
    def _():
        acc[...] = gate_ref[...]

    acc[...] += nt(repaired(grown_ref, edge_ref, back_ref), w_ref[...])

    @pl.when(step == pl.num_programs(0) - 1)
    def _():
        x = tokens_ref[...].astype(F32)
        total = acc[...] + nn(logits_ref[...], rates_ref[...])
        for j in range(4):
            total = total + nn(inner_ref[j], low_ref[j * RANK : (j + 1) * RANK, :])
        out_ref[...] = dmid_ref[...] + rms_back(x, gain_ref[...], total)


def last(grown, edge, back, w_in, inner, gate_part, tokens, gain, low, d_logits, rates, d_middle):
    return pl.pallas_call(
        last_kernel,
        grid=(3,),
        in_specs=[
            block_piece(ROWS), block_piece(8), block_piece(8),
            pl.BlockSpec((D, D), lambda t: (0, t)),
            whole((4, ROWS, RANK)),
            whole((ROWS, D)), whole((ROWS, D)), whole((1, D)),
            whole((4 * RANK, D)), whole((ROWS, 16)), whole((16, D)), whole((ROWS, D)),
        ],
        out_specs=whole((ROWS, D)),
        out_shape=jax.ShapeDtypeStruct((ROWS, D), F32),
        scratch_shapes=[pltpu.VMEM((ROWS, D), F32)],
        compiler_params=params(),
        name="last",
        cost_estimate=cost(9),
    )(grown, edge, back, w_in, inner, gate_part, tokens, gain, low, d_logits, rates, d_middle)


def gate_kernel(grown_ref, w_ref, inner_ref, up_ref, out_ref, inner_out, g_up):
    grown = grown_ref[...]
    out_ref[...] = nt(grown, w_ref[...])
    inner_out[...] = nt(grown, up_ref[...])
    up = tn(inner_ref[...], grown)
    g_up[0] = up[:, : D // 2]
    g_up[1] = up[:, D // 2 :]


def gate_part(grown, w_in, inner, up):
    return pl.pallas_call(
        gate_kernel,
        grid=(1,),
        in_specs=[
            whole((ROWS, D)),
            pl.BlockSpec((D, D), lambda t: (0, 3)),
            whole((ROWS, RANK)),
            pl.BlockSpec((RANK, D), lambda t: (0, 3)),
        ],
        out_specs=[whole((ROWS, D)), whole((ROWS, RANK)), whole((2, RANK, D // 2))],
        out_shape=[
            jax.ShapeDtypeStruct((ROWS, D), F32),
            jax.ShapeDtypeStruct((ROWS, RANK), F32),
            jax.ShapeDtypeStruct((2, RANK, D // 2), F32),
        ],
        compiler_params=params(),
        name="gate_part",
        cost_estimate=cost(3.5),
    )(grown, w_in, inner, up)


def along(axis, offset):
    count = lax.axis_size(axis)
    return [(i, (i + offset) % count) for i in range(count)]


def rep_pairs(dz, dx):
    return [(z * 4 + x, (z + dz) % 4 * 4 + (x + dx) % 4) for z in range(4) for x in range(4)]


def placed(gathered, sizes):
    n = gathered[0].shape[2] - 128

    def body(*refs):
        sources, outs, total = refs[: len(gathered)], refs[len(gathered) : -1], refs[-1]
        total[...] = jnp.zeros_like(total)
        for ref in sources:
            for s in range(ref.shape[0]):
                number = ref[s, :, n:].astype(F32)[:, :1]
                part = ref[s, :, :n].astype(F32)
                for a in range(8):
                    total[a] += jnp.where(number == a, part, 0.0)
        everything = total[...].reshape(8 * RANK, n)
        begin = 0
        for out, (rows, blocks) in zip(outs, sizes):
            padded = -(-rows // 128) * 128
            for m in range(blocks):
                out[:, m * 128 : (m + 1) * 128] = everything[:, begin : begin + padded].T[:rows]
                begin += padded

    return pl.pallas_call(
        body,
        in_specs=[pl.BlockSpec(memory_space=pltpu.VMEM)] * len(gathered),
        out_specs=[pl.BlockSpec(memory_space=pltpu.VMEM)] * len(sizes),
        out_shape=[jax.ShapeDtypeStruct((rows, blocks * 128), F32) for rows, blocks in sizes],
        scratch_shapes=[pltpu.VMEM((8, RANK, n), F32)],
        compiler_params=params(),
        name="placed",
        cost_estimate=cost(3),
    )(*gathered)


def numbered(sums, adapter):
    number = jnp.full((RANK, 128), adapter, F32).astype(sums.dtype)
    return jnp.concatenate([sums, number], axis=1)


def reduced_calls(stacked, adapter, sizes):
    own = lax.psum_scatter(stacked, "shard", scatter_dimension=0, tiled=False)
    return placed([lax.all_gather(numbered(own, adapter), "rep")], sizes)


def reduced(stacked, adapter, sizes):
    index = lax.axis_index("shard")
    y, core = index // 2, lax.rem(index, 2)
    n = stacked.shape[2]
    by_core = stacked.astype(BF16).reshape(4, 2, RANK, n)
    came = swap(lax.dynamic_index_in_dim(by_core, 1 - core, 1, False))
    chip = lax.dynamic_index_in_dim(by_core, core, 1, False).astype(F32) + came.astype(F32)
    total = lax.dynamic_index_in_dim(chip, y, 0, False)
    low = chip.astype(BF16)
    for step in (1, 2, 3):
        part = lax.dynamic_index_in_dim(low, lax.rem(y + step, 4), 0, False)
        total = total + lax.ppermute(part, "shard", along("shard", 2 * step)).astype(F32)
    own = numbered(total.astype(BF16), adapter)
    row = jnp.stack([own] + [lax.ppermute(own, "rep", rep_pairs(0, k)) for k in (1, 2, 3)])
    planes = [row] + [lax.ppermute(row, "rep", rep_pairs(k, 0)) for k in (1, 2, 3)]
    return placed(planes, sizes)


def chosen(array, adapter, blocks):
    rows = array.shape[0]
    span = array.shape[1] // blocks
    return jnp.concatenate(
        [
            lax.dynamic_slice(array, (0, b * span + adapter * RANK), (rows, RANK)).T
            for b in range(blocks)
        ],
        axis=0,
    )


def owners(part):
    split = part.reshape(RANK, 8, -1).transpose(1, 0, 2)
    return jnp.pad(split, ((0, 0), (0, 0), (0, -split.shape[2] % 128)))


def per_device(
    tokens, segment_ids, pad_mask, adapter_id, out_grad, gain_first, proj_in, proj_rates,
    conv_taps, decay_rate, ridge, gain_heads, proj_out, gain_second, proj_gu, proj_down,
    in_lower, in_upper, out_lower, out_upper, ffn_lower, ffn_upper, proj_lower, proj_upper,
):
    tail = CONV - 1
    adapter = adapter_id[0]
    w_in = lax.all_gather(proj_in, "shard", axis=0, tiled=True)
    own_og = jnp.concatenate([proj_gu, proj_out], axis=1)
    in_low, in_up = chosen(in_lower, adapter, 4), chosen(in_upper, adapter, 1)
    out_low, out_up = chosen(out_lower, adapter, 1), chosen(out_upper, adapter, 1)
    ffn_low, ffn_up = chosen(ffn_lower, adapter, 2), chosen(ffn_upper, adapter, 1)
    proj_low, proj_up = chosen(proj_lower, adapter, 1), chosen(proj_upper, adapter, 1)
    tail_ids = lax.ppermute(segment_ids[ROWS - tail :], "shard", [(i, i + 1) for i in range(7)])

    inputs = tokens.astype(F32)
    scale = lax.rsqrt(jnp.mean(inputs * inputs, axis=-1, keepdims=True) + 1e-06)
    first = (inputs * scale * gain_first).astype(BF16)
    inner_in = jnp.stack([nt(first, in_low[j * RANK : (j + 1) * RANK]) for j in range(4)]).astype(BF16)
    logits = nn(first, proj_rates)
    live = pad_mask.astype(F32)
    _, _, cols, rows, shift = token_scalars(logits, live, segment_ids, tail_ids, decay_rate)

    setup = (
        own_og, proj_down, first, inner_in, logits, cols, rows, shift,
        in_low, in_up, out_low, out_up, ffn_low, ffn_up, proj_low, proj_up,
    )
    (
        own_og, own_down, first, inner_in, logits, cols, rows, shift,
        in_low, in_up, out_low, out_up, ffn_low, ffn_up, proj_low, proj_up,
    ) = lax.optimization_barrier(setup)
    w_og = lax.all_gather(own_og, "shard", axis=0, tiled=True)
    w_down = lax.all_gather(own_down, "shard", axis=0, tiled=True)

    def handed_on(conv):
        return lax.ppermute(conv[ROWS - 16 :], "shard", [(i, i + 1) for i in range(7)])

    conv_kv = project(first, w_in, inner_in, in_up, D, 2 * D, BF16)
    tail_kv = handed_on(conv_kv)
    k, v, m_first, w_first, load = front(conv_kv, tail_kv, conv_taps, cols, rows)
    conv_q = project(first, w_in, inner_in, in_up, 0, D, BF16)
    gate_in = project(first, w_in, inner_in, in_up, 3 * D, D, F32)
    tail_q = handed_on(conv_q)
    q = front_query(conv_q, tail_q, conv_taps, cols)
    m0, w0 = exchanged(load, True)
    gain = gain_heads[None]
    merged, r, y, p, i = read(ridge, q, k, v, gate_in, gain, cols, rows, m0, w0, m_first, w_first)

    (mixed, d_middle, d_merged, g_out_low, g_out_up, g_ffn_low, g_up_a, g_up_b, g_proj_low, g_proj_up) = second_half(
        merged, tokens, out_grad, gain_second[None], w_og, w_down,
        out_low, out_up, ffn_low, ffn_up, proj_low, proj_up,
    )
    d_gate, dq, dk, dv, dcol, drow, load, dm1, dw1 = read_back(
        ridge, q, k, v, gate_in, gain, cols, rows, m0, w0, m_first, w_first, r, y, p, i, d_merged
    )
    early = jnp.concatenate(
        [owners(g) for g in (
            g_out_low, g_out_up, g_ffn_low[:RANK], g_ffn_low[RANK:],
            jnp.concatenate([g_up_a, g_up_b], axis=1), g_proj_low, g_proj_up,
        )],
        axis=2,
    )
    early = reduced_calls(early, adapter, [(128, 1), (128, 1), (128, 2), (704, 1), (352, 1), (128, 1)])
    gate_grad, gate_inner, g_up_gate = gate_part(d_gate, w_in, inner_in[3], in_up)
    dm2, dw2 = exchanged(load, False)
    grown, edge, top, dcol = front_back(
        conv_q, conv_kv, tail_q, tail_kv, conv_taps, cols, rows, shift, k, v, dq, dk, dv, dcol,
        m0, w0, m_first, w_first, dm1, dw1, dm2, dw2,
    )
    back = lax.ppermute(top, "shard", [(i + 1, i) for i in range(7)])
    d_logits = scalar_back(logits, live, decay_rate, dcol, drow).astype(BF16)
    inner_grads, g_up, g_low = inner_part(grown, edge, back, inner_in, in_up, gate_inner, first)
    late = jnp.concatenate([g_low, jnp.concatenate([g_up, g_up_gate], axis=0)], axis=2)
    token_grad = last(
        grown, edge, back, w_in, inner_grads, gate_grad, tokens, gain_first[None],
        in_low, d_logits, proj_rates.T, d_middle,
    )
    late = reduced(late, adapter, [(128, 4), (512, 1)])
    return (mixed, token_grad, late[0], late[1], *early)


def solution(mesh):
    whole_spec, by_shard, by_token = P(), P("shard", None), P(("rep", "shard"), None)
    by_row = P(("rep", "shard"))
    return jax.shard_map(
        per_device,
        mesh=mesh,
        in_specs=(
            by_token, by_row, by_row, P("rep"), by_token, whole_spec, by_shard, whole_spec,
            whole_spec, whole_spec, whole_spec, whole_spec, by_shard, whole_spec, by_shard, by_shard,
        )
        + (whole_spec,) * 8,
        out_specs=(by_token, by_token) + (by_shard,) * 8,
        check_vma=False,
    )
```

```python
import functools

import jax
import jax.numpy as jnp
from jax import lax
from jax.experimental import pallas as pl
from jax.experimental.pallas import tpu as pltpu
from jax.sharding import PartitionSpec as P

F32 = jnp.float32
BF16 = jnp.bfloat16
ROWS = 256
CHUNK = 128
HEADS = 8
HEAD = 128
D = 1024
FF = 2816
RANK = 16
CONV = 4
ITERS = 8
VMEM = 60 * 1024 * 1024
TOGETHER = 2
TOT, KEPT, SAME, IDS = 8, 16, 17, 20


def nt(a, b):
    return lax.dot_general(a, b, (((1,), (1,)), ((), ())), preferred_element_type=F32)


def nn(a, b):
    return lax.dot_general(a, b, (((1,), (0,)), ((), ())), preferred_element_type=F32)


def tn(a, b):
    return lax.dot_general(a, b, (((0,), (0,)), ((), ())), preferred_element_type=F32)


def halves(x):
    high = x.astype(BF16)
    return high, (x - high.astype(F32)).astype(BF16)


def left3(x, axis=1):
    high, rest = halves(x)
    return jnp.concatenate([high, rest, high], axis=axis)


def right3(x, axis):
    high, rest = halves(x)
    return jnp.concatenate([high, high, rest], axis=axis)


def row_dot(a, b):
    return jnp.sum(a * b, axis=1, keepdims=True)


def column(packed, index):
    lane = lax.broadcasted_iota(jnp.int32, packed.shape, 1)
    return jnp.sum(jnp.where(lane == index, packed, 0.0), axis=1, keepdims=True)


def sigmoid(x):
    return 1.0 / (1.0 + jnp.exp(-x))


def chunk_scalars(cols, row_ref, head, chunk, slot=0):
    begin = chunk * CHUNK
    part = cols[begin : begin + CHUNK]
    total = column(part, TOT + head)
    kept = column(part, KEPT)
    ids = column(part, IDS)
    span = slice(begin, begin + CHUNK)
    return {
        "beta": column(part, head),
        "total": total,
        "kept": kept,
        "ids": ids,
        "opening": jnp.exp(total) * kept,
        "beta_row": row_ref[slot, 0:1, span],
        "total_row": row_ref[slot, 1:2, span],
        "ids_row": row_ref[slot, 2:3, span],
    }


def weights_of(s):
    t = lax.broadcasted_iota(jnp.int32, (CHUNK, CHUNK), 0)
    u = lax.broadcasted_iota(jnp.int32, (CHUNK, CHUNK), 1)
    allowed = (t >= u) & (s["ids"] == s["ids_row"])
    return jnp.where(allowed, jnp.exp(jnp.where(allowed, s["total"] - s["total_row"], 0.0)), 0.0)


def weights_t_of(s):
    u = lax.broadcasted_iota(jnp.int32, (CHUNK, CHUNK), 0)
    t = lax.broadcasted_iota(jnp.int32, (CHUNK, CHUNK), 1)
    allowed = (t >= u) & (s["ids"] == s["ids_row"])
    return jnp.where(allowed, jnp.exp(jnp.where(allowed, s["total_row"] - s["total"], 0.0)), 0.0)


def last_weight(s):
    end = CHUNK - 1
    same = s["ids"] == s["ids"][end:]
    return jnp.where(same, jnp.exp(jnp.where(same, s["total"][end:] - s["total"], 0.0)), 0.0)


LOAD = 272


def places():
    return (
        lax.broadcasted_iota(jnp.int32, (HEAD, HEAD), 0),
        lax.broadcasted_iota(jnp.int32, (HEAD, HEAD), 1),
    )


def extra_rows(opening, diagonal):
    row = lax.broadcasted_iota(jnp.int32, (16, HEAD), 0)
    high, rest = halves(opening)
    out = jnp.where(row == 1, high.astype(F32), jnp.where(row == 2, rest.astype(F32), 0.0))
    return jnp.where(row == 0, diagonal, out).astype(BF16)


def pack_state(opening, memory, lookup):
    r, c = places()
    high, rest = halves(memory)
    high, rest = high.astype(F32), rest.astype(F32)
    diagonal = jnp.sum(jnp.where(r == c, rest, 0.0), axis=0, keepdims=True)
    mixed = jnp.where(r >= c, high, rest).astype(BF16)
    return jnp.concatenate([mixed, lookup.astype(BF16), extra_rows(opening, diagonal)], axis=0)


def unpack_state(load):
    r, c = places()
    x = load.astype(F32)
    mixed, extra = x[:HEAD], x[2 * HEAD :]
    turned = mixed.T
    high = jnp.where(r >= c, mixed, turned)
    rest = jnp.where(r < c, mixed, jnp.where(r > c, turned, extra[0:1]))
    return extra[1:2, 0:1] + extra[2:3, 0:1], high + rest, x[HEAD : 2 * HEAD]


def pack_plain(opening, memory, lookup):
    zero = jnp.zeros((1, HEAD), F32)
    return jnp.concatenate(
        [memory.astype(BF16), lookup.astype(BF16), extra_rows(opening, zero)], axis=0
    )


def unpack_plain(load):
    x = load.astype(F32)
    extra = x[2 * HEAD :]
    return extra[1:2, 0:1] + extra[2:3, 0:1], x[:HEAD], x[HEAD : 2 * HEAD]


def then(earlier, later):
    return tuple([earlier[0] * later[0]] + [later[0] * a + b for a, b in zip(earlier[1:], later[1:])])


def back_then(earlier, later):
    return tuple([earlier[0] * later[0]] + [a + earlier[0] * b for a, b in zip(earlier[1:], later[1:])])


def pair_kernel(forward, core_ref, mine_ref, came_ref, out_ref):
    pack, unpack = (pack_state, unpack_state) if forward else (pack_plain, unpack_plain)
    core = core_ref[0]
    for n in range(HEADS // 2):
        mine = jnp.where(core == 0, mine_ref[n], mine_ref[n + HEADS // 2])
        came = came_ref[n]
        first = unpack(jnp.where(core == 0, mine, came))
        second = unpack(jnp.where(core == 0, came, mine))
        out_ref[n] = pack(*(then if forward else back_then)(first, second))


def entry_kernel(forward, core_ref, mine_ref, came_ref, near_ref, middle_ref, far_ref, m_ref, w_ref, out_ref):
    pack, unpack = (pack_state, unpack_state) if forward else (pack_plain, unpack_plain)
    core = core_ref[0]
    for n in range(HEADS // 2):
        mine = jnp.where(core == 0, mine_ref[n], mine_ref[n + HEADS // 2])
        near, middle, far = unpack(near_ref[n]), unpack(middle_ref[n]), unpack(far_ref[n])
        own_first = core == 0
        if forward:
            outer = then(then(far, middle), near)
            inner = then(outer, unpack(jnp.where(own_first, mine, came_ref[n])))
            own = [jnp.where(own_first, a, b) for a, b in zip(outer, inner)]
            other = [jnp.where(own_first, b, a) for a, b in zip(outer, inner)]
        else:
            outer = back_then(near, back_then(middle, far))
            inner = back_then(unpack(jnp.where(own_first, came_ref[n], mine)), outer)
            own = [jnp.where(own_first, b, a) for a, b in zip(outer, inner)]
            other = [jnp.where(own_first, a, b) for a, b in zip(outer, inner)]
        m_ref[n] = own[1]
        w_ref[n] = own[2]
        out_ref[n] = pack(*other)


def join_kernel(forward, core_ref, own_m, own_w, came_ref, m_ref, w_ref):
    unpack = unpack_state if forward else unpack_plain
    core = core_ref[0]
    for n in range(HEADS // 2):
        _, memory, lookup = unpack(came_ref[n])
        for out, own, came in ((m_ref, own_m[n], memory), (w_ref, own_w[n], lookup)):
            out[n] = jnp.where(core == 0, own, came)
            out[n + HEADS // 2] = jnp.where(core == 0, came, own)


def small_call(kernel, forward, outs, *operands):
    return pl.pallas_call(
        functools.partial(kernel, forward),
        in_specs=[pl.BlockSpec(memory_space=pltpu.SMEM)]
        + [pl.BlockSpec(memory_space=pltpu.VMEM)] * (len(operands) - 1),
        out_specs=[pl.BlockSpec(memory_space=pltpu.VMEM)] * len(outs),
        out_shape=outs,
        compiler_params=params(),
        cost_estimate=cost(2),
    )(*operands)


def swap(value):
    count = lax.axis_size("shard")
    return lax.ppermute(value, "shard", [(i, i ^ 1) for i in range(count)])


def over_chips(value, steps):
    count = lax.axis_size("shard")
    pairs = [(i, i + 2 * steps) for i in range(count) if 0 <= i + 2 * steps < count]
    return lax.ppermute(value, "shard", pairs)


def exchanged(load, forward, inputs, work):
    half = HEADS // 2
    core = lax.rem(lax.axis_index("shard"), 2)
    scalar = core.reshape(1)
    packed = jax.ShapeDtypeStruct((half, LOAD, HEAD), BF16)
    states = jax.ShapeDtypeStruct((half, HEAD, HEAD), F32)
    full = jax.ShapeDtypeStruct((HEADS, HEAD, HEAD), F32)
    came = swap(lax.dynamic_slice_in_dim(load, (1 - core) * half, half, 0))
    (chip,) = small_call(pair_kernel, forward, [packed], scalar, load, came)
    chip, inputs = lax.optimization_barrier((chip, inputs))
    others = [over_chips(chip, n if forward else -n) for n in (1, 2, 3)]
    beside = work(*inputs)
    others, beside = lax.optimization_barrier((others, beside))
    own_m, own_w, out = small_call(
        entry_kernel, forward, [states, states, packed], scalar, load, came, *others
    )
    return small_call(join_kernel, forward, [full, full], scalar, own_m, own_w, swap(out)), beside


def conv_rows(x_ref, tail_ref, taps_ref, ext_ref, spot, cols, lanes):
    ext = ext_ref.at[spot]
    ext[0:8, :] = tail_ref[8:16, lanes].astype(F32)
    ext[8 : 8 + ROWS, :] = x_ref[:, lanes].astype(F32)
    total = taps_ref[0:1, lanes] * ext[8 : 8 + ROWS, :]
    for j in range(1, CONV):
        same = cols[:, SAME + j - 1 : SAME + j]
        total = total + (taps_ref[j : j + 1, lanes] * ext[8 - j : 8 - j + ROWS, :]) * same
    return total


def front_kernel(
    k_in, v_in, k_tail, v_tail, k_taps, v_taps, cols_ref, row_ref,
    k_out, v_out, m_first, w_first, load_ref, ext,
):
    cols = cols_ref[...]
    for slot in range(TOGETHER):
        head = pl.program_id(0) * TOGETHER + slot
        lanes = slice(slot * HEAD, (slot + 1) * HEAD)
        acts = []
        for n, (x_ref, tail_ref, taps_ref) in enumerate(((k_in, k_tail, k_taps), (v_in, v_tail, v_taps))):
            c = conv_rows(x_ref, tail_ref, taps_ref, ext, 2 * slot + n, cols, lanes)
            acts.append(c * sigmoid(c))
        k, v = acts
        k = k * lax.rsqrt(row_dot(k, k) + 1e-06)
        k_out[:, lanes] = k
        v_out[:, lanes] = v
        parts = []
        for chunk in range(2):
            begin = chunk * CHUNK
            s = chunk_scalars(cols, row_ref, head, chunk, slot)
            kc, vc = k[begin : begin + CHUNK], v[begin : begin + CHUNK]
            last = last_weight(s) * s["beta"]
            right = right3(kc, 0)
            parts.append((
                tn(left3(kc * last, 0), right), tn(left3(vc * last, 0), right), s["opening"][CHUNK - 1 :]
            ))
        m_first[slot] = parts[0][0]
        w_first[slot] = parts[0][1]
        o2 = parts[1][2]
        load_ref[slot] = pack_state(
            parts[0][2] * o2, o2 * parts[0][0] + parts[1][0], o2 * parts[0][1] + parts[1][1]
        )


def query_kernel(q_in, q_tail, q_taps, cols_ref, q_out, ext):
    for slot in range(TOGETHER):
        lanes = slice(slot * HEAD, (slot + 1) * HEAD)
        c = conv_rows(q_in, q_tail, q_taps, ext, slot, cols_ref[...], lanes)
        q = c * sigmoid(c)
        q_out[:, lanes] = q * lax.rsqrt(row_dot(q, q) + 1e-06)


def head_block(rows, offset=0, heads=1):
    return pl.BlockSpec((rows, heads * HEAD), lambda h: (0, h + offset))


def whole(shape):
    return pl.BlockSpec(shape, lambda h: (0,) * len(shape))


def head_rows(count, heads=1):
    return pl.BlockSpec((heads, count, ROWS), lambda h: (h, 0, 0))


def square(heads=1):
    return pl.BlockSpec((heads, HEAD, HEAD), lambda h: (h, 0, 0))


def loads(heads=1):
    return pl.BlockSpec((heads, LOAD, HEAD), lambda h: (h, 0, 0))


def params():
    return pltpu.CompilerParams(vmem_limit_bytes=VMEM)


def cost(micros):
    return pl.CostEstimate(
        flops=int(micros * 1.15e9), bytes_accessed=int(micros * 3.0e6), transcendentals=0
    )


def front(conv_kv, tail_kv, taps, cols, rows):
    flat = jax.ShapeDtypeStruct((ROWS, D), F32)
    states = jax.ShapeDtypeStruct((HEADS, HEAD, HEAD), F32)
    per = HEADS // TOGETHER
    return pl.pallas_call(
        front_kernel,
        grid=(per,),
        in_specs=[head_block(ROWS, o, TOGETHER) for o in (0, per)]
        + [head_block(16, o, TOGETHER) for o in (0, per)]
        + [head_block(CONV, o, TOGETHER) for o in (per, 2 * per)]
        + [whole((ROWS, 128)), head_rows(8, TOGETHER)],
        out_specs=[head_block(ROWS, 0, TOGETHER)] * 2 + [square(TOGETHER)] * 2 + [loads(TOGETHER)],
        out_shape=[flat] * 2 + [states] * 2 + [jax.ShapeDtypeStruct((HEADS, LOAD, HEAD), BF16)],
        scratch_shapes=[pltpu.VMEM((2 * TOGETHER, ROWS + 8, HEAD), F32)],
        compiler_params=params(),
        name="front",
        cost_estimate=cost(6.4),
    )(conv_kv, conv_kv, tail_kv, tail_kv, taps, taps, cols, rows)


def front_query(conv_q, tail_q, taps, cols):
    return pl.pallas_call(
        query_kernel,
        grid=(HEADS // TOGETHER,),
        in_specs=[head_block(n, 0, TOGETHER) for n in (ROWS, 16, CONV)] + [whole((ROWS, 128))],
        out_specs=head_block(ROWS, 0, TOGETHER),
        out_shape=jax.ShapeDtypeStruct((ROWS, D), F32),
        scratch_shapes=[pltpu.VMEM((TOGETHER, ROWS + 8, HEAD), F32)],
        compiler_params=params(),
        name="front_query",
        cost_estimate=cost(4.5),
    )(conv_q, tail_q, taps, cols)


def read_kernel(
    ridge_ref, q_ref, k_ref, v_ref, gate_ref, gain_ref, cols_ref, row_ref,
    m0_ref, w0_ref, m_first, w_first, merged_ref, r_ref, y_ref, p_ref, i_ref,
):
    cols = cols_ref[...]
    chains = []
    for slot in range(TOGETHER):
        head = pl.program_id(0) * TOGETHER + slot
        lanes = slice(slot * HEAD, (slot + 1) * HEAD)
        memory, lookup = m0_ref[slot], w0_ref[slot]
        for chunk in range(2):
            begin = chunk * CHUNK
            at = slice(begin, begin + CHUNK)
            s = chunk_scalars(cols, row_ref, head, chunk, slot)
            if chunk == 1:
                o1 = chains[-1]["o"][CHUNK - 1 :]
                memory = o1 * memory + m_first[slot]
                lookup = o1 * lookup + w_first[slot]
            kc = k_ref[at, lanes]
            q = q_ref[at, lanes]
            chains.append({
                "at": (at, lanes),
                "lanes": lanes,
                "ridge": ridge_ref[head],
                "g": weights_of(s) * s["beta_row"],
                "o": s["opening"],
                "score": jnp.concatenate([right3(kc, 1), right3(memory, 1)], axis=0),
                "score_w": jnp.concatenate([right3(kc, 1), right3(lookup, 1)], axis=0),
                "keys": right3(kc, 0),
                "y": jnp.zeros_like(q),
                "r": q,
                "p": q,
                "rr": row_dot(q, q),
            })
    for j in range(ITERS):
        boths = [nt(left3(c["p"]), c["score"]) for c in chains]
        mixings = [left3(c["g"] * both[:, :CHUNK]) for c, both in zip(chains, boths)]
        recents = [nn(mixing, c["keys"]) for c, mixing in zip(chains, mixings)]
        for c, both, recent in zip(chains, boths, recents):
            p = c["p"]
            image = recent + c["o"] * both[:, CHUNK:] + c["ridge"] * p
            p_ref[(j,) + c["at"]] = p
            i_ref[(j,) + c["at"]] = image
            alpha = c["rr"] / (row_dot(p, image) + 0.01)
            c["y"] = c["y"] + alpha * p
            if j < ITERS - 1:
                c["r"] = c["r"] - alpha * image
                following = row_dot(c["r"], c["r"])
                c["p"] = c["r"] + (following / (c["rr"] + 0.01)) * p
                c["rr"] = following
    for c in chains:
        both = nt(left3(c["y"]), c["score_w"])
        mixing = c["g"] * both[:, :CHUNK]
        out = nn(left3(mixing), right3(v_ref[c["at"]], 0)) + c["o"] * both[:, CHUNK:]
        y_ref[c["at"]] = c["y"]
        r_ref[c["at"]] = out
        gain = gain_ref[:, c["lanes"]]
        normed = out * lax.rsqrt(row_dot(out, out) * (1.0 / HEAD) + 1e-06) * gain
        gate = gate_ref[c["at"]]
        merged_ref[c["at"]] = (normed * (gate * sigmoid(gate))).astype(BF16)


def read(ridge, q, k, v, gate, gain, cols, rows, m0, w0, m_first, w_first):
    flat = jax.ShapeDtypeStruct((ROWS, D), F32)
    steps = jax.ShapeDtypeStruct((ITERS, ROWS, D), F32)
    step_block = pl.BlockSpec((ITERS, ROWS, TOGETHER * HEAD), lambda h: (0, 0, h))
    return pl.pallas_call(
        read_kernel,
        grid=(HEADS // TOGETHER,),
        in_specs=[pl.BlockSpec(memory_space=pltpu.SMEM)]
        + [head_block(ROWS, 0, TOGETHER)] * 4
        + [head_block(1, 0, TOGETHER), whole((ROWS, 128)), head_rows(8, TOGETHER)]
        + [square(TOGETHER)] * 4,
        out_specs=[head_block(ROWS, 0, TOGETHER)] * 3 + [step_block] * 2,
        out_shape=[jax.ShapeDtypeStruct((ROWS, D), BF16), flat, flat, steps, steps],
        compiler_params=params(),
        name="readout",
        cost_estimate=cost(26),
    )(ridge, q, k, v, gate, gain, cols, rows, m0, w0, m_first, w_first)


def read_back_kernel(
    ridge_ref, q_ref, k_ref, v_ref, gate_ref, gain_ref, cols_ref, row_ref,
    m0_ref, w0_ref, m_first, w_first, r_ref, y_ref, p_ref, i_ref, dm_ref,
    dgate_ref, dq_ref, dk_ref, dv_ref, dcol_ref, drow_ref, load_ref, dm1_ref, dw1_ref,
    stack_a, stack_b,
):
    cols = cols_ref[...]
    chains = []
    for slot in range(TOGETHER):
        head = pl.program_id(0) * TOGETHER + slot
        lanes = slice(slot * HEAD, (slot + 1) * HEAD)
        memory, lookup = m0_ref[slot], w0_ref[slot]
        for chunk in range(2):
            begin = chunk * CHUNK
            at = (slice(begin, begin + CHUNK), lanes)
            s = chunk_scalars(cols, row_ref, head, chunk, slot)
            if chunk == 1:
                o1 = chains[-1]["o"][CHUNK - 1 :]
                memory = o1 * memory + m_first[slot]
                lookup = o1 * lookup + w_first[slot]
            kc, vc, q, y = k_ref[at], v_ref[at], q_ref[at], y_ref[at]
            o = s["opening"]
            weights_t = weights_t_of(s)
            g = weights_of(s) * s["beta_row"]
            g_t = weights_t * s["beta"]
            out, gate, dm, gain = r_ref[at], gate_ref[at], dm_ref[at], gain_ref[:, lanes]
            scale = lax.rsqrt(row_dot(out, out) * (1.0 / HEAD) + 1e-06)
            sig = sigmoid(gate)
            dgate_ref[at] = (
                dm * (out * scale * gain) * (sig * (1.0 + gate * (1.0 - sig)))
            ).astype(BF16)
            dn = dm * (gate * sig) * gain
            dout = scale * dn - out * ((scale * scale * scale) * (row_dot(out, dn) * (1.0 / HEAD)))
            k_high, y_high, d_high, v_high = (a.astype(BF16) for a in (kc, y, dout, vc))
            dmix_dy = nn(left3(dout), right3(lookup, 0))
            dmix = nt(left3(dout), right3(vc, 1))
            keys = right3(kc, 0)
            score = jnp.concatenate([right3(kc, 1), right3(memory, 1)], axis=0)
            dy = nn(left3(g * dmix), keys) + o * dmix_dy
            s_t = nt(k_high, y_high)
            dmix_t = nt(v_high, d_high)
            dv_ref[at] = nn((g_t * s_t).astype(BF16), d_high)
            chains.append({
                "at": at, "g": g, "g_t": g_t, "w_t": weights_t, "o": o, "score": score, "keys": keys,
                "k_high": k_high, "dy": dy, "dk": nn((g_t * dmix_t).astype(BF16), y_high),
                "dg_t": dmix_t * s_t, "do": row_dot(y, dmix_dy),
                "dlookup": tn((o * dout).astype(BF16), y_high),
                "rs": [q], "rrs": [row_dot(q, q)], "alphas": [], "dens": [], "q": q,
                "number": slot * 2 + chunk, "head": head, "slot": slot, "ridge": ridge_ref[head],
                "r_bar": None, "p_bar": None, "rr_bar": None,
            })
    for j in range(ITERS):
        for c in chains:
            image = i_ref[(j,) + c["at"]]
            den = row_dot(p_ref[(j,) + c["at"]], image) + 0.01
            alpha = c["rrs"][j] / den
            c["alphas"].append(alpha)
            c["dens"].append(den)
            if j < ITERS - 1:
                r = c["rs"][j] - alpha * image
                c["rs"].append(r)
                c["rrs"].append(row_dot(r, r))
    for j in range(ITERS - 1, -1, -1):
        for c in chains:
            p, image = p_ref[(j,) + c["at"]], i_ref[(j,) + c["at"]]
            alpha, den, rr = c["alphas"][j], c["dens"][j], c["rrs"][j]
            dy = c["dy"]
            if j == ITERS - 1:
                alpha_bar = row_dot(dy, p)
                p_bar = alpha * dy
                rr_bar = alpha_bar / den
                den_bar = -alpha_bar * alpha / den
                i_bar = den_bar * p
                r_bar = None
            else:
                below = 1.0 / (rr + 0.01)
                b = c["rrs"][j + 1] * below
                b_bar = row_dot(c["p_bar"], p)
                r_bar = c["p_bar"] if c["r_bar"] is None else c["r_bar"] + c["p_bar"]
                rr_next = c["rr_bar"] + b_bar * below
                r_bar = r_bar + (2.0 * rr_next) * c["rs"][j + 1]
                alpha_bar = row_dot(dy, p) - row_dot(r_bar, image)
                p_bar = b * c["p_bar"] + alpha * dy
                rr_bar = alpha_bar / den - b_bar * b * below
                den_bar = -alpha_bar * alpha / den
                i_bar = den_bar * p - alpha * r_bar
            c["r_bar"], c["p_bar"], c["rr_bar"] = r_bar, p_bar + den_bar * image, rr_bar
            c["i_bar"], c["left"] = i_bar, left3(i_bar)
        boths = [nt(c["left"], c["score"]) for c in chains]
        mixes = [left3(c["g"] * both[:, :CHUNK]) for c, both in zip(chains, boths)]
        moves = [nn(mix, c["keys"]) for c, mix in zip(chains, mixes)]
        for c, both, moved in zip(chains, boths, moves):
            im = both[:, CHUNK:]
            p = p_ref[(j,) + c["at"]]
            c["p_bar"] = c["p_bar"] + moved + c["o"] * im + c["ridge"] * c["i_bar"]
            c["do"] = c["do"] + row_dot(p, im)
            i_high, p_high = c["left"][:, :CHUNK], p.astype(BF16)
            turned = nt(c["k_high"], jnp.concatenate([p_high, i_high], axis=0))
            s_t, d_t = turned[:, :CHUNK], turned[:, CHUNK:]
            c["dg_t"] = c["dg_t"] + s_t * d_t
            c["dk"] = c["dk"] + nn(
                jnp.concatenate([c["g_t"] * s_t, c["g_t"] * d_t], axis=1).astype(BF16),
                jnp.concatenate([i_high, p_high], axis=0),
            )
            rows = slice(j * CHUNK, (j + 1) * CHUNK)
            stack_a[c["number"], rows, :] = (c["o"] * c["i_bar"]).astype(BF16)
            stack_b[c["number"], rows, :] = p_high
    lane = lax.broadcasted_iota(jnp.int32, (CHUNK, 128), 1)
    for c in chains:
        at = c["at"]
        dq_ref[at] = c["r_bar"] + c["p_bar"] + (2.0 * c["rr_bar"]) * c["q"]
        dk_ref[at] = c["dk"]
        c["dmem"] = tn(stack_a[c["number"]], stack_b[c["number"]])
        scaled = c["dg_t"] * c["w_t"]
        z_t = c["dg_t"] * c["g_t"]
        dbeta = jnp.sum(scaled, axis=1, keepdims=True)
        dtotal = c["do"] * c["o"] - jnp.sum(z_t, axis=1, keepdims=True)
        span, head = at[0], c["head"]
        dcol_ref[span, :] = jnp.where(
            lane == head, dbeta, jnp.where(lane == TOT + head, dtotal, dcol_ref[span, :])
        )
        drow_ref[c["slot"], :, span] = jnp.sum(z_t, axis=0, keepdims=True)
    for slot in range(TOGETHER):
        one, two = chains[2 * slot], chains[2 * slot + 1]
        o1 = one["o"][CHUNK - 1 :]
        load_ref[slot] = pack_plain(
            o1 * two["o"][CHUNK - 1 :],
            one["dmem"] + o1 * two["dmem"],
            one["dlookup"] + o1 * two["dlookup"],
        )
        dm1_ref[slot] = two["dmem"]
        dw1_ref[slot] = two["dlookup"]


def read_back(ridge, q, k, v, gate, gain, cols, rows, m0, w0, m_first, w_first, r, y, p, i, dm):
    flat = jax.ShapeDtypeStruct((ROWS, D), F32)
    states = jax.ShapeDtypeStruct((HEADS, HEAD, HEAD), F32)
    step_block = pl.BlockSpec((ITERS, ROWS, TOGETHER * HEAD), lambda h: (0, 0, h))
    return pl.pallas_call(
        read_back_kernel,
        grid=(HEADS // TOGETHER,),
        in_specs=[pl.BlockSpec(memory_space=pltpu.SMEM)]
        + [head_block(ROWS, 0, TOGETHER)] * 4
        + [head_block(1, 0, TOGETHER), whole((ROWS, 128)), head_rows(8, TOGETHER)]
        + [square(TOGETHER)] * 4
        + [head_block(ROWS, 0, TOGETHER)] * 2
        + [step_block] * 2
        + [head_block(ROWS, 0, TOGETHER)],
        out_specs=[head_block(ROWS, 0, TOGETHER)] * 4
        + [whole((ROWS, 128)), head_rows(1, TOGETHER)]
        + [loads(TOGETHER)]
        + [square(TOGETHER)] * 2,
        out_shape=[jax.ShapeDtypeStruct((ROWS, D), BF16)]
        + [flat] * 3
        + [jax.ShapeDtypeStruct((ROWS, 128), F32), jax.ShapeDtypeStruct((HEADS, 1, ROWS), F32)]
        + [jax.ShapeDtypeStruct((HEADS, LOAD, HEAD), BF16)]
        + [states] * 2,
        scratch_shapes=[
            pltpu.VMEM((2 * TOGETHER, ITERS * CHUNK, HEAD), BF16),
            pltpu.VMEM((2 * TOGETHER, ITERS * CHUNK, HEAD), BF16),
        ],
        compiler_params=params(),
        name="readout_back",
        cost_estimate=cost(39),
    )(ridge, q, k, v, gate, gain, cols, rows, m0, w0, m_first, w_first, r, y, p, i, dm)


def front_back_kernel(
    q_in, k_in, v_in, q_tail, k_tail, v_tail, q_taps, k_taps, v_taps, cols_ref, row_ref, shift_ref,
    k_ref, v_ref, dq_ref, dk_ref, dv_ref, dcol_ref,
    m0_ref, w0_ref, m_first, w_first, dm1_ref, dw1_ref, dm2_ref, dw2_ref,
    out_ref, edge_ref, top_ref, dcol_out, ext, grown_ref,
):
    cols = cols_ref[...]
    lane = lax.broadcasted_iota(jnp.int32, (CHUNK, 128), 1)
    row = lax.broadcasted_iota(jnp.int32, (CHUNK, 1), 0)
    added = [dcol_ref[:CHUNK, :], dcol_ref[CHUNK:, :]]
    fresh = pl.program_id(0) == 0
    added = [jnp.where(fresh, a, dcol_out[c * CHUNK : (c + 1) * CHUNK, :]) for c, a in enumerate(added)]
    for slot in range(TOGETHER):
        head = pl.program_id(0) * TOGETHER + slot
        lanes = slice(slot * HEAD, (slot + 1) * HEAD)
        s1 = chunk_scalars(cols, row_ref, head, 0, slot)
        s2 = chunk_scalars(cols, row_ref, head, 1, slot)
        o1, o2 = s1["opening"][CHUNK - 1 :], s2["opening"][CHUNK - 1 :]
        dm2, dw2 = dm2_ref[slot], dw2_ref[slot]
        m0, w0 = m0_ref[slot], w0_ref[slot]
        m1, w1 = o1 * m0 + m_first[slot], o1 * w0 + w_first[slot]
        dm1, dw1 = dm1_ref[slot] + o2 * dm2, dw1_ref[slot] + o2 * dw2
        dks, dvs = [], []
        for chunk, s, dm, dw, m, w in ((0, s1, dm1, dw1, m0, w0), (1, s2, dm2, dw2, m1, w1)):
            at = (slice(chunk * CHUNK, (chunk + 1) * CHUNK), lanes)
            kc, vc = k_ref[at], v_ref[at]
            weight = last_weight(s)
            last = weight * s["beta"]
            kb, vb, dmb, dwb = (a.astype(BF16) for a in (kc, vc, dm, dw))
            mk = nt(kb, dmb)
            wk = nt(kb, dwb)
            dks.append(dk_ref[at] + last * (mk + nn(kb, dmb) + nn(vb, dwb)))
            dvs.append(dv_ref[at] + last * wk)
            dlast = jnp.sum(kc * mk + vc * wk, axis=1, keepdims=True)
            part = dlast * last
            do = jnp.sum(jnp.sum(dm * m + dw * w, axis=0, keepdims=True), axis=1, keepdims=True)
            at_end = do * s["opening"][CHUNK - 1 :] + jnp.sum(part, axis=0, keepdims=True)
            dtotal = jnp.where(row == CHUNK - 1, at_end - part, -part)
            added[chunk] = added[chunk] + jnp.where(
                lane == head, dlast * weight, jnp.where(lane == TOT + head, dtotal, 0.0)
            )
        dk = jnp.concatenate(dks, axis=0)
        dv = jnp.concatenate(dvs, axis=0)
        for n, (x_ref, tail_ref, taps_ref, grad, unit) in enumerate((
            (q_in, q_tail, q_taps, dq_ref[:, lanes], True),
            (k_in, k_tail, k_taps, dk, True),
            (v_in, v_tail, v_taps, dv, False),
        )):
            c = conv_rows(x_ref, tail_ref, taps_ref, ext, 3 * slot + n, cols, lanes)
            sig = sigmoid(c)
            if unit:
                act = c * sig
                scale = lax.rsqrt(row_dot(act, act) + 1e-06)
                grad = scale * grad - act * ((scale * scale * scale) * row_dot(act, grad))
            dc = grad * (sig * (1.0 + c * (1.0 - sig)))
            grown = grown_ref.at[3 * slot + n]
            grown[0:8, :] = jnp.zeros((8, HEAD), F32)
            grown[8 : 8 + ROWS, :] = dc
            grown[8 + ROWS :, :] = jnp.zeros((8, HEAD), F32)
            total = taps_ref[0:1, lanes] * grown[0 : ROWS + 8, :]
            for j in range(1, CONV):
                mask = shift_ref[:, j : j + 1]
                total = total + (taps_ref[j : j + 1, lanes] * grown[j : j + ROWS + 8, :]) * mask
            out_ref[n, :, lanes] = total[8:, :].astype(BF16)
            edge_ref[n, :, lanes] = total[ROWS:, :]
            top_ref[n, :, lanes] = total[:8, :].astype(BF16)
    for chunk in range(2):
        dcol_out[chunk * CHUNK : (chunk + 1) * CHUNK, :] = added[chunk]


def front_back(conv_q, conv_kv, tail_q, tail_kv, taps, cols, rows, shift, k, v, dq, dk, dv, dcol,
               m0, w0, m_first, w_first, dm1, dw1, dm2, dw2):
    per = HEADS // TOGETHER

    def stacked(count):
        return pl.BlockSpec((3, count, TOGETHER * HEAD), lambda h: (0, 0, h))

    return pl.pallas_call(
        front_back_kernel,
        grid=(per,),
        in_specs=[head_block(ROWS, o, TOGETHER) for o in (0, 0, per)]
        + [head_block(16, o, TOGETHER) for o in (0, 0, per)]
        + [head_block(CONV, o, TOGETHER) for o in (0, per, 2 * per)]
        + [whole((ROWS, 128)), head_rows(8, TOGETHER), whole((ROWS + 8, 128))]
        + [head_block(ROWS, 0, TOGETHER)] * 5
        + [whole((ROWS, 128))]
        + [square(TOGETHER)] * 8,
        out_specs=[stacked(ROWS), stacked(8), stacked(8), whole((ROWS, 128))],
        out_shape=[
            jax.ShapeDtypeStruct((3, ROWS, D), BF16),
            jax.ShapeDtypeStruct((3, 8, D), F32),
            jax.ShapeDtypeStruct((3, 8, D), BF16),
            jax.ShapeDtypeStruct((ROWS, 128), F32),
        ],
        scratch_shapes=[
            pltpu.VMEM((3 * TOGETHER, ROWS + 8, HEAD), F32),
            pltpu.VMEM((3 * TOGETHER, ROWS + 16, HEAD), F32),
        ],
        compiler_params=params(),
        name="front_back",
        cost_estimate=cost(10),
    )(conv_q, conv_kv, conv_kv, tail_q, tail_kv, tail_kv, taps, taps, taps, cols, rows, shift,
      k, v, dq, dk, dv, dcol, m0, w0, m_first, w_first, dm1, dw1, dm2, dw2)


def running_sums():
    t = lax.broadcasted_iota(jnp.int32, (ROWS, ROWS), 0)
    u = lax.broadcasted_iota(jnp.int32, (ROWS, ROWS), 1)
    return ((t >= u) & (t // CHUNK == u // CHUNK)).astype(F32)


def scalar_back(logits, live, decay_rate, dcol, drow):
    dtotal = dcol[:, TOT : TOT + HEADS] + drow[:, 0].T
    dbeta = dcol[:, :HEADS]
    ddecay = lax.dot_general(
        running_sums(), dtotal, (((0,), (0,)), ((), ())), precision=lax.Precision.HIGHEST
    )
    sig = jax.nn.sigmoid(logits[:, :HEADS])
    slope = jax.nn.sigmoid(logits[:, HEADS : 2 * HEADS] + 1.0)
    return jnp.concatenate(
        [dbeta * live[:, None] * sig * (1.0 - sig), -decay_rate[None, :] * slope * ddecay], axis=1
    )


def choose_kernel(counts, adapter_ref, *refs):
    adapter = adapter_ref[0]
    row = lax.broadcasted_iota(jnp.int32, (RANK, 128), 0)
    lane = lax.broadcasted_iota(jnp.int32, (RANK, 128), 1)
    picks = jnp.where(lane == row + adapter * RANK, 1.0, 0.0).astype(BF16)
    for n, blocks in enumerate(counts):
        source, out = refs[n], refs[n + len(counts)]
        for b in range(blocks):
            part = nt(picks, source[:, b * 128 : (b + 1) * 128])
            out[b * RANK : (b + 1) * RANK, :] = part.astype(BF16)


def choose(adapter_id, arrays):
    counts = [a.shape[1] // 128 for a in arrays]
    vmem = pl.BlockSpec(memory_space=pltpu.VMEM)
    return pl.pallas_call(
        functools.partial(choose_kernel, counts),
        in_specs=[pl.BlockSpec(memory_space=pltpu.SMEM)] + [vmem] * len(arrays),
        out_specs=[vmem] * len(arrays),
        out_shape=[jax.ShapeDtypeStruct((RANK * c, a.shape[0]), BF16) for c, a in zip(counts, arrays)],
        compiler_params=params(),
        name="choose",
        cost_estimate=cost(5),
    )(adapter_id, *arrays)


def softplus(x):
    return jnp.maximum(x, 0.0) + jnp.log(1.0 + jnp.exp(-jnp.abs(x)))


def setup_kernel(
    tokens_ref, gain_ref, low_ref, rates_ref, wide_ref, live_ref, live_row_ref, ids_ref, ids_row_ref,
    decay_row_ref, decay_col_ref,
    first_ref, inner_ref, logits_ref, cols_ref, rows_ref, shift_ref, spread,
):
    x = tokens_ref[...].astype(F32)
    first = (x * lax.rsqrt(row_dot(x, x) * (1.0 / D) + 1e-06) * gain_ref[...]).astype(BF16)
    first_ref[...] = first
    for j in range(4):
        inner_ref[j] = nt(first, low_ref[j * RANK : (j + 1) * RANK, :]).astype(BF16)
    t = lax.broadcasted_iota(jnp.int32, (ROWS, ROWS), 0)
    u = lax.broadcasted_iota(jnp.int32, (ROWS, ROWS), 1)
    together = (t < CHUNK) == (u < CHUNK)
    lower = jnp.where((t >= u) & together, 1.0, 0.0).astype(BF16)
    upper = jnp.where((t <= u) & together, 1.0, 0.0).astype(BF16)
    logits = nt(first, wide_ref[...])
    logits_ref[...] = logits
    beta = sigmoid(logits) * live_ref[...]
    total = summed3(lower, -decay_row_ref[...] * softplus(logits + 1.0), True)
    lane = lax.broadcasted_iota(jnp.int32, (ROWS, 128), 1)
    row = lax.broadcasted_iota(jnp.int32, (ROWS, 1), 0)
    ids = ids_ref[8:, :]
    before = jnp.where(row < CHUNK, ids_ref[7:8, :], ids_ref[7 + CHUNK : 8 + CHUNK, :])
    cols = jnp.where(lane < 8, beta, jnp.where(lane < 16, total, 0.0))
    cols = jnp.where(lane == KEPT, jnp.where(ids == before, 1.0, 0.0), cols)
    cols = jnp.where(lane == IDS, ids, cols)
    for j in range(1, CONV):
        same = jnp.where(ids_ref[8 - j : 8 - j + ROWS, :] == ids, 1.0, 0.0)
        cols = jnp.where(lane == SAME + j - 1, same, cols)
    cols_ref[...] = cols
    spread[0:8, :] = jnp.zeros((8, 128), F32)
    spread[8 : 8 + ROWS, :] = cols
    spread[8 + ROWS :, :] = jnp.zeros((8, 128), F32)
    out_lane = lax.broadcasted_iota(jnp.int32, (ROWS + 8, 128), 1)
    shift = jnp.zeros((ROWS + 8, 128), F32)
    for j in range(1, CONV):
        moved = column(spread[j : j + ROWS + 8, :], SAME + j - 1)
        shift = jnp.where(out_lane == j, moved, shift)
    shift_ref[...] = shift
    logits = nt(rates_ref[...], first)
    beta = sigmoid(logits) * live_row_ref[...]
    total = summed3(upper, -decay_col_ref[...] * softplus(logits + 1.0), False)
    rows_ref[...] = jnp.zeros_like(rows_ref)
    for h in range(HEADS):
        rows_ref[h, 0:1, :] = beta[h : h + 1, :]
        rows_ref[h, 1:2, :] = total[TOT + h : TOT + h + 1, :]
        rows_ref[h, 2:3, :] = ids_row_ref[...]


def summed3(ones, x, left):
    high = x.astype(BF16)
    rest = x - high.astype(F32)
    middle = rest.astype(BF16)
    low = (rest - middle.astype(F32)).astype(BF16)
    out = 0.0
    for part in (low, middle, high):
        out = out + (nn(ones, part) if left else nn(part, ones))
    return out


def set_up(tokens, gain, low, rates, live, ids, tail_ids, decay_rate):
    rates_t = rates.T
    wide = jnp.pad(rates_t, ((0, 128 - 2 * HEADS), (0, 0)))
    decay = jnp.concatenate([jnp.zeros_like(decay_rate), decay_rate])
    ids = ids.astype(F32)
    ext = jnp.concatenate([jnp.zeros((8 - CONV + 1,), F32), tail_ids.astype(F32), ids])
    vmem = pl.BlockSpec(memory_space=pltpu.VMEM)
    return pl.pallas_call(
        setup_kernel,
        in_specs=[vmem] * 11,
        out_specs=[vmem] * 6,
        out_shape=[
            jax.ShapeDtypeStruct((ROWS, D), BF16),
            jax.ShapeDtypeStruct((4, ROWS, RANK), BF16),
            jax.ShapeDtypeStruct((ROWS, 128), F32),
            jax.ShapeDtypeStruct((ROWS, 128), F32),
            jax.ShapeDtypeStruct((HEADS, 8, ROWS), F32),
            jax.ShapeDtypeStruct((ROWS + 8, 128), F32),
        ],
        scratch_shapes=[pltpu.VMEM((ROWS + 16, 128), F32)],
        compiler_params=params(),
        name="set_up",
        cost_estimate=cost(5),
    )(tokens, gain, low, rates_t, wide, live[:, None], live[None, :], ext[:, None], ids[None, :],
      jnp.pad(decay, (0, 128 - 16))[None, :], decay[:, None]), rates_t


TILE = 1024
FF_TILE = 1408


def rms_back(value, gain, grad):
    scale = lax.rsqrt(row_dot(value, value) * (1.0 / D) + 1e-06)
    dn = grad * gain
    return scale * dn - value * ((scale * scale * scale) * (row_dot(value, dn) * (1.0 / D)))


def project_kernel(first_ref, w_ref, inner_ref, up_ref, out_ref):
    out = nn(first_ref[...], w_ref[...]) + nn(inner_ref[0], up_ref[...])
    out_ref[...] = out.astype(out_ref.dtype)


def project(first, weights, inner, up, begin, width, dtype):
    tiles, per_block = width // PROJ, D // PROJ
    return pl.pallas_call(
        project_kernel,
        grid=(tiles,),
        in_specs=[
            pl.BlockSpec((ROWS, D), lambda t: (0, 0)),
            pl.BlockSpec((D, PROJ), lambda t: (0, t + begin // PROJ)),
            pl.BlockSpec((1, ROWS, RANK), lambda t: ((t + begin // PROJ) // per_block, 0, 0)),
            pl.BlockSpec((RANK, PROJ), lambda t: (0, t + begin // PROJ)),
        ],
        out_specs=pl.BlockSpec((ROWS, PROJ), lambda t: (0, t)),
        out_shape=jax.ShapeDtypeStruct((ROWS, width), dtype),
        compiler_params=params(),
        name="project",
        cost_estimate=cost(2 * width / D),
    )(first, weights, inner, up)


PROJ = 1024


def share(out_ref, lane, grads):
    for owner in range(8):
        out_ref[owner, :, lane : lane + 128] = grads[:, owner * 128 : (owner + 1) * 128]


def half_kernel(
    merged_ref, tokens_ref, grad_ref, gain_ref, wout_a, wout_b, out_low, out_up, ffn_low, proj_up,
    gate_w, up_w, down_w, up_a, up_b, proj_low,
    mixed_ref, dmid_ref, dmerged_ref, early_ref,
    middle_s, second_s, ffn_s, dproj_s, acc_out, acc_ds, acc_ip, acc_df,
):
    step = pl.program_id(0)
    g = grad_ref[...]

    @pl.when(step == 0)
    def _():
        merged = merged_ref[...]
        inner_out = nt(merged, out_low[...]).astype(BF16)
        branch = jnp.concatenate([nn(merged, wout_a[...]), nn(merged, wout_b[...])], axis=1)
        middle = tokens_ref[...].astype(F32) + (branch + nn(inner_out, out_up[...]))
        scale = lax.rsqrt(row_dot(middle, middle) * (1.0 / D) + 1e-06)
        second = (middle * scale * gain_ref[...]).astype(BF16)
        inner_ffn = nt(second, ffn_low[...]).astype(BF16)
        middle_s[...] = middle
        acc_out[...] = middle
        second_s[...] = second
        ffn_s[0] = inner_ffn[:, :RANK]
        ffn_s[1] = inner_ffn[:, RANK:]
        dproj_s[...] = nt(g, proj_up[...]).astype(BF16)
        early_ref[...] = jnp.zeros_like(early_ref)
        acc_ds[...] = jnp.zeros_like(acc_ds)
        acc_ip[...] = jnp.zeros_like(acc_ip)
        acc_df[...] = jnp.zeros_like(acc_df)

    second = second_s[...]
    a = nn(second, gate_w[...]) + nn(ffn_s[0], up_a[...])
    b = nn(second, up_w[...]) + nn(ffn_s[1], up_b[...])
    down = down_w[...]
    d_hidden = nt(g, down) + nn(dproj_s[...], proj_low[...])
    sig = sigmoid(a)
    act = a * sig
    hidden = (act * b).astype(BF16)
    da = (d_hidden * b * (sig * (1.0 + a * (1.0 - sig)))).astype(BF16)
    db = (d_hidden * act).astype(BF16)
    acc_out[...] += nn(hidden, down)
    acc_ds[...] += nt(da, gate_w[...]) + nt(db, up_w[...])
    acc_ip[...] += nt(hidden, proj_low[...])
    acc_df[0] += nt(da, up_a[...])
    acc_df[1] += nt(db, up_b[...])
    own, rows = FF // 4, FF // 8
    count = FF_TILE // own
    for part, grads in enumerate((tn(ffn_s[0], da), tn(ffn_s[1], db))):
        for n in range(count):
            early_ref[part * 4 + step * count + n, :, 512 : 512 + own] = grads[:, n * own : (n + 1) * own]
    grads = tn(dproj_s[...], hidden)
    for n in range(2 * count):
        early_ref[step * 2 * count + n, :, 1280 : 1280 + rows] = grads[:, n * rows : (n + 1) * rows]

    @pl.when(step == pl.num_programs(0) - 1)
    def _():
        merged, second, middle = merged_ref[...], second_s[...], middle_s[...]
        inner_proj = acc_ip[...].astype(BF16)
        mixed_ref[...] = (acc_out[...] + nn(inner_proj, proj_up[...])).astype(BF16)
        share(early_ref, 1664, tn(inner_proj, g))
        da, db = acc_df[0].astype(BF16), acc_df[1].astype(BF16)
        d_second = acc_ds[...] + (nn(da, ffn_low[:RANK, :]) + nn(db, ffn_low[RANK:, :]))
        share(early_ref, 256, tn(da, second))
        share(early_ref, 384, tn(db, second))
        d_middle = g.astype(F32) + rms_back(middle, gain_ref[...], d_second)
        dmid_ref[...] = d_middle
        d_branch = d_middle.astype(BF16)
        d_inner = nt(d_branch, out_up[...]).astype(BF16)
        half = D // 2
        d_branch_out = nt(d_branch[:, :half], wout_a[...]) + nt(d_branch[:, half:], wout_b[...])
        dmerged_ref[...] = d_branch_out + nn(d_inner, out_low[...])
        inner_out = nt(merged, out_low[...]).astype(BF16)
        share(early_ref, 0, tn(d_inner, merged))
        share(early_ref, 128, tn(inner_out, d_branch))


def second_half(merged, tokens, grad, gain, w_out, w_gu, w_down, out_low, out_up, ffn_low, ffn_up, proj_low, proj_up):
    steps = FF // FF_TILE
    wide = jax.ShapeDtypeStruct((ROWS, D), F32)
    tile = pl.BlockSpec((RANK, FF_TILE), lambda f: (0, f))
    row = whole((RANK, D))

    def out_half(n):
        return pl.BlockSpec((D, D // 2), lambda f: (0, n))

    return pl.pallas_call(
        half_kernel,
        grid=(steps,),
        in_specs=[whole((ROWS, D))] * 3
        + [whole((1, D)), out_half(0), out_half(1), row, row, whole((2 * RANK, D)), row]
        + [
            pl.BlockSpec((D, FF_TILE), lambda f: (0, f)),
            pl.BlockSpec((D, FF_TILE), lambda f: (0, f + steps)),
            pl.BlockSpec((FF_TILE, D), lambda f: (f, 0)),
            tile,
            pl.BlockSpec((RANK, FF_TILE), lambda f: (0, f + steps)),
            tile,
        ],
        out_specs=[whole((ROWS, D))] * 3 + [whole((8, RANK, 1792))],
        out_shape=[
            jax.ShapeDtypeStruct((ROWS, D), BF16), wide, wide,
            jax.ShapeDtypeStruct((8, RANK, 1792), F32),
        ],
        scratch_shapes=[
            pltpu.VMEM((ROWS, D), F32), pltpu.VMEM((ROWS, D), BF16),
            pltpu.VMEM((2, ROWS, RANK), BF16), pltpu.VMEM((ROWS, RANK), BF16),
            pltpu.VMEM((ROWS, D), F32), pltpu.VMEM((ROWS, D), F32),
            pltpu.VMEM((ROWS, RANK), F32), pltpu.VMEM((2, ROWS, RANK), F32),
        ],
        compiler_params=params(),
        name="second_half",
        cost_estimate=cost(23),
    )(merged, tokens, grad, gain, w_out, w_out, out_low, out_up, ffn_low, proj_up,
      w_gu, w_gu, w_down, ffn_up, ffn_up, proj_low)


def repaired(grown_ref, edge_ref, back_ref):
    end = edge_ref[0] + back_ref[0].astype(F32)
    return jnp.concatenate([grown_ref[0, : ROWS - 8, :].astype(F32), end], axis=0).astype(BF16)


def inner_kernel(
    grown_ref, edge_ref, back_ref, inner_ref, up_ref, gate_inner, first_ref,
    inner_out, g_up, g_low,
):
    block = pl.program_id(0)
    grown = repaired(grown_ref, edge_ref, back_ref)
    inner_out[block] = nt(grown, up_ref[...]).astype(BF16)
    up = tn(inner_ref[0], grown)
    g_up[0] = up[:, : D // 2]
    g_up[1] = up[:, D // 2 :]

    @pl.when(block == pl.num_programs(0) - 1)
    def _():
        inner_out[3] = gate_inner[...].astype(BF16)
        for j in range(4):
            low = tn(inner_out[j], first_ref[...])
            for owner in range(8):
                g_low[owner, :, j * 128 : (j + 1) * 128] = low[:, owner * 128 : (owner + 1) * 128]


def block_piece(rows):
    return pl.BlockSpec((1, rows, D), lambda t: (t, 0, 0))


def inner_part(grown, edge, back, inner, up, gate_inner, first):
    return pl.pallas_call(
        inner_kernel,
        grid=(3,),
        in_specs=[
            block_piece(ROWS), block_piece(8), block_piece(8),
            pl.BlockSpec((1, ROWS, RANK), lambda t: (t, 0, 0)),
            pl.BlockSpec((RANK, D), lambda t: (0, t)),
            whole((ROWS, RANK)), whole((ROWS, D)),
        ],
        out_specs=[
            whole((4, ROWS, RANK)),
            pl.BlockSpec((2, RANK, D // 2), lambda t: (t, 0, 0)),
            whole((8, RANK, D // 2)),
        ],
        out_shape=[
            jax.ShapeDtypeStruct((4, ROWS, RANK), BF16),
            jax.ShapeDtypeStruct((6, RANK, D // 2), F32),
            jax.ShapeDtypeStruct((8, RANK, D // 2), F32),
        ],
        compiler_params=params(),
        name="inner_part",
        cost_estimate=cost(4),
    )(grown, edge, back, inner, up, gate_inner, first)


def last_kernel(
    grown_ref, edge_ref, back_ref, w_ref, inner_ref, gate_ref, tokens_ref, gain_ref,
    low_ref, logits_ref, rates_ref, dmid_ref, out_ref, acc,
):
    step = pl.program_id(0)

    @pl.when(step == 0)
    def _():
        acc[...] = gate_ref[...]

    acc[...] += nt(repaired(grown_ref, edge_ref, back_ref), w_ref[...])

    @pl.when(step == pl.num_programs(0) - 1)
    def _():
        x = tokens_ref[...].astype(F32)
        total = acc[...] + nn(logits_ref[...], rates_ref[...])
        for j in range(4):
            total = total + nn(inner_ref[j], low_ref[j * RANK : (j + 1) * RANK, :])
        out_ref[...] = dmid_ref[...] + rms_back(x, gain_ref[...], total)


def last(grown, edge, back, w_in, inner, gate_part, tokens, gain, low, d_logits, rates, d_middle):
    return pl.pallas_call(
        last_kernel,
        grid=(3,),
        in_specs=[
            block_piece(ROWS), block_piece(8), block_piece(8),
            pl.BlockSpec((D, D), lambda t: (0, t)),
            whole((4, ROWS, RANK)),
            whole((ROWS, D)), whole((ROWS, D)), whole((1, D)),
            whole((4 * RANK, D)), whole((ROWS, 16)), whole((16, D)), whole((ROWS, D)),
        ],
        out_specs=whole((ROWS, D)),
        out_shape=jax.ShapeDtypeStruct((ROWS, D), F32),
        scratch_shapes=[pltpu.VMEM((ROWS, D), F32)],
        compiler_params=params(),
        name="last",
        cost_estimate=cost(9),
    )(grown, edge, back, w_in, inner, gate_part, tokens, gain, low, d_logits, rates, d_middle)


def gate_kernel(grown_ref, w_ref, inner_ref, up_ref, out_ref, inner_out, g_up):
    grown = grown_ref[...]
    out_ref[...] = nt(grown, w_ref[...])
    inner_out[...] = nt(grown, up_ref[...])
    up = tn(inner_ref[...], grown)
    g_up[0] = up[:, : D // 2]
    g_up[1] = up[:, D // 2 :]


def gate_part(grown, w_in, inner, up):
    return pl.pallas_call(
        gate_kernel,
        grid=(1,),
        in_specs=[
            whole((ROWS, D)),
            pl.BlockSpec((D, D), lambda t: (0, 3)),
            whole((ROWS, RANK)),
            pl.BlockSpec((RANK, D), lambda t: (0, 3)),
        ],
        out_specs=[whole((ROWS, D)), whole((ROWS, RANK)), whole((2, RANK, D // 2))],
        out_shape=[
            jax.ShapeDtypeStruct((ROWS, D), F32),
            jax.ShapeDtypeStruct((ROWS, RANK), F32),
            jax.ShapeDtypeStruct((2, RANK, D // 2), F32),
        ],
        compiler_params=params(),
        name="gate_part",
        cost_estimate=cost(3.5),
    )(grown, w_in, inner, up)


def spread_kernel(rows, own_ref, own_pair, rest_ref, rest_pair, down_ref, out_ref):
    rep, index = lax.axis_index("rep"), lax.axis_index("shard")
    z, x, y, core = rep // 4, lax.rem(rep, 4), index // 2, lax.rem(index, 2)
    down, out = rows

    def put(block, source, first_row, lanes_from, piece, width):
        at = pl.ds(pl.multiple_of(piece * 128, 128), width)
        lanes = slice(lanes_from, lanes_from + width)
        down_ref[pl.ds(pl.multiple_of(block * down, 16), down), at] = source[
            first_row : first_row + down, lanes
        ]
        out_ref[pl.ds(pl.multiple_of(block * out, 16), out), at] = source[
            first_row + down : first_row + down + out, lanes
        ]

    for own, rest, c in ((own_ref, rest_ref, core), (own_pair, rest_pair, 1 - core)):
        put(2 * y + c, own, 0, 0, 0, D)
        for n in (1, 2, 3):
            block = 2 * lax.rem(y + 4 - n, 4) + c
            for group in range(8):
                if group == 0:
                    piece = x
                elif group == 1:
                    piece = 4 + z
                elif group < 5:
                    piece = lax.rem(x + 4 - (group - 1), 4)
                else:
                    piece = 4 + lax.rem(z + 4 - (group - 4), 4)
                put(block, rest, (n - 1) * (down + out), group * 128, piece, 128)


def rows_over_y(proj_down, proj_out):
    own = jnp.concatenate([proj_down, proj_out], axis=0)
    rep = lax.axis_index("rep")
    z, x = rep // 4, lax.rem(rep, 4)
    pieces = jnp.concatenate(
        [
            lax.dynamic_slice_in_dim(own, x * 128, 128, 1),
            lax.dynamic_slice_in_dim(own, (4 + z) * 128, 128, 1),
        ],
        axis=1,
    )
    return own, [lax.ppermute(pieces, "shard", along("shard", 2 * n)) for n in (1, 2, 3)]


def rows_over_planes(came):
    by_x = jnp.concatenate([c[:, :128] for c in came], axis=0)
    by_z = jnp.concatenate([c[:, 128:] for c in came], axis=0)
    rest = [lax.ppermute(by_x, "rep", rep_pairs(0, n)) for n in (1, 2, 3)]
    rest += [lax.ppermute(by_z, "rep", rep_pairs(n, 0)) for n in (1, 2, 3)]
    return [by_x, by_z] + rest


def gathered_rows(own, own_pair, rest, rest_pair, rows):
    return pl.pallas_call(
        functools.partial(spread_kernel, rows),
        in_specs=[pl.BlockSpec(memory_space=pltpu.VMEM)] * 4,
        out_specs=[pl.BlockSpec(memory_space=pltpu.VMEM)] * 2,
        out_shape=[jax.ShapeDtypeStruct((8 * n, D), BF16) for n in rows],
        compiler_params=params(),
        name="gathered_rows",
        cost_estimate=cost(6),
    )(own, own_pair, rest, rest_pair)


def along(axis, offset):
    count = lax.axis_size(axis)
    return [(i, (i + offset) % count) for i in range(count)]


def rep_pairs(dz, dx):
    return [(z * 4 + x, (z + dz) % 4 * 4 + (x + dx) % 4) for z in range(4) for x in range(4)]


def placed(gathered, sizes):
    n = gathered[0].shape[2] - 128

    def body(*refs):
        sources, outs, total = refs[: len(gathered)], refs[len(gathered) : -1], refs[-1]
        total[...] = jnp.zeros_like(total)
        for ref in sources:
            for s in range(ref.shape[0]):
                number = ref[s, :, n:].astype(F32)[:, :1]
                part = ref[s, :, :n].astype(F32)
                for a in range(8):
                    total[a] += jnp.where(number == a, part, 0.0)
        everything = total[...].reshape(8 * RANK, n)
        begin = 0
        for out, (rows, blocks) in zip(outs, sizes):
            padded = -(-rows // 128) * 128
            for m in range(blocks):
                out[:, m * 128 : (m + 1) * 128] = everything[:, begin : begin + padded].T[:rows]
                begin += padded

    return pl.pallas_call(
        body,
        in_specs=[pl.BlockSpec(memory_space=pltpu.VMEM)] * len(gathered),
        out_specs=[pl.BlockSpec(memory_space=pltpu.VMEM)] * len(sizes),
        out_shape=[jax.ShapeDtypeStruct((rows, blocks * 128), F32) for rows, blocks in sizes],
        scratch_shapes=[pltpu.VMEM((8, RANK, n), F32)],
        compiler_params=params(),
        name="placed",
        cost_estimate=cost(3),
    )(*gathered)


def numbered(sums, adapter):
    number = jnp.full((RANK, 128), adapter, F32).astype(sums.dtype)
    return jnp.concatenate([sums, number], axis=1)


def reduced_calls(own, adapter, sizes):
    return placed([lax.all_gather(numbered(own, adapter), "rep")], sizes)


def reduced(stacked, adapter, sizes):
    index = lax.axis_index("shard")
    y, core = index // 2, lax.rem(index, 2)
    n = stacked.shape[2]
    by_core = stacked.astype(BF16).reshape(4, 2, RANK, n)
    came = swap(lax.dynamic_index_in_dim(by_core, 1 - core, 1, False))
    chip = lax.dynamic_index_in_dim(by_core, core, 1, False).astype(F32) + came.astype(F32)
    total = lax.dynamic_index_in_dim(chip, y, 0, False)
    low = chip.astype(BF16)
    for step in (1, 2, 3):
        part = lax.dynamic_index_in_dim(low, lax.rem(y + step, 4), 0, False)
        total = total + lax.ppermute(part, "shard", along("shard", 2 * step)).astype(F32)
    own = numbered(total.astype(BF16), adapter)
    row = jnp.stack([own] + [lax.ppermute(own, "rep", rep_pairs(0, k)) for k in (1, 2, 3)])
    planes = [row] + [lax.ppermute(row, "rep", rep_pairs(k, 0)) for k in (1, 2, 3)]
    return placed(planes, sizes)


def owners(part):
    split = part.reshape(RANK, 8, -1).transpose(1, 0, 2)
    return jnp.pad(split, ((0, 0), (0, 0), (0, -split.shape[2] % 128)))


def per_device(
    tokens, segment_ids, pad_mask, adapter_id, out_grad, gain_first, proj_in, proj_rates,
    conv_taps, decay_rate, ridge, gain_heads, proj_out, gain_second, proj_gu, proj_down,
    in_lower, in_upper, out_lower, out_upper, ffn_lower, ffn_upper, proj_lower, proj_upper,
):
    tail = CONV - 1
    adapter = adapter_id[0]
    w_in = lax.all_gather(proj_in, "shard", axis=0, tiled=True)
    own_rows, rows_came = rows_over_y(proj_down, proj_out)
    own_pair = swap(own_rows)
    in_low, in_up, out_low, out_up, ffn_low, ffn_up, proj_low, proj_up = choose(
        adapter_id, (in_lower, in_upper, out_lower, out_upper, ffn_lower, ffn_upper, proj_lower, proj_upper)
    )
    tail_ids = lax.ppermute(segment_ids[ROWS - tail :], "shard", [(i, i + 1) for i in range(7)])

    rows_came, in_low, tokens_here = lax.optimization_barrier((rows_came, in_low, tokens))
    rest_rows = rows_over_planes(rows_came)
    live = pad_mask.astype(F32)
    (first, inner_in, logits, cols, rows, shift), rates_t = set_up(
        tokens_here, gain_first[None], in_low, proj_rates, live, segment_ids, tail_ids, decay_rate
    )

    own_gu, own_pair, rest_rows, first, cols, rows = lax.optimization_barrier(
        (proj_gu, own_pair, rest_rows, first, cols, rows)
    )
    w_gu = lax.all_gather(own_gu, "shard", axis=0, tiled=True)

    def handed_on(conv):
        return lax.ppermute(conv[ROWS - 16 :], "shard", [(i, i + 1) for i in range(7)])

    conv_kv = project(first, w_in, inner_in, in_up, D, 2 * D, BF16)
    tail_kv = handed_on(conv_kv)
    k, v, m_first, w_first, load = front(conv_kv, tail_kv, conv_taps, cols, rows)
    rest_rows = jnp.concatenate(rest_rows, axis=1)
    rest_pair = swap(rest_rows)
    conv_q = project(first, w_in, inner_in, in_up, 0, D, BF16)
    gate_in = project(first, w_in, inner_in, in_up, 3 * D, D, F32)
    tail_q = handed_on(conv_q)

    def first_work(tail_q, *pieces):
        return front_query(conv_q, tail_q, conv_taps, cols), *gathered_rows(*pieces, (FF // 8, D // 8))

    (m0, w0), (q, w_down, w_out) = exchanged(
        load, True, (tail_q, own_rows, own_pair, rest_rows, rest_pair), first_work
    )
    gain = gain_heads[None]
    merged, r, y, p, i = read(ridge, q, k, v, gate_in, gain, cols, rows, m0, w0, m_first, w_first)

    mixed, d_middle, d_merged, early = second_half(
        merged, tokens, out_grad, gain_second[None], w_out, w_gu, w_down,
        out_low, out_up, ffn_low, ffn_up, proj_low, proj_up,
    )
    d_gate, dq, dk, dv, dcol, drow, load, dm1, dw1 = read_back(
        ridge, q, k, v, gate_in, gain, cols, rows, m0, w0, m_first, w_first, r, y, p, i, d_merged
    )
    early = lax.psum_scatter(early, "shard", scatter_dimension=0, tiled=False)
    load, early = lax.optimization_barrier((load, early))
    early = reduced_calls(
        early, adapter, [(128, 1), (128, 1), (128, 2), (704, 1), (352, 1), (128, 1)]
    )
    (dm2, dw2), (gate_grad, gate_inner, g_up_gate) = exchanged(
        load, False, (d_gate,), lambda d_gate: gate_part(d_gate, w_in, inner_in[3], in_up)
    )
    grown, edge, top, dcol = front_back(
        conv_q, conv_kv, tail_q, tail_kv, conv_taps, cols, rows, shift, k, v, dq, dk, dv, dcol,
        m0, w0, m_first, w_first, dm1, dw1, dm2, dw2,
    )
    back = lax.ppermute(top, "shard", [(i + 1, i) for i in range(7)])
    d_logits = scalar_back(logits, live, decay_rate, dcol, drow).astype(BF16)
    inner_grads, g_up, g_low = inner_part(grown, edge, back, inner_in, in_up, gate_inner, first)
    late = jnp.concatenate([g_low, jnp.concatenate([g_up, g_up_gate], axis=0)], axis=2)
    token_grad = last(
        grown, edge, back, w_in, inner_grads, gate_grad, tokens, gain_first[None],
        in_low, d_logits, rates_t, d_middle,
    )
    late = reduced(late, adapter, [(128, 4), (512, 1)])
    return (mixed, token_grad, late[0], late[1], *early)


def solution(mesh):
    whole_spec, by_shard, by_token = P(), P("shard", None), P(("rep", "shard"), None)
    by_row = P(("rep", "shard"))
    return jax.shard_map(
        per_device,
        mesh=mesh,
        in_specs=(
            by_token, by_row, by_row, P("rep"), by_token, whole_spec, by_shard, whole_spec,
            whole_spec, whole_spec, whole_spec, whole_spec, by_shard, whole_spec, by_shard, by_shard,
        )
        + (whole_spec,) * 8,
        out_specs=(by_token, by_token) + (by_shard,) * 8,
        check_vma=False,
    )
```

```python
import functools

import jax
import jax.numpy as jnp
from jax import lax
from jax.experimental import pallas as pl
from jax.experimental.pallas import tpu as pltpu
from jax.sharding import PartitionSpec as P

F32 = jnp.float32
BF16 = jnp.bfloat16
ROWS = 256
CHUNK = 128
HEADS = 8
HEAD = 128
D = 1024
FF = 2816
RANK = 16
CONV = 4
ITERS = 8
VMEM = 60 * 1024 * 1024
TOGETHER = 2
TAIL = 16
TOT, KEPT, SAME, IDS = 8, 16, 17, 20


def nt(a, b):
    return lax.dot_general(a, b, (((1,), (1,)), ((), ())), preferred_element_type=F32)


def nn(a, b):
    return lax.dot_general(a, b, (((1,), (0,)), ((), ())), preferred_element_type=F32)


def tn(a, b):
    return lax.dot_general(a, b, (((0,), (0,)), ((), ())), preferred_element_type=F32)


def halves(x):
    high = x.astype(BF16)
    return high, (x - high.astype(F32)).astype(BF16)


def left3(x, axis=1):
    high, rest = halves(x)
    return jnp.concatenate([high, rest, high], axis=axis)


def right3(x, axis):
    high, rest = halves(x)
    return jnp.concatenate([high, high, rest], axis=axis)


def row_dot(a, b):
    return jnp.sum(a * b, axis=1, keepdims=True)


def column(packed, index):
    lane = lax.broadcasted_iota(jnp.int32, packed.shape, 1)
    return jnp.sum(jnp.where(lane == index, packed, 0.0), axis=1, keepdims=True)


def sigmoid(x):
    return 1.0 / (1.0 + jnp.exp(-x))


def chunk_scalars(cols, row_ref, head, chunk, slot=0):
    begin = chunk * CHUNK
    part = cols[begin : begin + CHUNK]
    total = column(part, TOT + head)
    kept = column(part, KEPT)
    ids = column(part, IDS)
    span = slice(begin, begin + CHUNK)
    return {
        "beta": column(part, head),
        "total": total,
        "kept": kept,
        "ids": ids,
        "opening": jnp.exp(total) * kept,
        "beta_row": row_ref[slot, 0:1, span],
        "total_row": row_ref[slot, 1:2, span],
        "ids_row": row_ref[slot, 2:3, span],
    }


def weights_of(s):
    t = lax.broadcasted_iota(jnp.int32, (CHUNK, CHUNK), 0)
    u = lax.broadcasted_iota(jnp.int32, (CHUNK, CHUNK), 1)
    allowed = (t >= u) & (s["ids"] == s["ids_row"])
    return jnp.where(allowed, jnp.exp(jnp.where(allowed, s["total"] - s["total_row"], 0.0)), 0.0)


def weights_t_of(s):
    u = lax.broadcasted_iota(jnp.int32, (CHUNK, CHUNK), 0)
    t = lax.broadcasted_iota(jnp.int32, (CHUNK, CHUNK), 1)
    allowed = (t >= u) & (s["ids"] == s["ids_row"])
    return jnp.where(allowed, jnp.exp(jnp.where(allowed, s["total_row"] - s["total"], 0.0)), 0.0)


def last_weight(s):
    end = CHUNK - 1
    same = s["ids"] == s["ids"][end:]
    return jnp.where(same, jnp.exp(jnp.where(same, s["total"][end:] - s["total"], 0.0)), 0.0)


LOAD = 272


def places():
    return (
        lax.broadcasted_iota(jnp.int32, (HEAD, HEAD), 0),
        lax.broadcasted_iota(jnp.int32, (HEAD, HEAD), 1),
    )


def extra_rows(opening, diagonal):
    row = lax.broadcasted_iota(jnp.int32, (16, HEAD), 0)
    high, rest = halves(opening)
    out = jnp.where(row == 1, high.astype(F32), jnp.where(row == 2, rest.astype(F32), 0.0))
    return jnp.where(row == 0, diagonal, out).astype(BF16)


def pack_state(opening, memory, lookup):
    r, c = places()
    high, rest = halves(memory)
    high, rest = high.astype(F32), rest.astype(F32)
    diagonal = jnp.sum(jnp.where(r == c, rest, 0.0), axis=0, keepdims=True)
    mixed = jnp.where(r >= c, high, rest).astype(BF16)
    return jnp.concatenate([mixed, lookup.astype(BF16), extra_rows(opening, diagonal)], axis=0)


def unpack_state(load):
    r, c = places()
    x = load.astype(F32)
    mixed, extra = x[:HEAD], x[2 * HEAD :]
    turned = mixed.T
    high = jnp.where(r >= c, mixed, turned)
    rest = jnp.where(r < c, mixed, jnp.where(r > c, turned, extra[0:1]))
    return extra[1:2, 0:1] + extra[2:3, 0:1], high + rest, x[HEAD : 2 * HEAD]


def pack_plain(opening, memory, lookup):
    zero = jnp.zeros((1, HEAD), F32)
    return jnp.concatenate(
        [memory.astype(BF16), lookup.astype(BF16), extra_rows(opening, zero)], axis=0
    )


def unpack_plain(load):
    x = load.astype(F32)
    extra = x[2 * HEAD :]
    return extra[1:2, 0:1] + extra[2:3, 0:1], x[:HEAD], x[HEAD : 2 * HEAD]


def then(earlier, later):
    return tuple([earlier[0] * later[0]] + [later[0] * a + b for a, b in zip(earlier[1:], later[1:])])


def back_then(earlier, later):
    return tuple([earlier[0] * later[0]] + [a + earlier[0] * b for a, b in zip(earlier[1:], later[1:])])


def pair_kernel(forward, core_ref, mine_ref, came_ref, out_ref):
    pack, unpack = (pack_state, unpack_state) if forward else (pack_plain, unpack_plain)
    core = core_ref[0]
    for n in range(HEADS // 2):
        mine = jnp.where(core == 0, mine_ref[n], mine_ref[n + HEADS // 2])
        came = came_ref[n]
        first = unpack(jnp.where(core == 0, mine, came))
        second = unpack(jnp.where(core == 0, came, mine))
        out_ref[n] = pack(*(then if forward else back_then)(first, second))


def entry_kernel(forward, core_ref, mine_ref, came_ref, near_ref, middle_ref, far_ref, m_ref, w_ref, out_ref):
    pack, unpack = (pack_state, unpack_state) if forward else (pack_plain, unpack_plain)
    core = core_ref[0]
    for n in range(HEADS // 2):
        mine = jnp.where(core == 0, mine_ref[n], mine_ref[n + HEADS // 2])
        near, middle, far = unpack(near_ref[n]), unpack(middle_ref[n]), unpack(far_ref[n])
        own_first = core == 0
        if forward:
            outer = then(then(far, middle), near)
            inner = then(outer, unpack(jnp.where(own_first, mine, came_ref[n])))
            own = [jnp.where(own_first, a, b) for a, b in zip(outer, inner)]
            other = [jnp.where(own_first, b, a) for a, b in zip(outer, inner)]
        else:
            outer = back_then(near, back_then(middle, far))
            inner = back_then(unpack(jnp.where(own_first, came_ref[n], mine)), outer)
            own = [jnp.where(own_first, b, a) for a, b in zip(outer, inner)]
            other = [jnp.where(own_first, a, b) for a, b in zip(outer, inner)]
        m_ref[n] = own[1]
        w_ref[n] = own[2]
        out_ref[n] = pack(*other)


def join_kernel(forward, core_ref, own_m, own_w, came_ref, m_ref, w_ref):
    unpack = unpack_state if forward else unpack_plain
    core = core_ref[0]
    for n in range(HEADS // 2):
        _, memory, lookup = unpack(came_ref[n])
        for out, own, came in ((m_ref, own_m[n], memory), (w_ref, own_w[n], lookup)):
            out[n] = jnp.where(core == 0, own, came)
            out[n + HEADS // 2] = jnp.where(core == 0, came, own)


def small_call(kernel, forward, outs, *operands):
    return pl.pallas_call(
        functools.partial(kernel, forward),
        in_specs=[pl.BlockSpec(memory_space=pltpu.SMEM)]
        + [pl.BlockSpec(memory_space=pltpu.VMEM)] * (len(operands) - 1),
        out_specs=[pl.BlockSpec(memory_space=pltpu.VMEM)] * len(outs),
        out_shape=outs,
        compiler_params=params(),
        cost_estimate=cost(2),
    )(*operands)


def swap(value):
    count = lax.axis_size("shard")
    return lax.ppermute(value, "shard", [(i, i ^ 1) for i in range(count)])


def over_chips(value, steps):
    count = lax.axis_size("shard")
    pairs = [(i, i + 2 * steps) for i in range(count) if 0 <= i + 2 * steps < count]
    return lax.ppermute(value, "shard", pairs)


def exchanged(load, forward, inputs, work):
    half = HEADS // 2
    core = lax.rem(lax.axis_index("shard"), 2)
    scalar = core.reshape(1)
    packed = jax.ShapeDtypeStruct((half, LOAD, HEAD), BF16)
    states = jax.ShapeDtypeStruct((half, HEAD, HEAD), F32)
    full = jax.ShapeDtypeStruct((HEADS, HEAD, HEAD), F32)
    came = swap(lax.dynamic_slice_in_dim(load, (1 - core) * half, half, 0))
    (chip,) = small_call(pair_kernel, forward, [packed], scalar, load, came)
    chip, inputs = lax.optimization_barrier((chip, inputs))
    others = [over_chips(chip, n if forward else -n) for n in (1, 2, 3)]
    beside = work(*inputs)
    others, beside = lax.optimization_barrier((others, beside))
    own_m, own_w, out = small_call(
        entry_kernel, forward, [states, states, packed], scalar, load, came, *others
    )
    return small_call(join_kernel, forward, [full, full], scalar, own_m, own_w, swap(out)), beside


def conv_rows(x_ref, taps_ref, ext_ref, spot, cols, lanes):
    ext = ext_ref.at[spot]
    ext[...] = x_ref[:, lanes].astype(F32)[TAIL - 8 :]
    total = taps_ref[0:1, lanes] * ext[8 : 8 + ROWS, :]
    for j in range(1, CONV):
        same = cols[:, SAME + j - 1 : SAME + j]
        total = total + (taps_ref[j : j + 1, lanes] * ext[8 - j : 8 - j + ROWS, :]) * same
    return total


def front_kernel(
    k_in, v_in, k_taps, v_taps, cols_ref, row_ref,
    k_out, v_out, m_first, w_first, load_ref, ext,
):
    cols = cols_ref[...]
    for slot in range(TOGETHER):
        head = pl.program_id(0) * TOGETHER + slot
        lanes = slice(slot * HEAD, (slot + 1) * HEAD)
        acts = []
        for n, (x_ref, taps_ref) in enumerate(((k_in, k_taps), (v_in, v_taps))):
            c = conv_rows(x_ref, taps_ref, ext, 2 * slot + n, cols, lanes)
            acts.append(c * sigmoid(c))
        k, v = acts
        k = k * lax.rsqrt(row_dot(k, k) + 1e-06)
        k_out[:, lanes] = k
        v_out[:, lanes] = v
        parts = []
        for chunk in range(2):
            begin = chunk * CHUNK
            s = chunk_scalars(cols, row_ref, head, chunk, slot)
            kc, vc = k[begin : begin + CHUNK], v[begin : begin + CHUNK]
            last = last_weight(s) * s["beta"]
            right = right3(kc, 0)
            parts.append((
                tn(left3(kc * last, 0), right), tn(left3(vc * last, 0), right), s["opening"][CHUNK - 1 :]
            ))
        m_first[slot] = parts[0][0]
        w_first[slot] = parts[0][1]
        o2 = parts[1][2]
        load_ref[slot] = pack_state(
            parts[0][2] * o2, o2 * parts[0][0] + parts[1][0], o2 * parts[0][1] + parts[1][1]
        )


def query_kernel(q_in, q_taps, cols_ref, q_out, ext):
    for slot in range(TOGETHER):
        lanes = slice(slot * HEAD, (slot + 1) * HEAD)
        c = conv_rows(q_in, q_taps, ext, slot, cols_ref[...], lanes)
        q = c * sigmoid(c)
        q_out[:, lanes] = q * lax.rsqrt(row_dot(q, q) + 1e-06)


def head_block(rows, offset=0, heads=1):
    return pl.BlockSpec((rows, heads * HEAD), lambda h: (0, h + offset))


def whole(shape):
    return pl.BlockSpec(shape, lambda h: (0,) * len(shape))


def head_rows(count, heads=1):
    return pl.BlockSpec((heads, count, ROWS), lambda h: (h, 0, 0))


def square(heads=1):
    return pl.BlockSpec((heads, HEAD, HEAD), lambda h: (h, 0, 0))


def loads(heads=1):
    return pl.BlockSpec((heads, LOAD, HEAD), lambda h: (h, 0, 0))


def params():
    return pltpu.CompilerParams(vmem_limit_bytes=VMEM)


def cost(micros):
    return pl.CostEstimate(
        flops=int(micros * 1.15e9), bytes_accessed=int(micros * 3.0e6), transcendentals=0
    )


def front(conv_kv, taps, cols, rows):
    flat = jax.ShapeDtypeStruct((ROWS, D), F32)
    states = jax.ShapeDtypeStruct((HEADS, HEAD, HEAD), F32)
    per = HEADS // TOGETHER
    return pl.pallas_call(
        front_kernel,
        grid=(per,),
        in_specs=[head_block(TAIL + ROWS, o, TOGETHER) for o in (0, per)]
        + [head_block(CONV, o, TOGETHER) for o in (per, 2 * per)]
        + [whole((ROWS, 128)), head_rows(8, TOGETHER)],
        out_specs=[head_block(ROWS, 0, TOGETHER)] * 2 + [square(TOGETHER)] * 2 + [loads(TOGETHER)],
        out_shape=[flat] * 2 + [states] * 2 + [jax.ShapeDtypeStruct((HEADS, LOAD, HEAD), BF16)],
        scratch_shapes=[pltpu.VMEM((2 * TOGETHER, ROWS + 8, HEAD), F32)],
        compiler_params=params(),
        name="front",
        cost_estimate=cost(6.4),
    )(conv_kv, conv_kv, taps, taps, cols, rows)


def front_query(conv_q, taps, cols):
    return pl.pallas_call(
        query_kernel,
        grid=(HEADS // TOGETHER,),
        in_specs=[head_block(n, 0, TOGETHER) for n in (TAIL + ROWS, CONV)] + [whole((ROWS, 128))],
        out_specs=head_block(ROWS, 0, TOGETHER),
        out_shape=jax.ShapeDtypeStruct((ROWS, D), F32),
        scratch_shapes=[pltpu.VMEM((TOGETHER, ROWS + 8, HEAD), F32)],
        compiler_params=params(),
        name="front_query",
        cost_estimate=cost(4.5),
    )(conv_q, taps, cols)


def read_kernel(
    ridge_ref, q_ref, k_ref, v_ref, gate_ref, gain_ref, cols_ref, row_ref,
    m0_ref, w0_ref, m_first, w_first, merged_ref, r_ref, y_ref, p_ref, i_ref,
):
    cols = cols_ref[...]
    chains = []
    for slot in range(TOGETHER):
        head = pl.program_id(0) * TOGETHER + slot
        lanes = slice(slot * HEAD, (slot + 1) * HEAD)
        memory, lookup = m0_ref[slot], w0_ref[slot]
        for chunk in range(2):
            begin = chunk * CHUNK
            at = slice(begin, begin + CHUNK)
            s = chunk_scalars(cols, row_ref, head, chunk, slot)
            if chunk == 1:
                o1 = chains[-1]["o"][CHUNK - 1 :]
                memory = o1 * memory + m_first[slot]
                lookup = o1 * lookup + w_first[slot]
            kc = k_ref[at, lanes]
            q = q_ref[at, lanes]
            chains.append({
                "at": (at, lanes),
                "lanes": lanes,
                "ridge": ridge_ref[head],
                "g": weights_of(s) * s["beta_row"],
                "o": s["opening"],
                "score": jnp.concatenate([right3(kc, 1), right3(memory, 1)], axis=0),
                "score_w": jnp.concatenate([right3(kc, 1), right3(lookup, 1)], axis=0),
                "keys": right3(kc, 0),
                "y": jnp.zeros_like(q),
                "r": q,
                "p": q,
                "rr": row_dot(q, q),
            })
    for j in range(ITERS):
        boths = [nt(left3(c["p"]), c["score"]) for c in chains]
        mixings = [left3(c["g"] * both[:, :CHUNK]) for c, both in zip(chains, boths)]
        recents = [nn(mixing, c["keys"]) for c, mixing in zip(chains, mixings)]
        for c, both, recent in zip(chains, boths, recents):
            p = c["p"]
            image = recent + c["o"] * both[:, CHUNK:] + c["ridge"] * p
            p_ref[(j,) + c["at"]] = p
            i_ref[(j,) + c["at"]] = image
            alpha = c["rr"] / (row_dot(p, image) + 0.01)
            c["y"] = c["y"] + alpha * p
            if j < ITERS - 1:
                c["r"] = c["r"] - alpha * image
                following = row_dot(c["r"], c["r"])
                c["p"] = c["r"] + (following / (c["rr"] + 0.01)) * p
                c["rr"] = following
    for c in chains:
        both = nt(left3(c["y"]), c["score_w"])
        mixing = c["g"] * both[:, :CHUNK]
        out = nn(left3(mixing), right3(v_ref[c["at"]], 0)) + c["o"] * both[:, CHUNK:]
        y_ref[c["at"]] = c["y"]
        r_ref[c["at"]] = out
        gain = gain_ref[:, c["lanes"]]
        normed = out * lax.rsqrt(row_dot(out, out) * (1.0 / HEAD) + 1e-06) * gain
        gate = gate_ref[c["at"]]
        merged_ref[c["at"]] = (normed * (gate * sigmoid(gate))).astype(BF16)


def read(ridge, q, k, v, gate, gain, cols, rows, m0, w0, m_first, w_first):
    flat = jax.ShapeDtypeStruct((ROWS, D), F32)
    steps = jax.ShapeDtypeStruct((ITERS, ROWS, D), F32)
    step_block = pl.BlockSpec((ITERS, ROWS, TOGETHER * HEAD), lambda h: (0, 0, h))
    return pl.pallas_call(
        read_kernel,
        grid=(HEADS // TOGETHER,),
        in_specs=[pl.BlockSpec(memory_space=pltpu.SMEM)]
        + [head_block(ROWS, 0, TOGETHER)] * 4
        + [head_block(1, 0, TOGETHER), whole((ROWS, 128)), head_rows(8, TOGETHER)]
        + [square(TOGETHER)] * 4,
        out_specs=[head_block(ROWS, 0, TOGETHER)] * 3 + [step_block] * 2,
        out_shape=[jax.ShapeDtypeStruct((ROWS, D), BF16), flat, flat, steps, steps],
        compiler_params=params(),
        name="readout",
        cost_estimate=cost(26),
    )(ridge, q, k, v, gate, gain, cols, rows, m0, w0, m_first, w_first)


def read_back_kernel(
    ridge_ref, q_ref, k_ref, v_ref, gate_ref, gain_ref, cols_ref, row_ref,
    m0_ref, w0_ref, m_first, w_first, r_ref, y_ref, p_ref, i_ref, dm_ref,
    dgate_ref, dq_ref, dk_ref, dv_ref, dcol_ref, drow_ref, load_ref, dm1_ref, dw1_ref,
    stack_a, stack_b,
):
    cols = cols_ref[...]
    chains = []
    for slot in range(TOGETHER):
        head = pl.program_id(0) * TOGETHER + slot
        lanes = slice(slot * HEAD, (slot + 1) * HEAD)
        memory, lookup = m0_ref[slot], w0_ref[slot]
        for chunk in range(2):
            begin = chunk * CHUNK
            at = (slice(begin, begin + CHUNK), lanes)
            s = chunk_scalars(cols, row_ref, head, chunk, slot)
            if chunk == 1:
                o1 = chains[-1]["o"][CHUNK - 1 :]
                memory = o1 * memory + m_first[slot]
                lookup = o1 * lookup + w_first[slot]
            kc, vc, q, y = k_ref[at], v_ref[at], q_ref[at], y_ref[at]
            o = s["opening"]
            weights_t = weights_t_of(s)
            g = weights_of(s) * s["beta_row"]
            g_t = weights_t * s["beta"]
            out, gate, dm, gain = r_ref[at], gate_ref[at], dm_ref[at], gain_ref[:, lanes]
            scale = lax.rsqrt(row_dot(out, out) * (1.0 / HEAD) + 1e-06)
            sig = sigmoid(gate)
            dgate_ref[at] = (
                dm * (out * scale * gain) * (sig * (1.0 + gate * (1.0 - sig)))
            ).astype(BF16)
            dn = dm * (gate * sig) * gain
            dout = scale * dn - out * ((scale * scale * scale) * (row_dot(out, dn) * (1.0 / HEAD)))
            k_high, y_high, d_high, v_high = (a.astype(BF16) for a in (kc, y, dout, vc))
            dmix_dy = nn(left3(dout), right3(lookup, 0))
            dmix = nt(left3(dout), right3(vc, 1))
            keys = right3(kc, 0)
            score = jnp.concatenate([right3(kc, 1), right3(memory, 1)], axis=0)
            dy = nn(left3(g * dmix), keys) + o * dmix_dy
            s_t = nt(k_high, y_high)
            dmix_t = nt(v_high, d_high)
            dv_ref[at] = nn((g_t * s_t).astype(BF16), d_high)
            chains.append({
                "at": at, "g": g, "g_t": g_t, "w_t": weights_t, "o": o, "score": score, "keys": keys,
                "k_high": k_high, "dy": dy, "dk": nn((g_t * dmix_t).astype(BF16), y_high),
                "dg_t": dmix_t * s_t, "do": row_dot(y, dmix_dy),
                "dlookup": tn((o * dout).astype(BF16), y_high),
                "rs": [q], "rrs": [row_dot(q, q)], "alphas": [], "dens": [], "q": q,
                "number": slot * 2 + chunk, "head": head, "slot": slot, "ridge": ridge_ref[head],
                "r_bar": None, "p_bar": None, "rr_bar": None,
            })
    for j in range(ITERS):
        for c in chains:
            image = i_ref[(j,) + c["at"]]
            den = row_dot(p_ref[(j,) + c["at"]], image) + 0.01
            alpha = c["rrs"][j] / den
            c["alphas"].append(alpha)
            c["dens"].append(den)
            if j < ITERS - 1:
                r = c["rs"][j] - alpha * image
                c["rs"].append(r)
                c["rrs"].append(row_dot(r, r))
    for j in range(ITERS - 1, -1, -1):
        for c in chains:
            p, image = p_ref[(j,) + c["at"]], i_ref[(j,) + c["at"]]
            alpha, den, rr = c["alphas"][j], c["dens"][j], c["rrs"][j]
            dy = c["dy"]
            if j == ITERS - 1:
                alpha_bar = row_dot(dy, p)
                p_bar = alpha * dy
                rr_bar = alpha_bar / den
                den_bar = -alpha_bar * alpha / den
                i_bar = den_bar * p
                r_bar = None
            else:
                below = 1.0 / (rr + 0.01)
                b = c["rrs"][j + 1] * below
                b_bar = row_dot(c["p_bar"], p)
                r_bar = c["p_bar"] if c["r_bar"] is None else c["r_bar"] + c["p_bar"]
                rr_next = c["rr_bar"] + b_bar * below
                r_bar = r_bar + (2.0 * rr_next) * c["rs"][j + 1]
                alpha_bar = row_dot(dy, p) - row_dot(r_bar, image)
                p_bar = b * c["p_bar"] + alpha * dy
                rr_bar = alpha_bar / den - b_bar * b * below
                den_bar = -alpha_bar * alpha / den
                i_bar = den_bar * p - alpha * r_bar
            c["r_bar"], c["p_bar"], c["rr_bar"] = r_bar, p_bar + den_bar * image, rr_bar
            c["i_bar"], c["left"] = i_bar, left3(i_bar)
        boths = [nt(c["left"], c["score"]) for c in chains]
        mixes = [left3(c["g"] * both[:, :CHUNK]) for c, both in zip(chains, boths)]
        moves = [nn(mix, c["keys"]) for c, mix in zip(chains, mixes)]
        for c, both, moved in zip(chains, boths, moves):
            im = both[:, CHUNK:]
            p = p_ref[(j,) + c["at"]]
            c["p_bar"] = c["p_bar"] + moved + c["o"] * im + c["ridge"] * c["i_bar"]
            c["do"] = c["do"] + row_dot(p, im)
            i_high, p_high = c["left"][:, :CHUNK], p.astype(BF16)
            turned = nt(c["k_high"], jnp.concatenate([p_high, i_high], axis=0))
            s_t, d_t = turned[:, :CHUNK], turned[:, CHUNK:]
            c["dg_t"] = c["dg_t"] + s_t * d_t
            c["dk"] = c["dk"] + nn(
                jnp.concatenate([c["g_t"] * s_t, c["g_t"] * d_t], axis=1).astype(BF16),
                jnp.concatenate([i_high, p_high], axis=0),
            )
            rows = slice(j * CHUNK, (j + 1) * CHUNK)
            stack_a[c["number"], rows, :] = (c["o"] * c["i_bar"]).astype(BF16)
            stack_b[c["number"], rows, :] = p_high
    lane = lax.broadcasted_iota(jnp.int32, (CHUNK, 128), 1)
    for c in chains:
        at = c["at"]
        dq_ref[at] = c["r_bar"] + c["p_bar"] + (2.0 * c["rr_bar"]) * c["q"]
        dk_ref[at] = c["dk"]
        c["dmem"] = tn(stack_a[c["number"]], stack_b[c["number"]])
        scaled = c["dg_t"] * c["w_t"]
        z_t = c["dg_t"] * c["g_t"]
        dbeta = jnp.sum(scaled, axis=1, keepdims=True)
        dtotal = c["do"] * c["o"] - jnp.sum(z_t, axis=1, keepdims=True)
        span, head = at[0], c["head"]
        dcol_ref[span, :] = jnp.where(
            lane == head, dbeta, jnp.where(lane == TOT + head, dtotal, dcol_ref[span, :])
        )
        drow_ref[c["slot"], :, span] = jnp.sum(z_t, axis=0, keepdims=True)
    for slot in range(TOGETHER):
        one, two = chains[2 * slot], chains[2 * slot + 1]
        o1 = one["o"][CHUNK - 1 :]
        load_ref[slot] = pack_plain(
            o1 * two["o"][CHUNK - 1 :],
            one["dmem"] + o1 * two["dmem"],
            one["dlookup"] + o1 * two["dlookup"],
        )
        dm1_ref[slot] = two["dmem"]
        dw1_ref[slot] = two["dlookup"]


def read_back(ridge, q, k, v, gate, gain, cols, rows, m0, w0, m_first, w_first, r, y, p, i, dm):
    flat = jax.ShapeDtypeStruct((ROWS, D), F32)
    states = jax.ShapeDtypeStruct((HEADS, HEAD, HEAD), F32)
    step_block = pl.BlockSpec((ITERS, ROWS, TOGETHER * HEAD), lambda h: (0, 0, h))
    return pl.pallas_call(
        read_back_kernel,
        grid=(HEADS // TOGETHER,),
        in_specs=[pl.BlockSpec(memory_space=pltpu.SMEM)]
        + [head_block(ROWS, 0, TOGETHER)] * 4
        + [head_block(1, 0, TOGETHER), whole((ROWS, 128)), head_rows(8, TOGETHER)]
        + [square(TOGETHER)] * 4
        + [head_block(ROWS, 0, TOGETHER)] * 2
        + [step_block] * 2
        + [head_block(ROWS, 0, TOGETHER)],
        out_specs=[head_block(ROWS, 0, TOGETHER)] * 4
        + [whole((ROWS, 128)), head_rows(1, TOGETHER)]
        + [loads(TOGETHER)]
        + [square(TOGETHER)] * 2,
        out_shape=[jax.ShapeDtypeStruct((ROWS, D), BF16)]
        + [flat] * 3
        + [jax.ShapeDtypeStruct((ROWS, 128), F32), jax.ShapeDtypeStruct((HEADS, 1, ROWS), F32)]
        + [jax.ShapeDtypeStruct((HEADS, LOAD, HEAD), BF16)]
        + [states] * 2,
        scratch_shapes=[
            pltpu.VMEM((2 * TOGETHER, ITERS * CHUNK, HEAD), BF16),
            pltpu.VMEM((2 * TOGETHER, ITERS * CHUNK, HEAD), BF16),
        ],
        compiler_params=params(),
        name="readout_back",
        cost_estimate=cost(39),
    )(ridge, q, k, v, gate, gain, cols, rows, m0, w0, m_first, w_first, r, y, p, i, dm)


def front_back_kernel(
    q_in, k_in, v_in, q_taps, k_taps, v_taps, cols_ref, row_ref, shift_ref,
    k_ref, v_ref, dq_ref, dk_ref, dv_ref, dcol_ref,
    m0_ref, w0_ref, m_first, w_first, dm1_ref, dw1_ref, dm2_ref, dw2_ref,
    out_ref, edge_ref, top_ref, dcol_out, ext, grown_ref,
):
    cols = cols_ref[...]
    lane = lax.broadcasted_iota(jnp.int32, (CHUNK, 128), 1)
    row = lax.broadcasted_iota(jnp.int32, (CHUNK, 1), 0)
    added = [dcol_ref[:CHUNK, :], dcol_ref[CHUNK:, :]]
    fresh = pl.program_id(0) == 0
    added = [jnp.where(fresh, a, dcol_out[c * CHUNK : (c + 1) * CHUNK, :]) for c, a in enumerate(added)]
    for slot in range(TOGETHER):
        head = pl.program_id(0) * TOGETHER + slot
        lanes = slice(slot * HEAD, (slot + 1) * HEAD)
        s1 = chunk_scalars(cols, row_ref, head, 0, slot)
        s2 = chunk_scalars(cols, row_ref, head, 1, slot)
        o1, o2 = s1["opening"][CHUNK - 1 :], s2["opening"][CHUNK - 1 :]
        dm2, dw2 = dm2_ref[slot], dw2_ref[slot]
        m0, w0 = m0_ref[slot], w0_ref[slot]
        m1, w1 = o1 * m0 + m_first[slot], o1 * w0 + w_first[slot]
        dm1, dw1 = dm1_ref[slot] + o2 * dm2, dw1_ref[slot] + o2 * dw2
        dks, dvs = [], []
        for chunk, s, dm, dw, m, w in ((0, s1, dm1, dw1, m0, w0), (1, s2, dm2, dw2, m1, w1)):
            at = (slice(chunk * CHUNK, (chunk + 1) * CHUNK), lanes)
            kc, vc = k_ref[at], v_ref[at]
            weight = last_weight(s)
            last = weight * s["beta"]
            kb, vb, dmb, dwb = (a.astype(BF16) for a in (kc, vc, dm, dw))
            mk = nt(kb, dmb)
            wk = nt(kb, dwb)
            dks.append(dk_ref[at] + last * (mk + nn(kb, dmb) + nn(vb, dwb)))
            dvs.append(dv_ref[at] + last * wk)
            dlast = jnp.sum(kc * mk + vc * wk, axis=1, keepdims=True)
            part = dlast * last
            do = jnp.sum(jnp.sum(dm * m + dw * w, axis=0, keepdims=True), axis=1, keepdims=True)
            at_end = do * s["opening"][CHUNK - 1 :] + jnp.sum(part, axis=0, keepdims=True)
            dtotal = jnp.where(row == CHUNK - 1, at_end - part, -part)
            added[chunk] = added[chunk] + jnp.where(
                lane == head, dlast * weight, jnp.where(lane == TOT + head, dtotal, 0.0)
            )
        dk = jnp.concatenate(dks, axis=0)
        dv = jnp.concatenate(dvs, axis=0)
        for n, (x_ref, taps_ref, grad, unit) in enumerate((
            (q_in, q_taps, dq_ref[:, lanes], True),
            (k_in, k_taps, dk, True),
            (v_in, v_taps, dv, False),
        )):
            c = conv_rows(x_ref, taps_ref, ext, 3 * slot + n, cols, lanes)
            sig = sigmoid(c)
            if unit:
                act = c * sig
                scale = lax.rsqrt(row_dot(act, act) + 1e-06)
                grad = scale * grad - act * ((scale * scale * scale) * row_dot(act, grad))
            dc = grad * (sig * (1.0 + c * (1.0 - sig)))
            grown = grown_ref.at[3 * slot + n]
            grown[0:8, :] = jnp.zeros((8, HEAD), F32)
            grown[8 : 8 + ROWS, :] = dc
            grown[8 + ROWS :, :] = jnp.zeros((8, HEAD), F32)
            total = taps_ref[0:1, lanes] * grown[0 : ROWS + 8, :]
            for j in range(1, CONV):
                mask = shift_ref[:, j : j + 1]
                total = total + (taps_ref[j : j + 1, lanes] * grown[j : j + ROWS + 8, :]) * mask
            out_ref[n, :, lanes] = total[8:, :].astype(BF16)
            edge_ref[n, :, lanes] = total[ROWS:, :]
            top_ref[n, :, lanes] = total[:8, :].astype(BF16)
    for chunk in range(2):
        dcol_out[chunk * CHUNK : (chunk + 1) * CHUNK, :] = added[chunk]


def front_back(conv_q, conv_kv, taps, cols, rows, shift, k, v, dq, dk, dv, dcol,
               m0, w0, m_first, w_first, dm1, dw1, dm2, dw2):
    per = HEADS // TOGETHER

    def stacked(count):
        return pl.BlockSpec((3, count, TOGETHER * HEAD), lambda h: (0, 0, h))

    return pl.pallas_call(
        front_back_kernel,
        grid=(per,),
        in_specs=[head_block(TAIL + ROWS, o, TOGETHER) for o in (0, 0, per)]
        + [head_block(CONV, o, TOGETHER) for o in (0, per, 2 * per)]
        + [whole((ROWS, 128)), head_rows(8, TOGETHER), whole((ROWS + 8, 128))]
        + [head_block(ROWS, 0, TOGETHER)] * 5
        + [whole((ROWS, 128))]
        + [square(TOGETHER)] * 8,
        out_specs=[stacked(ROWS), stacked(8), stacked(8), whole((ROWS, 128))],
        out_shape=[
            jax.ShapeDtypeStruct((3, ROWS, D), BF16),
            jax.ShapeDtypeStruct((3, 8, D), F32),
            jax.ShapeDtypeStruct((3, 8, D), BF16),
            jax.ShapeDtypeStruct((ROWS, 128), F32),
        ],
        scratch_shapes=[
            pltpu.VMEM((3 * TOGETHER, ROWS + 8, HEAD), F32),
            pltpu.VMEM((3 * TOGETHER, ROWS + 16, HEAD), F32),
        ],
        compiler_params=params(),
        name="front_back",
        cost_estimate=cost(10),
    )(conv_q, conv_kv, conv_kv, taps, taps, taps, cols, rows, shift,
      k, v, dq, dk, dv, dcol, m0, w0, m_first, w_first, dm1, dw1, dm2, dw2)


def running_sums():
    t = lax.broadcasted_iota(jnp.int32, (ROWS, ROWS), 0)
    u = lax.broadcasted_iota(jnp.int32, (ROWS, ROWS), 1)
    return ((t >= u) & (t // CHUNK == u // CHUNK)).astype(F32)


def scalar_back(logits, live, decay_rate, dcol, drow):
    dtotal = dcol[:, TOT : TOT + HEADS] + drow[:, 0].T
    dbeta = dcol[:, :HEADS]
    ddecay = lax.dot_general(
        running_sums(), dtotal, (((0,), (0,)), ((), ())), precision=lax.Precision.HIGHEST
    )
    sig = jax.nn.sigmoid(logits[:, :HEADS])
    slope = jax.nn.sigmoid(logits[:, HEADS : 2 * HEADS] + 1.0)
    return jnp.concatenate(
        [dbeta * live[:, None] * sig * (1.0 - sig), -decay_rate[None, :] * slope * ddecay], axis=1
    )


def choose_kernel(counts, adapter_ref, *refs):
    adapter = adapter_ref[0]
    row = lax.broadcasted_iota(jnp.int32, (RANK, 128), 0)
    lane = lax.broadcasted_iota(jnp.int32, (RANK, 128), 1)
    picks = jnp.where(lane == row + adapter * RANK, 1.0, 0.0).astype(BF16)
    for n, blocks in enumerate(counts):
        source, out = refs[n], refs[n + len(counts)]
        for b in range(blocks):
            part = nt(picks, source[:, b * 128 : (b + 1) * 128])
            out[b * RANK : (b + 1) * RANK, :] = part.astype(BF16)


def choose(adapter_id, arrays):
    counts = [a.shape[1] // 128 for a in arrays]
    vmem = pl.BlockSpec(memory_space=pltpu.VMEM)
    return pl.pallas_call(
        functools.partial(choose_kernel, counts),
        in_specs=[pl.BlockSpec(memory_space=pltpu.SMEM)] + [vmem] * len(arrays),
        out_specs=[vmem] * len(arrays),
        out_shape=[jax.ShapeDtypeStruct((RANK * c, a.shape[0]), BF16) for c, a in zip(counts, arrays)],
        compiler_params=params(),
        name="choose",
        cost_estimate=cost(5),
    )(adapter_id, *arrays)


def softplus(x):
    return jnp.maximum(x, 0.0) + jnp.log(1.0 + jnp.exp(-jnp.abs(x)))


def setup_kernel(
    tokens_ref, tail_ref, gain_ref, low_ref, rates_ref, wide_ref, live_ref, live_row_ref, ids_ref, ids_row_ref,
    decay_row_ref, decay_col_ref,
    first_ref, inner_ref, logits_ref, cols_ref, rows_ref, shift_ref, spread,
):
    parts = []
    for x in (tail_ref[...].astype(F32), tokens_ref[...].astype(F32)):
        parts.append((x * lax.rsqrt(row_dot(x, x) * (1.0 / D) + 1e-06) * gain_ref[...]).astype(BF16))
    both, first = jnp.concatenate(parts, axis=0), parts[1]
    first_ref[...] = both
    for j in range(4):
        inner_ref[j] = nt(both, low_ref[j * RANK : (j + 1) * RANK, :]).astype(BF16)
    t = lax.broadcasted_iota(jnp.int32, (ROWS, ROWS), 0)
    u = lax.broadcasted_iota(jnp.int32, (ROWS, ROWS), 1)
    together = (t < CHUNK) == (u < CHUNK)
    lower = jnp.where((t >= u) & together, 1.0, 0.0).astype(BF16)
    upper = jnp.where((t <= u) & together, 1.0, 0.0).astype(BF16)
    logits = nt(first, wide_ref[...])
    logits_ref[...] = logits
    beta = sigmoid(logits) * live_ref[...]
    total = summed3(lower, -decay_row_ref[...] * softplus(logits + 1.0), True)
    lane = lax.broadcasted_iota(jnp.int32, (ROWS, 128), 1)
    row = lax.broadcasted_iota(jnp.int32, (ROWS, 1), 0)
    ids = ids_ref[8:, :]
    before = jnp.where(row < CHUNK, ids_ref[7:8, :], ids_ref[7 + CHUNK : 8 + CHUNK, :])
    cols = jnp.where(lane < 8, beta, jnp.where(lane < 16, total, 0.0))
    cols = jnp.where(lane == KEPT, jnp.where(ids == before, 1.0, 0.0), cols)
    cols = jnp.where(lane == IDS, ids, cols)
    for j in range(1, CONV):
        same = jnp.where(ids_ref[8 - j : 8 - j + ROWS, :] == ids, 1.0, 0.0)
        cols = jnp.where(lane == SAME + j - 1, same, cols)
    cols_ref[...] = cols
    spread[0:8, :] = jnp.zeros((8, 128), F32)
    spread[8 : 8 + ROWS, :] = cols
    spread[8 + ROWS :, :] = jnp.zeros((8, 128), F32)
    out_lane = lax.broadcasted_iota(jnp.int32, (ROWS + 8, 128), 1)
    shift = jnp.zeros((ROWS + 8, 128), F32)
    for j in range(1, CONV):
        moved = column(spread[j : j + ROWS + 8, :], SAME + j - 1)
        shift = jnp.where(out_lane == j, moved, shift)
    shift_ref[...] = shift
    logits = nt(rates_ref[...], first)
    beta = sigmoid(logits) * live_row_ref[...]
    total = summed3(upper, -decay_col_ref[...] * softplus(logits + 1.0), False)
    rows_ref[...] = jnp.zeros_like(rows_ref)
    for h in range(HEADS):
        rows_ref[h, 0:1, :] = beta[h : h + 1, :]
        rows_ref[h, 1:2, :] = total[TOT + h : TOT + h + 1, :]
        rows_ref[h, 2:3, :] = ids_row_ref[...]


def summed3(ones, x, left):
    high = x.astype(BF16)
    rest = x - high.astype(F32)
    middle = rest.astype(BF16)
    low = (rest - middle.astype(F32)).astype(BF16)
    out = 0.0
    for part in (low, middle, high):
        out = out + (nn(ones, part) if left else nn(part, ones))
    return out


def set_up(tokens, tail, gain, low, rates, live, ids, tail_ids, decay_rate):
    rates_t = rates.T
    wide = jnp.pad(rates_t, ((0, 128 - 2 * HEADS), (0, 0)))
    decay = jnp.concatenate([jnp.zeros_like(decay_rate), decay_rate])
    ids = ids.astype(F32)
    ext = jnp.concatenate([jnp.zeros((8 - CONV + 1,), F32), tail_ids.astype(F32), ids])
    vmem = pl.BlockSpec(memory_space=pltpu.VMEM)
    return pl.pallas_call(
        setup_kernel,
        in_specs=[vmem] * 12,
        out_specs=[vmem] * 6,
        out_shape=[
            jax.ShapeDtypeStruct((TAIL + ROWS, D), BF16),
            jax.ShapeDtypeStruct((4, TAIL + ROWS, RANK), BF16),
            jax.ShapeDtypeStruct((ROWS, 128), F32),
            jax.ShapeDtypeStruct((ROWS, 128), F32),
            jax.ShapeDtypeStruct((HEADS, 8, ROWS), F32),
            jax.ShapeDtypeStruct((ROWS + 8, 128), F32),
        ],
        scratch_shapes=[pltpu.VMEM((ROWS + 16, 128), F32)],
        compiler_params=params(),
        name="set_up",
        cost_estimate=cost(5),
    )(tokens, tail, gain, low, rates_t, wide, live[:, None], live[None, :], ext[:, None], ids[None, :],
      jnp.pad(decay, (0, 128 - 16))[None, :], decay[:, None]), rates_t


TILE = 1024
FF_TILE = 1408


def rms_back(value, gain, grad):
    scale = lax.rsqrt(row_dot(value, value) * (1.0 / D) + 1e-06)
    dn = grad * gain
    return scale * dn - value * ((scale * scale * scale) * (row_dot(value, dn) * (1.0 / D)))


def project_kernel(first_ref, w_ref, inner_ref, up_ref, out_ref):
    skip = first_ref.shape[0] - out_ref.shape[0]
    out = nn(first_ref[skip:, :], w_ref[...]) + nn(inner_ref[0, skip:, :], up_ref[...])
    out_ref[...] = out.astype(out_ref.dtype)


def project(first, weights, inner, up, begin, width, rows, dtype):
    tiles, per_block = width // PROJ, D // PROJ
    return pl.pallas_call(
        project_kernel,
        grid=(tiles,),
        in_specs=[
            pl.BlockSpec((TAIL + ROWS, D), lambda t: (0, 0)),
            pl.BlockSpec((D, PROJ), lambda t: (0, t + begin // PROJ)),
            pl.BlockSpec((1, TAIL + ROWS, RANK), lambda t: ((t + begin // PROJ) // per_block, 0, 0)),
            pl.BlockSpec((RANK, PROJ), lambda t: (0, t + begin // PROJ)),
        ],
        out_specs=pl.BlockSpec((rows, PROJ), lambda t: (0, t)),
        out_shape=jax.ShapeDtypeStruct((rows, width), dtype),
        compiler_params=params(),
        name="project",
        cost_estimate=cost(2 * width / D),
    )(first, weights, inner, up)


PROJ = 1024


def share(out_ref, lane, grads):
    for owner in range(8):
        out_ref[owner, :, lane : lane + 128] = grads[:, owner * 128 : (owner + 1) * 128]


def half_kernel(
    merged_ref, tokens_ref, grad_ref, gain_ref, wout_a, wout_b, out_low, out_up, ffn_low, proj_up,
    gate_w, up_w, down_w, up_a, up_b, proj_low,
    mixed_ref, dmid_ref, dmerged_ref, early_ref,
    middle_s, second_s, ffn_s, dproj_s, acc_out, acc_ds, acc_ip, acc_df,
):
    step = pl.program_id(0)
    g = grad_ref[...]

    @pl.when(step == 0)
    def _():
        merged = merged_ref[...]
        inner_out = nt(merged, out_low[...]).astype(BF16)
        branch = jnp.concatenate([nn(merged, wout_a[...]), nn(merged, wout_b[...])], axis=1)
        middle = tokens_ref[...].astype(F32) + (branch + nn(inner_out, out_up[...]))
        scale = lax.rsqrt(row_dot(middle, middle) * (1.0 / D) + 1e-06)
        second = (middle * scale * gain_ref[...]).astype(BF16)
        inner_ffn = nt(second, ffn_low[...]).astype(BF16)
        middle_s[...] = middle
        acc_out[...] = middle
        second_s[...] = second
        ffn_s[0] = inner_ffn[:, :RANK]
        ffn_s[1] = inner_ffn[:, RANK:]
        dproj_s[...] = nt(g, proj_up[...]).astype(BF16)
        early_ref[...] = jnp.zeros_like(early_ref)
        acc_ds[...] = jnp.zeros_like(acc_ds)
        acc_ip[...] = jnp.zeros_like(acc_ip)
        acc_df[...] = jnp.zeros_like(acc_df)

    second = second_s[...]
    a = nn(second, gate_w[...]) + nn(ffn_s[0], up_a[...])
    b = nn(second, up_w[...]) + nn(ffn_s[1], up_b[...])
    down = down_w[...]
    d_hidden = nt(g, down) + nn(dproj_s[...], proj_low[...])
    sig = sigmoid(a)
    act = a * sig
    hidden = (act * b).astype(BF16)
    da = (d_hidden * b * (sig * (1.0 + a * (1.0 - sig)))).astype(BF16)
    db = (d_hidden * act).astype(BF16)
    acc_out[...] += nn(hidden, down)
    acc_ds[...] += nt(da, gate_w[...]) + nt(db, up_w[...])
    acc_ip[...] += nt(hidden, proj_low[...])
    acc_df[0] += nt(da, up_a[...])
    acc_df[1] += nt(db, up_b[...])
    own, rows = FF // 4, FF // 8
    count = FF_TILE // own
    for part, grads in enumerate((tn(ffn_s[0], da), tn(ffn_s[1], db))):
        for n in range(count):
            early_ref[part * 4 + step * count + n, :, 512 : 512 + own] = grads[:, n * own : (n + 1) * own]
    grads = tn(dproj_s[...], hidden)
    for n in range(2 * count):
        early_ref[step * 2 * count + n, :, 1280 : 1280 + rows] = grads[:, n * rows : (n + 1) * rows]

    @pl.when(step == pl.num_programs(0) - 1)
    def _():
        merged, second, middle = merged_ref[...], second_s[...], middle_s[...]
        inner_proj = acc_ip[...].astype(BF16)
        mixed_ref[...] = (acc_out[...] + nn(inner_proj, proj_up[...])).astype(BF16)
        share(early_ref, 1664, tn(inner_proj, g))
        da, db = acc_df[0].astype(BF16), acc_df[1].astype(BF16)
        d_second = acc_ds[...] + (nn(da, ffn_low[:RANK, :]) + nn(db, ffn_low[RANK:, :]))
        share(early_ref, 256, tn(da, second))
        share(early_ref, 384, tn(db, second))
        d_middle = g.astype(F32) + rms_back(middle, gain_ref[...], d_second)
        dmid_ref[...] = d_middle
        d_branch = d_middle.astype(BF16)
        d_inner = nt(d_branch, out_up[...]).astype(BF16)
        half = D // 2
        d_branch_out = nt(d_branch[:, :half], wout_a[...]) + nt(d_branch[:, half:], wout_b[...])
        dmerged_ref[...] = d_branch_out + nn(d_inner, out_low[...])
        inner_out = nt(merged, out_low[...]).astype(BF16)
        share(early_ref, 0, tn(d_inner, merged))
        share(early_ref, 128, tn(inner_out, d_branch))


def second_half(merged, tokens, grad, gain, w_out, w_gu, w_down, out_low, out_up, ffn_low, ffn_up, proj_low, proj_up):
    steps = FF // FF_TILE
    wide = jax.ShapeDtypeStruct((ROWS, D), F32)
    tile = pl.BlockSpec((RANK, FF_TILE), lambda f: (0, f))
    row = whole((RANK, D))

    def out_half(n):
        return pl.BlockSpec((D, D // 2), lambda f: (0, n))

    return pl.pallas_call(
        half_kernel,
        grid=(steps,),
        in_specs=[whole((ROWS, D))] * 3
        + [whole((1, D)), out_half(0), out_half(1), row, row, whole((2 * RANK, D)), row]
        + [
            pl.BlockSpec((D, FF_TILE), lambda f: (0, f)),
            pl.BlockSpec((D, FF_TILE), lambda f: (0, f + steps)),
            pl.BlockSpec((FF_TILE, D), lambda f: (f, 0)),
            tile,
            pl.BlockSpec((RANK, FF_TILE), lambda f: (0, f + steps)),
            tile,
        ],
        out_specs=[whole((ROWS, D))] * 3 + [whole((8, RANK, 1792))],
        out_shape=[
            jax.ShapeDtypeStruct((ROWS, D), BF16), wide, wide,
            jax.ShapeDtypeStruct((8, RANK, 1792), F32),
        ],
        scratch_shapes=[
            pltpu.VMEM((ROWS, D), F32), pltpu.VMEM((ROWS, D), BF16),
            pltpu.VMEM((2, ROWS, RANK), BF16), pltpu.VMEM((ROWS, RANK), BF16),
            pltpu.VMEM((ROWS, D), F32), pltpu.VMEM((ROWS, D), F32),
            pltpu.VMEM((ROWS, RANK), F32), pltpu.VMEM((2, ROWS, RANK), F32),
        ],
        compiler_params=params(),
        name="second_half",
        cost_estimate=cost(23),
    )(merged, tokens, grad, gain, w_out, w_out, out_low, out_up, ffn_low, proj_up,
      w_gu, w_gu, w_down, ffn_up, ffn_up, proj_low)


def repaired(grown_ref, edge_ref, back_ref):
    end = edge_ref[0] + back_ref[0].astype(F32)
    return jnp.concatenate([grown_ref[0, : ROWS - 8, :].astype(F32), end], axis=0).astype(BF16)


def inner_kernel(
    grown_ref, edge_ref, back_ref, inner_ref, up_ref, gate_inner, gate_up, first_ref, inner_out, late_ref,
):
    step = pl.program_id(0)
    half = D // 2
    grown = repaired(grown_ref, edge_ref, back_ref)
    inner_out[step] = nt(grown, up_ref[...]).astype(BF16)
    up = tn(inner_ref[0, TAIL:, :], grown).astype(BF16)
    late_ref[2 * step, :, half:] = up[:, :half]
    late_ref[2 * step + 1, :, half:] = up[:, half:]

    @pl.when(step == pl.num_programs(0) - 1)
    def _():
        inner_out[3] = gate_inner[...]
        late_ref[6, :, half:] = gate_up[0]
        late_ref[7, :, half:] = gate_up[1]
        for j in range(4):
            low = tn(inner_out[j], first_ref[TAIL:, :]).astype(BF16)
            for owner in range(8):
                late_ref[owner, :, j * 128 : (j + 1) * 128] = low[:, owner * 128 : (owner + 1) * 128]


def block_piece(rows):
    return pl.BlockSpec((1, rows, D), lambda t: (t, 0, 0))


def inner_part(grown, edge, back, inner, up, gate_inner, gate_up, first):
    return pl.pallas_call(
        inner_kernel,
        grid=(3,),
        in_specs=[
            block_piece(ROWS), block_piece(8), block_piece(8),
            pl.BlockSpec((1, TAIL + ROWS, RANK), lambda t: (t, 0, 0)),
            pl.BlockSpec((RANK, D), lambda t: (0, t)),
            whole((ROWS, RANK)), whole((2, RANK, D // 2)), whole((TAIL + ROWS, D)),
        ],
        out_specs=[whole((4, ROWS, RANK)), whole((8, RANK, D))],
        out_shape=[
            jax.ShapeDtypeStruct((4, ROWS, RANK), BF16),
            jax.ShapeDtypeStruct((8, RANK, D), BF16),
        ],
        compiler_params=params(),
        name="inner_part",
        cost_estimate=cost(4),
    )(grown, edge, back, inner, up, gate_inner, gate_up, first)


def last_kernel(
    grown_ref, edge_ref, back_ref, w_ref, inner_ref, gate_ref, tokens_ref, gain_ref,
    low_ref, logits_ref, rates_ref, dmid_ref, out_ref, acc,
):
    step = pl.program_id(0)

    @pl.when(step == 0)
    def _():
        acc[...] = gate_ref[...]

    acc[...] += nt(repaired(grown_ref, edge_ref, back_ref), w_ref[...])

    @pl.when(step == pl.num_programs(0) - 1)
    def _():
        x = tokens_ref[...].astype(F32)
        total = acc[...] + nn(logits_ref[...], rates_ref[...])
        for j in range(4):
            total = total + nn(inner_ref[j], low_ref[j * RANK : (j + 1) * RANK, :])
        out_ref[...] = dmid_ref[...] + rms_back(x, gain_ref[...], total)


def last(grown, edge, back, w_in, inner, gate_part, tokens, gain, low, d_logits, rates, d_middle):
    return pl.pallas_call(
        last_kernel,
        grid=(3,),
        in_specs=[
            block_piece(ROWS), block_piece(8), block_piece(8),
            pl.BlockSpec((D, D), lambda t: (0, t)),
            whole((4, ROWS, RANK)),
            whole((ROWS, D)), whole((ROWS, D)), whole((1, D)),
            whole((4 * RANK, D)), whole((ROWS, 16)), whole((16, D)), whole((ROWS, D)),
        ],
        out_specs=whole((ROWS, D)),
        out_shape=jax.ShapeDtypeStruct((ROWS, D), F32),
        scratch_shapes=[pltpu.VMEM((ROWS, D), F32)],
        compiler_params=params(),
        name="last",
        cost_estimate=cost(8),
    )(grown, edge, back, w_in, inner, gate_part, tokens, gain, low, d_logits, rates, d_middle)


def gate_kernel(grown_ref, w_ref, inner_ref, up_ref, out_ref, inner_out, up_out):
    grown = grown_ref[...]
    out_ref[...] = nt(grown, w_ref[...])
    inner_out[...] = nt(grown, up_ref[...]).astype(BF16)
    up = tn(inner_ref[0, TAIL:, :], grown).astype(BF16)
    up_out[0] = up[:, : D // 2]
    up_out[1] = up[:, D // 2 :]


def gate_part(grown, w_in, inner, up):
    return pl.pallas_call(
        gate_kernel,
        grid=(1,),
        in_specs=[
            whole((ROWS, D)),
            pl.BlockSpec((D, D), lambda t: (0, 3)),
            pl.BlockSpec((1, TAIL + ROWS, RANK), lambda t: (3, 0, 0)),
            pl.BlockSpec((RANK, D), lambda t: (0, 3)),
        ],
        out_specs=[whole((ROWS, D)), whole((ROWS, RANK)), whole((2, RANK, D // 2))],
        out_shape=[
            jax.ShapeDtypeStruct((ROWS, D), F32),
            jax.ShapeDtypeStruct((ROWS, RANK), BF16),
            jax.ShapeDtypeStruct((2, RANK, D // 2), BF16),
        ],
        compiler_params=params(),
        name="gate_part",
        cost_estimate=cost(3.5),
    )(grown, w_in, inner, up)


def spread_kernel(rows, own_ref, own_pair, rest_ref, rest_pair, down_ref, out_ref):
    rep, index = lax.axis_index("rep"), lax.axis_index("shard")
    z, x, y, core = rep // 4, lax.rem(rep, 4), index // 2, lax.rem(index, 2)
    down, out = rows

    def put(block, source, first_row, lanes_from, piece, width):
        at = pl.ds(pl.multiple_of(piece * 128, 128), width)
        lanes = slice(lanes_from, lanes_from + width)
        down_ref[pl.ds(pl.multiple_of(block * down, 16), down), at] = source[
            first_row : first_row + down, lanes
        ]
        out_ref[pl.ds(pl.multiple_of(block * out, 16), out), at] = source[
            first_row + down : first_row + down + out, lanes
        ]

    for own, rest, c in ((own_ref, rest_ref, core), (own_pair, rest_pair, 1 - core)):
        put(2 * y + c, own, 0, 0, 0, D)
        for n in (1, 2, 3):
            block = 2 * lax.rem(y + 4 - n, 4) + c
            for group in range(8):
                if group == 0:
                    piece = x
                elif group == 1:
                    piece = 4 + z
                elif group < 5:
                    piece = lax.rem(x + 4 - (group - 1), 4)
                else:
                    piece = 4 + lax.rem(z + 4 - (group - 4), 4)
                put(block, rest, (n - 1) * (down + out), group * 128, piece, 128)


def rows_over_y(proj_down, proj_out):
    own = jnp.concatenate([proj_down, proj_out], axis=0)
    rep = lax.axis_index("rep")
    z, x = rep // 4, lax.rem(rep, 4)
    pieces = jnp.concatenate(
        [
            lax.dynamic_slice_in_dim(own, x * 128, 128, 1),
            lax.dynamic_slice_in_dim(own, (4 + z) * 128, 128, 1),
        ],
        axis=1,
    )
    return own, [lax.ppermute(pieces, "shard", along("shard", 2 * n)) for n in (1, 2, 3)]


def rows_over_planes(came):
    by_x = jnp.concatenate([c[:, :128] for c in came], axis=0)
    by_z = jnp.concatenate([c[:, 128:] for c in came], axis=0)
    rest = [lax.ppermute(by_x, "rep", rep_pairs(0, n)) for n in (1, 2, 3)]
    rest += [lax.ppermute(by_z, "rep", rep_pairs(n, 0)) for n in (1, 2, 3)]
    return [by_x, by_z] + rest


def side_kernel(*refs):
    for n, ref in enumerate(refs[:-1]):
        refs[-1][:, n * 128 : (n + 1) * 128] = ref[...]


def side_by_side(parts):
    vmem = pl.BlockSpec(memory_space=pltpu.VMEM)
    return pl.pallas_call(
        side_kernel,
        in_specs=[vmem] * len(parts),
        out_specs=vmem,
        out_shape=jax.ShapeDtypeStruct((parts[0].shape[0], 128 * len(parts)), parts[0].dtype),
        compiler_params=params(),
        name="side_by_side",
        cost_estimate=cost(3),
    )(*parts)


def gathered_rows(own, own_pair, rest, rest_pair, rows):
    return pl.pallas_call(
        functools.partial(spread_kernel, rows),
        in_specs=[pl.BlockSpec(memory_space=pltpu.VMEM)] * 4,
        out_specs=[pl.BlockSpec(memory_space=pltpu.VMEM)] * 2,
        out_shape=[jax.ShapeDtypeStruct((8 * n, D), BF16) for n in rows],
        compiler_params=params(),
        name="gathered_rows",
        cost_estimate=cost(6),
    )(own, own_pair, rest, rest_pair)


def along(axis, offset):
    count = lax.axis_size(axis)
    return [(i, (i + offset) % count) for i in range(count)]


def rep_pairs(dz, dx):
    return [(z * 4 + x, (z + dz) % 4 * 4 + (x + dx) % 4) for z in range(4) for x in range(4)]


def placed(gathered, sizes):
    n = gathered[0].shape[2] - 128

    def body(*refs):
        sources, outs, total = refs[: len(gathered)], refs[len(gathered) : -1], refs[-1]
        total[...] = jnp.zeros_like(total)
        for ref in sources:
            for s in range(ref.shape[0]):
                number = ref[s, :, n:].astype(F32)[:, :1]
                part = ref[s, :, :n].astype(F32)
                for a in range(8):
                    total[a] += jnp.where(number == a, part, 0.0)
        everything = total[...].reshape(8 * RANK, n)
        begin = 0
        for out, (rows, blocks) in zip(outs, sizes):
            padded = -(-rows // 128) * 128
            for m in range(blocks):
                out[:, m * 128 : (m + 1) * 128] = everything[:, begin : begin + padded].T[:rows]
                begin += padded

    return pl.pallas_call(
        body,
        in_specs=[pl.BlockSpec(memory_space=pltpu.VMEM)] * len(gathered),
        out_specs=[pl.BlockSpec(memory_space=pltpu.VMEM)] * len(sizes),
        out_shape=[jax.ShapeDtypeStruct((rows, blocks * 128), F32) for rows, blocks in sizes],
        scratch_shapes=[pltpu.VMEM((8, RANK, n), F32)],
        compiler_params=params(),
        name="placed",
        cost_estimate=cost(3),
    )(*gathered)


def numbered(sums, adapter):
    number = jnp.full((RANK, 128), adapter, F32).astype(sums.dtype)
    return jnp.concatenate([sums, number], axis=1)


def reduced_calls(own, adapter, sizes):
    return placed([lax.all_gather(numbered(own, adapter), "rep")], sizes)


def reduced(stacked, adapter, sizes):
    index = lax.axis_index("shard")
    y, core = index // 2, lax.rem(index, 2)
    n = stacked.shape[2]
    by_core = stacked.astype(BF16).reshape(4, 2, RANK, n)
    came = swap(lax.dynamic_index_in_dim(by_core, 1 - core, 1, False))
    chip = lax.dynamic_index_in_dim(by_core, core, 1, False).astype(F32) + came.astype(F32)
    total = lax.dynamic_index_in_dim(chip, y, 0, False)
    low = chip.astype(BF16)
    for step in (1, 2, 3):
        part = lax.dynamic_index_in_dim(low, lax.rem(y + step, 4), 0, False)
        total = total + lax.ppermute(part, "shard", along("shard", 2 * step)).astype(F32)
    own = numbered(total.astype(BF16), adapter)
    row = jnp.stack([own] + [lax.ppermute(own, "rep", rep_pairs(0, k)) for k in (1, 2, 3)])
    planes = [row] + [lax.ppermute(row, "rep", rep_pairs(k, 0)) for k in (1, 2, 3)]
    return placed(planes, sizes)


def owners(part):
    split = part.reshape(RANK, 8, -1).transpose(1, 0, 2)
    return jnp.pad(split, ((0, 0), (0, 0), (0, -split.shape[2] % 128)))


def per_device(
    tokens, segment_ids, pad_mask, adapter_id, out_grad, gain_first, proj_in, proj_rates,
    conv_taps, decay_rate, ridge, gain_heads, proj_out, gain_second, proj_gu, proj_down,
    in_lower, in_upper, out_lower, out_upper, ffn_lower, ffn_upper, proj_lower, proj_upper,
):
    tail = CONV - 1
    adapter = adapter_id[0]
    w_in = lax.all_gather(proj_in, "shard", axis=0, tiled=True)
    own_rows, rows_came = rows_over_y(proj_down, proj_out)
    own_pair = swap(own_rows)
    in_low, in_up, out_low, out_up, ffn_low, ffn_up, proj_low, proj_up = choose(
        adapter_id, (in_lower, in_upper, out_lower, out_upper, ffn_lower, ffn_upper, proj_lower, proj_upper)
    )
    tail_tokens = lax.ppermute(tokens[ROWS - TAIL :], "shard", [(i, i + 1) for i in range(7)])
    tail_ids = lax.ppermute(segment_ids[ROWS - tail :], "shard", [(i, i + 1) for i in range(7)])

    rows_came, in_low, tokens_here = lax.optimization_barrier((rows_came, in_low, tokens))
    rest_rows = rows_over_planes(rows_came)
    live = pad_mask.astype(F32)
    (first, inner_in, logits, cols, rows, shift), rates_t = set_up(
        tokens_here, tail_tokens, gain_first[None], in_low, proj_rates, live, segment_ids, tail_ids, decay_rate
    )

    own_gu, own_pair, rest_rows, first, cols, rows = lax.optimization_barrier(
        (proj_gu, own_pair, rest_rows, first, cols, rows)
    )
    w_gu = lax.all_gather(own_gu, "shard", axis=0, tiled=True)

    conv_kv = project(first, w_in, inner_in, in_up, D, 2 * D, TAIL + ROWS, BF16)
    k, v, m_first, w_first, load = front(conv_kv, conv_taps, cols, rows)
    conv_q = project(first, w_in, inner_in, in_up, 0, D, TAIL + ROWS, BF16)
    gate_in = project(first, w_in, inner_in, in_up, 3 * D, D, ROWS, F32)

    def first_work(conv_q, own_rows, own_pair, *rest):
        rest = side_by_side(rest)
        sources = (own_rows, own_pair, rest, swap(rest))
        return front_query(conv_q, conv_taps, cols), *gathered_rows(*sources, (FF // 8, D // 8))

    (m0, w0), (q, w_down, w_out) = exchanged(
        load, True, (conv_q, own_rows, own_pair, *rest_rows), first_work
    )
    gain = gain_heads[None]
    merged, r, y, p, i = read(ridge, q, k, v, gate_in, gain, cols, rows, m0, w0, m_first, w_first)

    mixed, d_middle, d_merged, early = second_half(
        merged, tokens, out_grad, gain_second[None], w_out, w_gu, w_down,
        out_low, out_up, ffn_low, ffn_up, proj_low, proj_up,
    )
    d_gate, dq, dk, dv, dcol, drow, load, dm1, dw1 = read_back(
        ridge, q, k, v, gate_in, gain, cols, rows, m0, w0, m_first, w_first, r, y, p, i, d_merged
    )
    early = lax.psum_scatter(early, "shard", scatter_dimension=0, tiled=False)
    load, early = lax.optimization_barrier((load, early))
    early = reduced_calls(
        early, adapter, [(128, 1), (128, 1), (128, 2), (704, 1), (352, 1), (128, 1)]
    )
    (dm2, dw2), (gate_grad, gate_inner, g_up_gate) = exchanged(
        load, False, (d_gate,), lambda d_gate: gate_part(d_gate, w_in, inner_in, in_up)
    )
    grown, edge, top, dcol = front_back(
        conv_q, conv_kv, conv_taps, cols, rows, shift, k, v, dq, dk, dv, dcol,
        m0, w0, m_first, w_first, dm1, dw1, dm2, dw2,
    )
    back = lax.ppermute(top, "shard", [(i + 1, i) for i in range(7)])
    d_logits = scalar_back(logits, live, decay_rate, dcol, drow).astype(BF16)
    inner_grads, late = inner_part(grown, edge, back, inner_in, in_up, gate_inner, g_up_gate, first)
    token_grad = last(
        grown, edge, back, w_in, inner_grads, gate_grad, tokens, gain_first[None],
        in_low, d_logits, rates_t, d_middle,
    )
    late = reduced(late, adapter, [(128, 4), (512, 1)])
    return (mixed, token_grad, late[0], late[1], *early)


def solution(mesh):
    whole_spec, by_shard, by_token = P(), P("shard", None), P(("rep", "shard"), None)
    by_row = P(("rep", "shard"))
    return jax.shard_map(
        per_device,
        mesh=mesh,
        in_specs=(
            by_token, by_row, by_row, P("rep"), by_token, whole_spec, by_shard, whole_spec,
            whole_spec, whole_spec, whole_spec, whole_spec, by_shard, whole_spec, by_shard, by_shard,
        )
        + (whole_spec,) * 8,
        out_specs=(by_token, by_token) + (by_shard,) * 8,
        check_vma=False,
    )
```
